128 devices in a mesh: lon: 8 (over y, z_hi), lat: 16 (over z_lo, x, core).
Axes of the slice: x: 4, y: 4, z: 4 (z_hi: 2, z_lo: 2; z = z_hi * 2 + z_lo), core: 2. Of those that a mesh axis runs over, the one named last changes fastest.
Arguments:
- grid_field: bfloat16 [192, 192, 3, 512], P('lon', 'lat'), may hold values from -6 to 6
- fine_weights: bfloat16 [512, 2048], replicated, may hold values from -0.25 to 0.25
- fine_gain: float32 [512], replicated, may hold values from 0.1 to 1.9
- fine_scales: float32 [8], replicated, may hold values from 4 to 16
- merge_gain: float32 [2048], replicated, may hold values from 0.1 to 1.9
- merge_weight: bfloat16 [2048, 1024], replicated, may hold values from -0.125 to 0.125
- coarse_weights: bfloat16 [1024, 4096], replicated, may hold values from -0.1875 to 0.1875
- coarse_gain: float32 [1024], replicated, may hold values from 0.1 to 1.9
- coarse_scales: float32 [16], replicated, may hold values from 4 to 16
- cot_fine: bfloat16 [192, 192, 3, 512], P('lon', 'lat'), may hold values from -6 to 6
- cot_coarse: bfloat16 [96, 96, 3, 1024], P('lon', 'lat'), may hold values from -6 to 6
Outputs:
- coarse_out: bfloat16 [96, 96, 3, 1024], P('lon', 'lat')
- grad_input: bfloat16 [192, 192, 3, 512], P('lon', 'lat')
- grad_fine_weights: float32 [512, 2048], P(('lon', 'lat'))
The draws below stay inside these ranges and needn't reach their ends.
All inputs are finite; a program needn't handle non-finite values.
Results may differ from the reference program's by a relative error of at most 0.019.
Values may be sent and summed in bfloat16 or wider, within the bound.
No kernel may reach another device: no remote copies, remote signals or barrier semaphores. Data moves between devices by JAX's collectives and lax.ppermute only.
A program may use at most 192 MiB of HBM per device.

```python
import math
import jax
import jax.numpy as jnp
from jax import lax

D1 = 512
D2 = 1024
H1 = 8
H2 = 16
WLON = 12
WLAT = 6
LEVELS = 3
S_LON = 6
S_LAT = 3
NLON = 192
NLAT = 192


def strengthened(values, key, source, target, shards_of, factor):
    owner, partner = [(jnp.arange(values.shape[position]) // (values.shape[position] // shards_of)).reshape([-1 if axis == position else 1 for axis in range(values.ndim)]) for position in (source, target)]
    chosen = jax.random.permutation(key, shards_of)[partner]
    strong = (owner == chosen) | (owner == (partner + shards_of // 2) % shards_of)
    return jnp.where(strong, factor * values, values)


def block_levels(own_key, shape, shards, low, largest):
    gain, own = 1.0, jax.random.fold_in(own_key, 6)
    for position, blocks in shards:
        steps = jnp.exp(jax.random.uniform(jax.random.fold_in(own, position), (blocks,), jnp.float32, low / len(shards), largest / len(shards)))
        gain = gain * jnp.repeat(steps, shape[position] // blocks).reshape([-1 if axis == position else 1 for axis in range(len(shape))])
    return gain


def gaussian(key, dims, width, bound, split=(), kind=jnp.bfloat16):
    array = jax.random.normal(key, dims, jnp.float32) * width
    if len(split) > 0:
        array = block_levels(key, dims, split, -0.22, 0.18) * array
    return jnp.clip(array, min=-bound, max=bound).astype(kind)


def heavy_noise(key, extent, scale, most, cuts, heavy, held_as=jnp.bfloat16):
    entries = scale * jax.random.normal(key, extent, jnp.float32)
    if cuts:
        entries = entries * block_levels(key, extent, cuts, -0.22, 0.18)
    return jnp.clip(strengthened(entries, jax.random.fold_in(key, 3), *heavy), -most, most).astype(held_as)


def setup_inputs(seed: int = 0) -> dict:
    seeds = jax.random.split(jax.random.key(seed), 12)
    grid_field = heavy_noise(seeds[0], (NLON, NLAT, LEVELS, D1), 1.0, 6.0, ((0, 8), (1, 16)), (1, 3, 16, 2.0))
    fine_weights = gaussian(seeds[1], (D1, 4 * D1), D1 ** -0.5, 0.25)
    fine_gain = jnp.clip(1.0 + 0.18 * jax.random.normal(seeds[2], (D1,), jnp.float32), 0.1, 1.9)
    fine_scales = jnp.clip(jnp.exp(jax.random.uniform(seeds[3], (H1,), jnp.float32, math.log(4.0), math.log(16.0))), 4.0, 16.0)
    merge_gain = jnp.clip(1.0 + 0.18 * jax.random.normal(seeds[4], (4 * D1,), jnp.float32), 0.1, 1.9)
    merge_weight = gaussian(seeds[5], (4 * D1, D2), (4 * D1) ** -0.5, 0.125)
    coarse_weights = gaussian(seeds[6], (D2, 4 * D2), D2 ** -0.5, 0.1875)
    coarse_gain = jnp.clip(1.0 + 0.18 * jax.random.normal(seeds[7], (D2,), jnp.float32), 0.1, 1.9)
    coarse_scales = jnp.clip(jnp.exp(jax.random.uniform(seeds[8], (H2,), jnp.float32, math.log(4.0), math.log(16.0))), 4.0, 16.0)
    cot_fine = gaussian(seeds[9], (NLON, NLAT, LEVELS, D1), 1.0, 6.0, ((0, 8), (1, 16)))
    cot_coarse = gaussian(seeds[10], (NLON // 2, NLAT // 2, LEVELS, D2), 1.0, 6.0, ((0, 8), (1, 16)))
    return dict(grid_field=grid_field, fine_weights=fine_weights, fine_gain=fine_gain, fine_scales=fine_scales, merge_gain=merge_gain, merge_weight=merge_weight, coarse_weights=coarse_weights, coarse_gain=coarse_gain, coarse_scales=coarse_scales, cot_fine=cot_fine, cot_coarse=cot_coarse)


EPS_NORM = 1e-05
EPS_HEAD = 1e-06

def layer_norm(values, gain_vec):
    center = values - lax.optimization_barrier(jnp.mean(values, -1, keepdims=True))
    inverse = lax.rsqrt(lax.optimization_barrier(jnp.mean(center * center, -1, keepdims=True)) + EPS_NORM)
    normed = center * inverse
    return (normed * gain_vec, normed, inverse)

def layer_norm_back(grad_vals, normed, inverse, gain_vec):
    scaled = grad_vals * gain_vec
    return inverse * (scaled - lax.optimization_barrier(jnp.mean(scaled, -1, keepdims=True)) - normed * lax.optimization_barrier(jnp.mean(scaled * normed, -1, keepdims=True)))

def unit_heads(values, head_count):
    shaped = values.reshape(values.shape[:-1] + (head_count, values.shape[-1] // head_count))
    inverse = lax.rsqrt(lax.optimization_barrier(jnp.mean(shaped * shaped, -1, keepdims=True)) + EPS_HEAD)
    return (shaped * inverse, inverse)

def attn_parts(qkv_all, scales, window_marks, head_count):
    feat_width = qkv_all.shape[-1] // 3
    head_size = feat_width // head_count
    q_unit, q_inverse = unit_heads(qkv_all[..., :feat_width], head_count)
    k_unit, k_inverse = unit_heads(qkv_all[..., feat_width:2 * feat_width], head_count)
    q_scaled = (q_unit * (scales[:, None] / head_size)).astype(jnp.bfloat16)
    k_round = k_unit.astype(jnp.bfloat16)
    v_round = qkv_all[..., 2 * feat_width:].reshape(q_unit.shape).astype(jnp.bfloat16)
    scores = jnp.einsum('wqhd,wkhd->whqk', q_scaled.astype(jnp.float32), k_round.astype(jnp.float32))
    keep_mask = (window_marks[:, :, None] == window_marks[:, None, :]).astype(jnp.float32)
    raw_weights = jnp.exp(scores) * keep_mask[:, None]
    soft_weights = raw_weights / lax.optimization_barrier(jnp.sum(raw_weights, -1, keepdims=True))
    return (q_unit, q_inverse, k_unit, k_inverse, q_scaled, k_round, v_round, soft_weights)

def attend(qkv_all, scales, window_marks, head_count):
    parts_out = attn_parts(qkv_all, scales, window_marks, head_count)
    prob_round = parts_out[7].astype(jnp.bfloat16)
    attended = jnp.einsum('whqk,wkhd->wqhd', prob_round.astype(jnp.float32), parts_out[6].astype(jnp.float32))
    return attended.reshape(attended.shape[:2] + (-1,)).astype(jnp.bfloat16)

def attend_back(qkv_all, grad_att, scales, window_marks, head_count):
    q_unit, q_inverse, k_unit, k_inverse, q_scaled, k_round, v_round, soft_weights = attn_parts(qkv_all, scales, window_marks, head_count)
    head_size = q_unit.shape[-1]
    prob_round = soft_weights.astype(jnp.bfloat16).astype(jnp.float32)
    grad_heads = grad_att.reshape(v_round.shape).astype(jnp.float32)
    grad_probs = jnp.einsum('wqhd,wkhd->whqk', grad_heads, v_round.astype(jnp.float32))
    grad_values = jnp.einsum('whqk,wqhd->wkhd', prob_round, grad_heads)
    grad_scores = (soft_weights * (grad_probs - lax.optimization_barrier(jnp.sum(grad_probs * soft_weights, -1, keepdims=True)))).astype(jnp.bfloat16)
    grad_qscaled = jnp.einsum('whqk,wkhd->wqhd', grad_scores.astype(jnp.float32), k_round.astype(jnp.float32))
    grad_kunit = jnp.einsum('whqk,wqhd->wkhd', grad_scores.astype(jnp.float32), q_scaled.astype(jnp.float32))
    grad_qunit = grad_qscaled * (scales[:, None] / head_size)
    grad_query = q_inverse * (grad_qunit - q_unit * lax.optimization_barrier(jnp.mean(grad_qunit * q_unit, -1, keepdims=True)))
    grad_key = k_inverse * (grad_kunit - k_unit * lax.optimization_barrier(jnp.mean(grad_kunit * k_unit, -1, keepdims=True)))
    flat_shape = grad_att.shape
    joined = jnp.concatenate([grad_query.reshape(flat_shape), grad_key.reshape(flat_shape), grad_values.reshape(flat_shape)], -1)
    return joined.astype(jnp.bfloat16)

def to_windows(grid_tile, win_lon, win_lat):
    lon_count, lat_count, levels, feat_width = grid_tile.shape
    shaped = grid_tile.reshape(lon_count // win_lon, win_lon, lat_count // win_lat, win_lat, levels, feat_width)
    return shaped.transpose(0, 2, 1, 3, 4, 5).reshape(-1, win_lon * win_lat * levels, feat_width)

def from_windows(windows, lon_count, lat_count, win_lon, win_lat):
    feat_width = windows.shape[-1]
    levels = windows.shape[1] // (win_lon * win_lat)
    shaped = windows.reshape(lon_count // win_lon, lat_count // win_lat, win_lon, win_lat, levels, feat_width)
    return shaped.transpose(0, 2, 1, 3, 4, 5).reshape(lon_count, lat_count, levels, feat_width)

def window_marks_of(row_flags_vec, lon_count, levels, win_lon, win_lat):
    grid_marks = jnp.broadcast_to(row_flags_vec[None, :, None, None], (lon_count, row_flags_vec.shape[0], levels, 1))
    return to_windows(grid_marks, win_lon, win_lat)[..., 0]

def grouped(function, groups, *arrays):
    stacked = [part.reshape((groups, -1) + part.shape[1:]) for part in arrays]
    result = lax.map(lambda part_list: function(*part_list), stacked)
    return result.reshape((-1,) + result.shape[2:])

def merge_cells(grid_tile):
    lon_count, lat_count, levels, feat_width = grid_tile.shape
    shaped = grid_tile.reshape(lon_count // 2, 2, lat_count // 2, 2, levels, feat_width)
    return shaped.transpose(0, 2, 4, 1, 3, 5).reshape(lon_count // 2, lat_count // 2, levels, 4 * feat_width)

def split_cells(values, feat_width):
    lon_half, lat_half, levels = values.shape[:3]
    shaped = values.reshape(lon_half, lat_half, levels, 2, 2, feat_width)
    return shaped.transpose(0, 3, 1, 4, 2, 5).reshape(2 * lon_half, 2 * lat_half, levels, feat_width)

def roll_grid(grid_tile):
    return jnp.roll(jnp.roll(grid_tile, -S_LON, 0), -S_LAT, 1)

def unroll_grid(grid_tile):
    return jnp.roll(jnp.roll(grid_tile, S_LAT, 1), S_LON, 0)

def sublayer(block_tile, weights, gain_vec, scales, window_marks, head_count):
    lon_count, lat_count, levels, feat_width = block_tile.shape
    values = block_tile.astype(jnp.float32)
    scaled, normed, inverse = layer_norm(values, gain_vec)
    normed_round = scaled.astype(jnp.bfloat16)
    qkv_all = jnp.dot(normed_round.reshape(-1, feat_width), weights[:, :3 * feat_width], preferred_element_type=jnp.float32)
    qkv_windows = to_windows(qkv_all.reshape(lon_count, lat_count, levels, 3 * feat_width), WLON, WLAT)
    att_windows = grouped(lambda qkv_part, mark_part: attend(qkv_part, scales, mark_part, head_count), lon_count // WLON, qkv_windows, window_marks)
    attended = from_windows(att_windows, lon_count, lat_count, WLON, WLAT)
    projected = jnp.dot(attended.reshape(-1, feat_width), weights[:, 3 * feat_width:], preferred_element_type=jnp.float32)
    out_tile = (values + projected.reshape(values.shape)).astype(jnp.bfloat16)
    return (out_tile, (normed_round, normed, inverse, qkv_windows, attended))

def sublayer_back(cot_round, saved, weights, gain_vec, scales, window_marks, head_count, want_grads):
    normed_round, normed, inverse, qkv_windows, attended = saved
    lon_count, lat_count, levels, feat_width = cot_round.shape
    cot_flat = cot_round.reshape(-1, feat_width)
    grad_att = jnp.dot(cot_flat, weights[:, 3 * feat_width:].T, preferred_element_type=jnp.float32).astype(jnp.bfloat16)
    att_windows = to_windows(grad_att.reshape(cot_round.shape), WLON, WLAT)
    grad_windows = grouped(lambda qkv_part, grad_part, mark_part: attend_back(qkv_part, grad_part, scales, mark_part, head_count), lon_count // WLON, qkv_windows, att_windows, window_marks)
    grad_qkv = from_windows(grad_windows, lon_count, lat_count, WLON, WLAT).reshape(-1, 3 * feat_width)
    grad_normed = jnp.dot(grad_qkv, weights[:, :3 * feat_width].T, preferred_element_type=jnp.float32)
    grad_in = cot_round.astype(jnp.float32) + layer_norm_back(grad_normed.reshape(normed.shape), normed, inverse, gain_vec)
    if want_grads:
        grad_proj = jnp.dot(normed_round.reshape(-1, feat_width).T, grad_qkv, preferred_element_type=jnp.float32)
        grad_out = jnp.dot(attended.reshape(-1, feat_width).T, cot_flat, preferred_element_type=jnp.float32)
        return (grad_in, jnp.concatenate([grad_proj, grad_out], 1))
    else:
        return (grad_in, None)

def level_forward(grid_field, weights, gain_vec, scales, head_count):
    rolled = roll_grid(grid_field)
    lon_count, lat_count, levels = rolled.shape[:3]
    row_flags_vec = (jnp.arange(lat_count) >= lat_count - S_LAT).astype(jnp.int32)
    window_marks = window_marks_of(row_flags_vec, lon_count, levels, WLON, WLAT)
    out_tile, saved = sublayer(rolled, weights, gain_vec, scales, window_marks, head_count)
    return (unroll_grid(out_tile), (saved, window_marks))

def level_backward(cot_grid, state, weights, gain_vec, scales, head_count, want_grads):
    saved, window_marks = state
    grad_in, grad_w = sublayer_back(roll_grid(cot_grid), saved, weights, gain_vec, scales, window_marks, head_count, want_grads)
    return (unroll_grid(grad_in.astype(jnp.bfloat16)), grad_w)

def reference(grid_field, fine_weights, fine_gain, fine_scales, merge_gain, merge_weight, coarse_weights, coarse_gain, coarse_scales, cot_fine, cot_coarse):
    feat_width = grid_field.shape[-1]
    fine_out, fine_state = level_forward(grid_field, fine_weights, fine_gain, fine_scales, H1)
    merged = merge_cells(fine_out).astype(jnp.float32)
    merge_scaled, merge_normed, merge_inverse = layer_norm(merged, merge_gain)
    merge_round = merge_scaled.astype(jnp.bfloat16)
    coarse_flat = jnp.dot(merge_round.reshape(-1, 4 * feat_width), merge_weight, preferred_element_type=jnp.float32)
    coarse_in = coarse_flat.astype(jnp.bfloat16).reshape(merged.shape[:3] + (merge_weight.shape[1],))
    coarse_out, coarse_state = level_forward(coarse_in, coarse_weights, coarse_gain, coarse_scales, H2)
    coarse_grad, unused = level_backward(cot_coarse, coarse_state, coarse_weights, coarse_gain, coarse_scales, H2, False)
    grad_merge = jnp.dot(coarse_grad.reshape(-1, coarse_grad.shape[-1]), merge_weight.T, preferred_element_type=jnp.float32)
    grad_cells = split_cells(layer_norm_back(grad_merge.reshape(merged.shape), merge_normed, merge_inverse, merge_gain), feat_width)
    fine_cot = (cot_fine.astype(jnp.float32) + grad_cells).astype(jnp.bfloat16)
    grad_input, grad_weights = level_backward(fine_cot, fine_state, fine_weights, fine_gain, fine_scales, H1, True)
    return (coarse_out, grad_input, grad_weights)
```

```python
import functools

import jax
import jax.numpy as jnp
from jax import lax
from jax.experimental import pallas as pl
from jax.experimental.pallas import tpu as pltpu
from jax.sharding import Mesh, PartitionSpec as P

F32 = jnp.float32
BF16 = jnp.bfloat16
EPS_NORM = 1e-05
EPS_HEAD = 1e-06
D1, D2, H1, H2 = 512, 1024, 8, 16
HEAD = 64
TOK = 216
LON, LAT, LEV = 24, 12, 3
GROUPS = LAT * LEV
EDGE = 9
ROWS = GROUPS * LON
WIN = 12
VMEM_BYTES = 56 * 1024 * 1024


def dot(left, right, left_dim, right_dim):
    return lax.dot_general(
        left, right, (((left_dim,), (right_dim,)), ((), ())), preferred_element_type=F32
    )


def mean_last(values):
    return jnp.mean(values, -1, keepdims=True)


def normalize(values):
    center = values - mean_last(values)
    inverse = lax.rsqrt(mean_last(center * center) + EPS_NORM)
    return center * inverse, inverse


def norm_back(scaled, normed, inverse):
    return inverse * (scaled - mean_last(scaled) - normed * mean_last(scaled * normed))


def keep_matrix(last_ref):
    half = TOK // 2
    keys = lax.broadcasted_iota(jnp.int32, (TOK, TOK), 0) >= half
    queries = lax.broadcasted_iota(jnp.int32, (TOK, TOK), 1) >= half
    apart = jnp.where(keys == queries, 0.0, 1.0)
    return 1.0 - apart * last_ref[0].astype(F32)


def unit_rows(values):
    inverse = lax.rsqrt(jnp.mean(values * values, 0, keepdims=True) + EPS_HEAD)
    return values * inverse, inverse


def probabilities(k_round, q_scaled, keep):
    raw = jnp.exp(dot(k_round, q_scaled, 0, 0)) * keep
    return raw * (1.0 / jnp.sum(raw, 0, keepdims=True))


def head_back(grad, q_scaled, k_round, v_round, soft, soft_round, q_inverse, k_inverse, scale):
    grad_probs = dot(v_round, grad, 0, 0)
    grad_value = dot(grad, soft_round, 1, 1)
    centered = grad_probs - jnp.sum(grad_probs * soft, 0, keepdims=True)
    grad_scores = (soft * centered).astype(BF16)
    grad_q = dot(k_round, grad_scores, 1, 0)
    grad_k = dot(q_scaled, grad_scores, 1, 1)
    q_wide = q_scaled.astype(F32)
    k_wide = k_round.astype(F32)
    q_mean = jnp.mean(grad_q * q_wide, 0, keepdims=True)
    grad_query = q_inverse * (grad_q * scale - q_wide * (q_mean * (1.0 / scale)))
    grad_key = k_inverse * (grad_k - k_wide * jnp.mean(grad_k * k_wide, 0, keepdims=True))
    return grad_query, grad_key, grad_value


def head_rows(part, width, head):
    return pl.ds(pl.multiple_of(part * width + head * HEAD, HEAD), HEAD)


def fine_forward_kernel(
    x_ref, lat_ref, lon_ref, corner_ref, wt_ref, wo_ref, gain_ref, scale_ref, last_ref,
    y_ref, ylat_ref, ylon_ref, ycor_ref, xw_ref, qkv_ref, inv_ref, soft_ref, att_ref,
    cat, wins, full, qkv, keep,
):
    tile = x_ref[...].astype(F32).reshape(GROUPS, LON, D1)
    cat[0 : GROUPS - EDGE, 0:LON, :] = tile[EDGE:]
    cat[GROUPS - EDGE :, 0:LON, :] = lat_ref[...].astype(F32).reshape(EDGE, LON, D1)
    cat[0 : GROUPS - EDGE, LON:, :] = lon_ref[...].astype(F32).reshape(GROUPS - EDGE, 8, D1)
    cat[GROUPS - EDGE :, LON:, :] = corner_ref[...].astype(F32).reshape(EDGE, 8, D1)
    for win in range(4):
        for group in range(18):
            row = 6 + WIN * (win % 2)
            wins[win, WIN * group : WIN * group + WIN, :] = cat[
                18 * (win // 2) + group, row : row + WIN, :
            ]
    keep[...] = keep_matrix(last_ref)

    def window(win, carry):
        values = wins[win]
        xw_ref[win] = values.astype(BF16)
        normed = (normalize(values)[0] * gain_ref[...]).astype(BF16)
        for part in range(3):
            qkv[part * D1 : part * D1 + D1, :] = dot(
                wt_ref[part * D1 : part * D1 + D1, :], normed, 1, 1
            )
        use_keep = jnp.where(win >= 2, keep[...], 1.0)
        for head in range(H1):
            rows = slice(head * HEAD, head * HEAD + HEAD)
            krows = slice(D1 + head * HEAD, D1 + head * HEAD + HEAD)
            vrows = slice(2 * D1 + head * HEAD, 2 * D1 + head * HEAD + HEAD)
            q_unit, q_inverse = unit_rows(qkv[rows, :])
            k_unit, k_inverse = unit_rows(qkv[krows, :])
            q_scaled = (q_unit * (scale_ref[head] / HEAD)).astype(BF16)
            k_round = k_unit.astype(BF16)
            v_round = qkv[vrows, :].astype(BF16)
            qkv_ref[win, rows, :] = q_scaled
            qkv_ref[win, krows, :] = k_round
            qkv_ref[win, vrows, :] = v_round
            inv_ref[win, head : head + 1, :] = q_inverse
            inv_ref[win, H1 + head : H1 + head + 1, :] = k_inverse
            soft = probabilities(k_round, q_scaled, use_keep).astype(BF16)
            soft_ref[win, head] = soft
            att_ref[win, rows, :] = dot(v_round, soft, 1, 0).astype(BF16)
        wins[win] = values + dot(att_ref[win], wo_ref[...], 0, 0)
        return carry

    lax.fori_loop(0, 4, window, 0)
    for win in range(4):
        for group in range(18):
            row = WIN * (win % 2)
            full[18 * (win // 2) + group, row : row + WIN, :] = wins[
                win, WIN * group : WIN * group + WIN, :
            ]
    done = full[...]
    y_ref[...] = done.reshape(ROWS, D1).astype(BF16)
    ylat_ref[...] = done[:EDGE].reshape(EDGE * LON, D1).astype(BF16)
    ylon_ref[...] = done[EDGE:, 0:8].reshape((GROUPS - EDGE) * 8, D1).astype(BF16)
    ycor_ref[...] = done[:EDGE, 0:8].reshape(EDGE * 8, D1).astype(BF16)


def coarse_kernel(
    y_ref, lat_ref, lon_ref, corner_ref, cotf_ref, cotc_ref, mgain_ref, mw_ref, cw_ref, cwt_ref, gain_ref,
    scale_ref, last_ref,
    out_ref, g_ref, glat_ref, glon_ref, gcor_ref,
    cat, merged, mnorm, minv, qkv, gqkv, gatt, att, turned, keep,
):
    tile = y_ref[...].astype(F32).reshape(GROUPS, LON, D1)
    lat_rows = lat_ref[...].astype(F32).reshape(EDGE, LON, D1)
    lon_rows = lon_ref[...].astype(F32).reshape(GROUPS - EDGE, 8, D1)
    corner_rows = corner_ref[...].astype(F32).reshape(EDGE, 8, D1)
    for cut in range(4):
        lanes = slice(cut * 128, cut * 128 + 128)
        cat[cut, 0 : GROUPS - EDGE, 0:LON, :] = tile[EDGE:, :, lanes]
        cat[cut, GROUPS - EDGE :, 0:LON, :] = lat_rows[:, :, lanes]
        cat[cut, 0 : GROUPS - EDGE, LON:, :] = lon_rows[:, :, lanes]
        cat[cut, GROUPS - EDGE :, LON:, :] = corner_rows[:, :, lanes]
    for group in range(18):
        for part in range(4):
            source = (2 * (group // LEV) + part % 2) * LEV + group % LEV
            for cut in range(4):
                merged[
                    WIN * group : WIN * group + WIN,
                    part * D1 + cut * 128 : part * D1 + cut * 128 + 128,
                ] = cat[cut, source, pl.ds(6 + part // 2, WIN, stride=2), :]
    for start in range(0, TOK, 72):
        normed, inverse = normalize(merged[start : start + 72, :])
        merged[start : start + 72, :] = normed
        minv[start : start + 72, :] = jnp.broadcast_to(inverse, (72, 128))
        mnorm[start : start + 72, :] = normed * mgain_ref[...]
    keep[...] = keep_matrix(last_ref)
    values = dot(mnorm[...].astype(BF16), mw_ref[...], 1, 0).astype(BF16).astype(F32)
    value_norm, value_inverse = normalize(values)
    normed = (value_norm * gain_ref[...]).astype(BF16)
    for start in range(0, 3 * D2, 512):
        qkv[start : start + 512, :] = dot(cwt_ref[start : start + 512, :], normed, 1, 1)
    for start in range(0, D2, 512):
        gatt[start : start + 512, :] = dot(
            cw_ref[start : start + 512, 3 * D2 :], cotc_ref[...], 1, 1
        ).astype(BF16)

    def heads(step, carry):
        for inner in range(4):
            head = step * 4 + inner
            rows = head_rows(0, D2, head)
            krows = head_rows(1, D2, head)
            vrows = head_rows(2, D2, head)
            scale = scale_ref[head] / HEAD
            q_unit, q_inverse = unit_rows(qkv[rows, :])
            k_unit, k_inverse = unit_rows(qkv[krows, :])
            q_scaled = (q_unit * scale).astype(BF16)
            k_round = k_unit.astype(BF16)
            v_round = qkv[vrows, :].astype(BF16)
            soft = probabilities(k_round, q_scaled, keep[...])
            soft_round = soft.astype(BF16)
            att[rows, :] = dot(v_round, soft_round, 1, 0).astype(BF16)
            grads = head_back(
                gatt[rows, :], q_scaled, k_round, v_round, soft, soft_round, q_inverse, k_inverse, scale
            )
            gqkv[rows, :] = grads[0].astype(BF16)
            gqkv[krows, :] = grads[1].astype(BF16)
            gqkv[vrows, :] = grads[2].astype(BF16)
        return carry

    lax.fori_loop(0, H2 // 4, heads, 0)
    out_ref[...] = (values + dot(att[...], cw_ref[:, 3 * D2 :], 0, 0)).astype(BF16)
    for start in range(0, D2, 256):
        turned[start : start + 256, :] = dot(
            cw_ref[start : start + 256, : 3 * D2], gqkv[...], 1, 0
        )
    scaled = turned[...].T * gain_ref[...]
    grad_in = cotc_ref[...].astype(F32) + norm_back(scaled, value_norm, value_inverse)
    grad_in = grad_in.astype(BF16)
    for part in range(4):
        cols = slice(part * D1, part * D1 + D1)
        mnorm[:, cols] = dot(grad_in, mw_ref[cols, :], 1, 1) * mgain_ref[:, cols]
    for start in range(0, TOK, 72):
        mnorm[start : start + 72, :] = norm_back(
            mnorm[start : start + 72, :], merged[start : start + 72, :], minv[start : start + 72, 0:1]
        )
    for group in range(18):
        for part in range(4):
            target = (2 * (group // LEV) + part % 2) * LEV + group % LEV
            for cut in range(4):
                cat[cut, target, pl.ds(part // 2, WIN, stride=2), :] = mnorm[
                    WIN * group : WIN * group + WIN,
                    part * D1 + cut * 128 : part * D1 + cut * 128 + 128,
                ]
    cells = jnp.concatenate([cat[cut, :, 0:LON, :] for cut in range(4)], -1)
    done = cells + cotf_ref[...].astype(F32).reshape(GROUPS, LON, D1)
    g_ref[...] = done.reshape(ROWS, D1).astype(BF16)
    glat_ref[...] = done[GROUPS - EDGE :].reshape(EDGE * LON, D1).astype(BF16)
    glon_ref[...] = done[: GROUPS - EDGE, 16:].reshape((GROUPS - EDGE) * 8, D1).astype(BF16)
    gcor_ref[...] = done[GROUPS - EDGE :, 16:].reshape(EDGE * 8, D1).astype(BF16)


def fine_backward_kernel(
    g_ref, lat_ref, lon_ref, corner_ref, xw_ref, qkv_ref, inv_ref, soft_ref, att_ref, w_ref, gain_ref, scale_ref,
    gqkv_ref, e_ref, gw_ref,
    cat, wins, gatt, normt, gq, ewin,
):
    tile = g_ref[...].astype(F32).reshape(GROUPS, LON, D1)
    cat[EDGE:, 8:, :] = tile[: GROUPS - EDGE]
    cat[0:EDGE, 8:, :] = lat_ref[...].astype(F32).reshape(EDGE, LON, D1)
    cat[EDGE:, 0:8, :] = lon_ref[...].astype(F32).reshape(GROUPS - EDGE, 8, D1)
    cat[0:EDGE, 0:8, :] = corner_ref[...].astype(F32).reshape(EDGE, 8, D1)
    for win in range(4):
        for group in range(18):
            row = 2 + WIN * (win % 2)
            wins[win, WIN * group : WIN * group + WIN, :] = cat[
                18 * (win // 2) + group, row : row + WIN, :
            ]
    normt[...] = jnp.zeros_like(normt)
    gq[...] = jnp.zeros_like(gq)

    def window(win, carry):
        cot = wins[win].astype(BF16)
        e_ref[win] = cot
        gatt[...] = dot(w_ref[:, 3 * D1 :], cot, 1, 1).astype(BF16)
        normed = (normalize(xw_ref[win].astype(F32))[0] * gain_ref[...]).astype(BF16)
        normt[win, :, 0:TOK] = normed.T
        for head in range(H1):
            rows = slice(head * HEAD, head * HEAD + HEAD)
            krows = slice(D1 + head * HEAD, D1 + head * HEAD + HEAD)
            vrows = slice(2 * D1 + head * HEAD, 2 * D1 + head * HEAD + HEAD)
            soft_round = soft_ref[win, head]
            grads = head_back(
                gatt[rows, :], qkv_ref[win, rows, :], qkv_ref[win, krows, :], qkv_ref[win, vrows, :],
                soft_round.astype(F32), soft_round,
                inv_ref[win, head : head + 1, :], inv_ref[win, H1 + head : H1 + head + 1, :],
                scale_ref[head] / HEAD,
            )
            gq[win, rows, 0:TOK] = grads[0].astype(BF16)
            gq[win, krows, 0:TOK] = grads[1].astype(BF16)
            gq[win, vrows, 0:TOK] = grads[2].astype(BF16)
        return carry

    lax.fori_loop(0, 4, window, 0)
    for win in range(4):
        gqkv_ref[win] = gq[win, :, 0:TOK]
    for start in range(0, 3 * D1, 256):
        total = dot(normt[0], gq[0, start : start + 256, :], 1, 1)
        for win in range(1, 4):
            total += dot(normt[win], gq[win, start : start + 256, :], 1, 1)
        gw_ref[:, start : start + 256] = total.astype(BF16)
    total = dot(att_ref[0], e_ref[0], 1, 0)
    for win in range(1, 4):
        total += dot(att_ref[win], e_ref[win], 1, 0)
    gw_ref[:, 3 * D1 :] = total.astype(BF16)


def fine_input_kernel(
    gqkv_ref, e_ref, xw_ref, w_ref, gain_ref, g_ref, glat_ref, glon_ref, gcor_ref, full, turned
):
    for win in range(4):
        turned[...] = dot(w_ref[:, : 3 * D1], gqkv_ref[win], 1, 0)
        scaled = turned[...].T * gain_ref[...]
        normed, inverse = normalize(xw_ref[win].astype(F32))
        grad_in = e_ref[win].astype(F32) + norm_back(scaled, normed, inverse)
        for group in range(18):
            row = WIN * (win % 2)
            full[18 * (win // 2) + group, row : row + WIN, :] = grad_in[
                WIN * group : WIN * group + WIN, :
            ]
    done = full[...]
    g_ref[...] = done.reshape(ROWS, D1).astype(BF16)
    glat_ref[...] = done[GROUPS - EDGE :].reshape(EDGE * LON, D1).astype(BF16)
    glon_ref[...] = done[: GROUPS - EDGE, 16:].reshape((GROUPS - EDGE) * 8, D1).astype(BF16)
    gcor_ref[...] = done[GROUPS - EDGE :, 16:].reshape(EDGE * 8, D1).astype(BF16)


def call(kernel, outs, scratch, smem_from, args, name):
    whole = pl.BlockSpec(memory_space=pltpu.VMEM)
    scalars = pl.BlockSpec(memory_space=pltpu.SMEM)
    return pl.pallas_call(
        kernel,
        out_shape=[jax.ShapeDtypeStruct(shape, kind) for shape, kind in outs],
        in_specs=[scalars if position in smem_from else whole for position in range(len(args))],
        out_specs=[whole] * len(outs),
        scratch_shapes=[pltpu.VMEM(shape, kind) for shape, kind in scratch],
        compiler_params=pltpu.CompilerParams(vmem_limit_bytes=VMEM_BYTES),
        name=name,
    )(*args)


SLABS = [
    ((ROWS, D1), BF16),
    ((EDGE * LON, D1), BF16),
    (((GROUPS - EDGE) * 8, D1), BF16),
    ((EDGE * 8, D1), BF16),
]


def fine_forward(tile, halos, wt, wo, gain, scales, last):
    outs = SLABS + [
        ((4, TOK, D1), BF16),
        ((4, 3 * D1, TOK), BF16),
        ((4, 2 * H1, TOK), F32),
        ((4, H1, TOK, TOK), BF16),
        ((4, D1, TOK), BF16),
    ]
    scratch = [
        ((GROUPS, 32, D1), F32),
        ((4, TOK, D1), F32),
        ((GROUPS, LON, D1), F32),
        ((3 * D1, TOK), F32),
        ((TOK, TOK), F32),
    ]
    args = (tile, *halos, wt, wo, gain, scales, last)
    return call(fine_forward_kernel, outs, scratch, (7, 8), args, "fine_forward")


def coarse_both(tile, halos, cot_fine, cot_coarse, mgain, mw, cw, cwt, gain, scales, last):
    outs = [((TOK, D2), BF16)] + SLABS
    scratch = [
        ((4, GROUPS, 32, 128), F32),
        ((TOK, 4 * D1), F32),
        ((TOK, 4 * D1), F32),
        ((TOK, 128), F32),
        ((3 * D2, TOK), F32),
        ((3 * D2, TOK), BF16),
        ((D2, TOK), BF16),
        ((D2, TOK), BF16),
        ((D2, TOK), F32),
        ((TOK, TOK), F32),
    ]
    args = (tile, *halos, cot_fine, cot_coarse, mgain, mw, cw, cwt, gain, scales, last)
    return call(coarse_kernel, outs, scratch, (11, 12), args, "coarse_both")


def fine_backward(tile, halos, xw, qkv, inv, soft, att, weights, gain, scales):
    outs = [((4, 3 * D1, TOK), BF16), ((4, TOK, D1), BF16), ((D1, 4 * D1), BF16)]
    scratch = [
        ((GROUPS, 32, D1), F32),
        ((4, TOK, D1), F32),
        ((D1, TOK), BF16),
        ((4, D1, 256), BF16),
        ((4, 3 * D1, 256), BF16),
        ((8, 128), F32),
    ]
    args = (tile, *halos, xw, qkv, inv, soft, att, weights, gain, scales)
    return call(fine_backward_kernel, outs, scratch, (11,), args, "fine_backward")


def fine_input(gqkv, cot, xw, weights, gain):
    scratch = [((GROUPS, LON, D1), F32), ((D1, TOK), F32)]
    return call(fine_input_kernel, SLABS, scratch, (), (gqkv, cot, xw, weights, gain), "fine_input")


def ring(axis_size, step):
    return [(i, (i + step) % axis_size) for i in range(axis_size)]


def exchange(lat_block, lon_block, corner, step):
    nlon, nlat = lax.axis_size("lon"), lax.axis_size("lat")
    both = [
        (i * nlat + j, ((i + step) % nlon) * nlat + (j + step) % nlat)
        for i in range(nlon)
        for j in range(nlat)
    ]
    lon_block = lax.ppermute(lon_block, "lon", ring(nlon, step))
    corner = lax.ppermute(corner, ("lon", "lat"), both)
    lat_block = lax.ppermute(lat_block, "lat", ring(nlat, step))
    return (lat_block, lon_block, corner)


def quarter_exchange(tile, step):
    lat_half, lon_half = tile.shape[0] // 2, tile.shape[2] // 2
    near = (slice(0, lat_half), slice(0, lon_half))
    far = (slice(lat_half, None), slice(lon_half, None))
    out, stay = (near, far) if step < 0 else (far, near)
    lat_block = tile[out[0], :, stay[1]]
    lon_block = tile[stay[0], :, out[1]]
    corner = tile[out[0], :, out[1]]
    lat_block, lon_block, corner = exchange(lat_block, lon_block, corner, step)
    own = tile[stay[0], :, stay[1]]
    if step < 0:
        upper = jnp.concatenate([own, lon_block], 2)
        lower = jnp.concatenate([lat_block, corner], 2)
    else:
        upper = jnp.concatenate([corner, lat_block], 2)
        lower = jnp.concatenate([lon_block, own], 2)
    return jnp.concatenate([upper, lower], 0)


def share_sum(grad):
    nlon, nlat = lax.axis_size("lon"), lax.axis_size("lat")
    pieces = lax.all_to_all(grad.reshape(nlon * nlat, -1, grad.shape[1]), ("lon", "lat"), 0, 0)
    return jnp.sum(pieces.astype(F32), 0)


def on_device(
    grid_field, fine_weights, fine_gain, fine_scales, merge_gain, merge_weight, coarse_weights, coarse_gain,
    coarse_scales, cot_fine, cot_coarse,
):
    last = (lax.axis_index("lat") == lax.axis_size("lat") - 1).astype(jnp.int32).reshape(1)
    tile = grid_field.transpose(1, 2, 0, 3).reshape(GROUPS, LON, D1)
    halos = exchange(
        tile[:EDGE].reshape(-1, D1), tile[EDGE:, :8].reshape(-1, D1), tile[:EDGE, :8].reshape(-1, D1), -1
    )
    cot_fine_c = quarter_exchange(cot_fine.transpose(1, 2, 0, 3), -1).reshape(ROWS, D1)
    cot_coarse_c = quarter_exchange(cot_coarse.transpose(1, 2, 0, 3), -1).reshape(TOK, D2)
    fine_gain = fine_gain.reshape(1, -1)
    fine_wt = fine_weights[:, : 3 * D1].T
    coarse_wt = coarse_weights[:, : 3 * D2].T
    forward = fine_forward(
        tile.reshape(ROWS, D1), halos, fine_wt, fine_weights[:, 3 * D1 :], fine_gain, fine_scales, last
    )
    halos = exchange(*forward[1:4], -1)
    coarse_out, *grad = coarse_both(
        forward[0], halos, cot_fine_c, cot_coarse_c, merge_gain.reshape(1, -1), merge_weight, coarse_weights,
        coarse_wt, coarse_gain.reshape(1, -1), coarse_scales, last,
    )
    halos = exchange(*grad[1:], 1)
    coarse_out = quarter_exchange(coarse_out.reshape(LAT // 2, LEV, LON // 2, D2), 1)
    saved = forward[4:]
    gqkv, cot, grad_weights = fine_backward(
        grad[0], halos, *saved, fine_weights, fine_gain, fine_scales
    )
    grad = fine_input(gqkv, cot, saved[0], fine_weights, fine_gain)
    lat_block, lon_block, corner = exchange(*grad[1:], 1)
    own = grad[0].reshape(GROUPS, LON, D1)[: GROUPS - EDGE, : LON - 6]
    lat_block = lat_block.reshape(EDGE, LON, D1)[:, : LON - 6]
    upper = jnp.concatenate([corner.reshape(EDGE, 8, D1)[:, 2:], lat_block], 1)
    lower = jnp.concatenate([lon_block.reshape(-1, 8, D1)[:, 2:], own], 1)
    grad_input = jnp.concatenate([upper, lower], 0).reshape(LAT, LEV, LON, D1)
    return (
        coarse_out.transpose(2, 0, 1, 3),
        grad_input.transpose(2, 0, 1, 3),
        share_sum(grad_weights),
    )


def solution(mesh):
    tile = P("lon", "lat", None, None)
    in_specs = (tile,) + (P(),) * 8 + (tile, tile)
    out_specs = (tile, tile, P(("lon", "lat"), None))
    return jax.shard_map(
        on_device, mesh=mesh, in_specs=in_specs, out_specs=out_specs, check_vma=False
    )
```

```python
import functools

import jax
import jax.numpy as jnp
from jax import lax
from jax.experimental import pallas as pl
from jax.experimental.pallas import tpu as pltpu
from jax.sharding import Mesh, PartitionSpec as P

F32 = jnp.float32
BF16 = jnp.bfloat16
EPS_NORM = 1e-05
EPS_HEAD = 1e-06
D1, D2, H1, H2 = 512, 1024, 8, 16
HEAD = 64
TOK = 216
LON, LAT, LEV = 24, 12, 3
GROUPS = LAT * LEV
EDGE = 9
ROWS = GROUPS * LON
WIN = 12
MIB = 1024 * 1024


def dot(left, right, left_dim, right_dim):
    return lax.dot_general(
        left, right, (((left_dim,), (right_dim,)), ((), ())), preferred_element_type=F32
    )


def mean_last(values):
    return jnp.mean(values, -1, keepdims=True)


def normalize(values):
    center = values - mean_last(values)
    inverse = lax.rsqrt(mean_last(center * center) + EPS_NORM)
    return center * inverse, inverse


def norm_back(scaled, normed, inverse):
    return inverse * (scaled - mean_last(scaled) - normed * mean_last(scaled * normed))


def keep_matrix(last_ref):
    half = TOK // 2
    keys = lax.broadcasted_iota(jnp.int32, (TOK, TOK), 0) >= half
    queries = lax.broadcasted_iota(jnp.int32, (TOK, TOK), 1) >= half
    apart = jnp.where(keys == queries, 0.0, 1.0)
    return 1.0 - apart * last_ref[0].astype(F32)


def unit_rows(values):
    inverse = lax.rsqrt(jnp.mean(values * values, 0, keepdims=True) + EPS_HEAD)
    return values * inverse, inverse


def probabilities(k_round, q_scaled, keep):
    raw = jnp.exp(dot(k_round, q_scaled, 0, 0)) * keep
    return raw * (1.0 / jnp.sum(raw, 0, keepdims=True))


def head_back(grad, q_scaled, k_round, v_round, soft, soft_round, q_inverse, k_inverse, scale):
    grad_probs = dot(v_round, grad, 0, 0)
    grad_value = dot(grad, soft_round, 1, 1)
    centered = grad_probs - jnp.sum(grad_probs * soft, 0, keepdims=True)
    grad_scores = (soft * centered).astype(BF16)
    grad_q = dot(k_round, grad_scores, 1, 0)
    grad_k = dot(q_scaled, grad_scores, 1, 1)
    q_wide = q_scaled.astype(F32)
    k_wide = k_round.astype(F32)
    q_mean = jnp.mean(grad_q * q_wide, 0, keepdims=True)
    grad_query = q_inverse * (grad_q * scale - q_wide * (q_mean * (1.0 / scale)))
    grad_key = k_inverse * (grad_k - k_wide * jnp.mean(grad_k * k_wide, 0, keepdims=True))
    return grad_query, grad_key, grad_value


def head_rows(part, width, head):
    return pl.ds(pl.multiple_of(part * width + head * HEAD, HEAD), HEAD)


def attention_forward(head, width, base, scale, keep, qkv):
    q_unit, q_inverse = unit_rows(qkv[base, :])
    k_unit, k_inverse = unit_rows(qkv[head_rows(1, width, head), :])
    q_scaled = (q_unit * scale).astype(BF16)
    k_round = k_unit.astype(BF16)
    v_round = qkv[head_rows(2, width, head), :].astype(BF16)
    return q_scaled, k_round, v_round, q_inverse, k_inverse, probabilities(k_round, q_scaled, keep)


def edges_kernel(x_ref, lat_ref, lon_ref, corner_ref, lon_rows, corner_rows):
    tile = x_ref[...].astype(F32).reshape(GROUPS, LON, D1)
    lat_ref[...] = tile[:EDGE].reshape(EDGE * LON, D1).astype(BF16)
    for group in range(GROUPS):
        rows = tile[group, 0:6]
        if group < EDGE:
            corner_rows[6 * group : 6 * group + 6, :] = rows
        else:
            lon_rows[6 * (group - EDGE) : 6 * (group - EDGE) + 6, :] = rows
    lon_ref[...] = lon_rows[...].astype(BF16)
    corner_ref[...] = corner_rows[...].astype(BF16)


def fine_forward_kernel(side, *refs):
    if side == 0:
        (x_ref, lat_ref, wt_ref, w_ref, gain_ref, scale_ref, last_ref,
         y_ref, ylat_ref, ylon_ref, ycor_ref, xw_ref, qkv_ref, inv_ref, soft_ref, att_ref,
         wins, qkv, keep, lon_rows, corner_rows) = refs
    else:
        (x_ref, lat_ref, lon_ref, corner_ref, first_ref, wt_ref, w_ref, gain_ref, scale_ref, last_ref,
         y_ref, ylat_ref, xw_ref, qkv_ref, inv_ref, soft_ref, att_ref, wins, qkv, keep) = refs
    tile = x_ref[...].astype(F32).reshape(GROUPS, LON, D1)
    lat_rows = lat_ref[...].astype(F32).reshape(EDGE, LON, D1)
    if side == 1:
        lon_in = lon_ref[...].astype(F32)
        corner_in = corner_ref[...].astype(F32)
    for group in range(GROUPS):
        source = tile[group + EDGE] if group + EDGE < GROUPS else lat_rows[group + EDGE - GROUPS]
        win, row = group // 18, WIN * (group % 18)
        if side == 0:
            wins[win, row : row + WIN, :] = source[6:18]
        else:
            wins[win, row : row + 6, :] = source[18:24]
            if group + EDGE < GROUPS:
                halo = lon_in[6 * group : 6 * group + 6]
            else:
                halo = corner_in[6 * (group + EDGE - GROUPS) : 6 * (group + EDGE - GROUPS) + 6]
            wins[win, row + 6 : row + WIN, :] = halo
    keep[...] = keep_matrix(last_ref)

    def window(win, carry):
        values = wins[win]
        xw_ref[win] = values.astype(BF16)
        normed = (normalize(values)[0] * gain_ref[...]).astype(BF16)
        for part in range(3):
            qkv[part * D1 : part * D1 + D1, :] = dot(
                wt_ref[part * D1 : part * D1 + D1, :], normed, 1, 1
            )
        use_keep = jnp.where(win >= 1, keep[...], 1.0)
        for head in range(H1):
            rows = slice(head * HEAD, head * HEAD + HEAD)
            krows = slice(D1 + head * HEAD, D1 + head * HEAD + HEAD)
            vrows = slice(2 * D1 + head * HEAD, 2 * D1 + head * HEAD + HEAD)
            q_scaled, k_round, v_round, q_inverse, k_inverse, soft = attention_forward(
                head, D1, rows, scale_ref[head] / HEAD, use_keep, qkv
            )
            qkv_ref[win, rows, :] = q_scaled
            qkv_ref[win, krows, :] = k_round
            qkv_ref[win, vrows, :] = v_round
            inv_ref[win, head : head + 1, :] = q_inverse
            inv_ref[win, H1 + head : H1 + head + 1, :] = k_inverse
            soft = soft.astype(BF16)
            soft_ref[win, head] = soft
            att_ref[win, rows, :] = dot(v_round, soft, 1, 0).astype(BF16)
        result = values + dot(att_ref[win], w_ref[:, 3 * D1 :], 0, 0)
        wins[win] = result
        y_ref[win] = result.astype(BF16)
        return carry

    lax.fori_loop(0, 2, window, 0)
    if side == 0:
        ylat_ref[...] = wins[0, 0:112, :].astype(BF16)
        for group in range(GROUPS):
            rows = wins[group // 18, WIN * (group % 18) : WIN * (group % 18) + 6, :]
            if group < EDGE:
                corner_rows[6 * group : 6 * group + 6, :] = rows
            else:
                lon_rows[6 * (group - EDGE) : 6 * (group - EDGE) + 6, :] = rows
        ylon_ref[...] = lon_rows[...].astype(BF16)
        ycor_ref[...] = corner_rows[...].astype(BF16)
    else:
        ylat_ref[0:112, :] = first_ref[...]
        ylat_ref[112:224, :] = wins[0, 0:112, :].astype(BF16)


def coarse_kernel(
    y0_ref, y1_ref, lat_ref, lon_ref, corner_ref, cotc_ref, mgain_ref, mw_ref, cw_ref, gain_ref,
    scale_ref, last_ref,
    out_ref, g_ref, glat_ref, glon_ref, gcor_ref,
    near, far, halo, cells, merged, mnorm, minv, qkv, gqkv, gatt, att, turned, keep, lon_rows, corner_rows,
):
    for cut in range(4):
        lanes = slice(cut * 128, cut * 128 + 128)
        for win in range(2):
            near[cut, TOK * win : TOK * win + TOK, :] = y0_ref[win, :, lanes].astype(F32)
            far[cut, TOK * win : TOK * win + TOK, :] = y1_ref[win, :, lanes].astype(F32)
        near[cut, 2 * TOK :, :] = lat_ref[0:112, lanes].astype(F32)
        far[cut, 2 * TOK :, :] = lat_ref[112:224, lanes].astype(F32)
        halo[cut, 0:162, :] = lon_ref[:, lanes].astype(F32)
        halo[cut, 162:TOK, :] = corner_ref[:, lanes].astype(F32)
    for group in range(18):
        for part in range(4):
            cell = (2 * (group // LEV) + part % 2) * LEV + group % LEV
            source, odd, row = WIN * (cell + EDGE), part // 2, WIN * group
            for cut in range(4):
                lanes = slice(part * D1 + cut * 128, part * D1 + cut * 128 + 128)
                merged[row : row + 3, lanes] = near[cut, pl.ds(source + 6 + odd, 3, stride=2), :]
                merged[row + 3 : row + 9, lanes] = far[cut, pl.ds(source + odd, 6, stride=2), :]
                merged[row + 9 : row + WIN, lanes] = halo[cut, pl.ds(6 * cell + odd, 3, stride=2), :]
    for start in range(0, TOK, 72):
        normed, inverse = normalize(merged[start : start + 72, :])
        merged[start : start + 72, :] = normed
        minv[start : start + 72, :] = jnp.broadcast_to(inverse, (72, 128))
        mnorm[start : start + 72, :] = normed * mgain_ref[...]
    keep[...] = keep_matrix(last_ref)
    values = dot(mnorm[...].astype(BF16), mw_ref[...], 1, 0).astype(BF16).astype(F32)
    value_norm, value_inverse = normalize(values)
    normed = (value_norm * gain_ref[...]).astype(BF16)
    for start in range(0, 3 * D2, 512):
        qkv[start : start + 512, :] = dot(normed, cw_ref[:, start : start + 512], 1, 0).T
    for start in range(0, D2, 512):
        gatt[start : start + 512, :] = dot(
            cw_ref[start : start + 512, 3 * D2 :], cotc_ref[...], 1, 1
        ).astype(BF16)

    def heads(step, carry):
        for inner in range(4):
            head = step * 4 + inner
            rows = head_rows(0, D2, head)
            scale = scale_ref[head] / HEAD
            q_scaled, k_round, v_round, q_inverse, k_inverse, soft = attention_forward(
                head, D2, rows, scale, keep[...], qkv
            )
            soft_round = soft.astype(BF16)
            att[rows, :] = dot(v_round, soft_round, 1, 0).astype(BF16)
            grads = head_back(
                gatt[rows, :], q_scaled, k_round, v_round, soft, soft_round, q_inverse, k_inverse, scale
            )
            gqkv[rows, :] = grads[0].astype(BF16)
            gqkv[head_rows(1, D2, head), :] = grads[1].astype(BF16)
            gqkv[head_rows(2, D2, head), :] = grads[2].astype(BF16)
        return carry

    lax.fori_loop(0, H2 // 4, heads, 0)
    out_ref[...] = (values + dot(att[...], cw_ref[:, 3 * D2 :], 0, 0)).astype(BF16)
    for start in range(0, D2, 256):
        turned[start : start + 256, :] = dot(
            cw_ref[start : start + 256, : 3 * D2], gqkv[...], 1, 0
        )
    scaled = turned[...].T * gain_ref[...]
    grad_in = cotc_ref[...].astype(F32) + norm_back(scaled, value_norm, value_inverse)
    grad_in = grad_in.astype(BF16)
    for part in range(4):
        cols = slice(part * D1, part * D1 + D1)
        mnorm[:, cols] = dot(grad_in, mw_ref[cols, :], 1, 1) * mgain_ref[:, cols]
    for start in range(0, TOK, 72):
        mnorm[start : start + 72, :] = norm_back(
            mnorm[start : start + 72, :], merged[start : start + 72, :], minv[start : start + 72, 0:1]
        )
    for group in range(18):
        for part in range(4):
            target = (2 * (group // LEV) + part % 2) * LEV + group % LEV
            for cut in range(4):
                cells[cut, target, pl.ds(part // 2, WIN, stride=2), :] = mnorm[
                    WIN * group : WIN * group + WIN,
                    part * D1 + cut * 128 : part * D1 + cut * 128 + 128,
                ]
    done = jnp.concatenate([cells[cut] for cut in range(4)], -1)
    g_ref[...] = done.reshape(ROWS, D1).astype(BF16)
    glat_ref[...] = done[GROUPS - EDGE :].reshape(EDGE * LON, D1).astype(BF16)
    for group in range(GROUPS):
        rows = done[group, 18:24]
        if group < GROUPS - EDGE:
            lon_rows[6 * group : 6 * group + 6, :] = rows
        else:
            at = 6 * (group + EDGE - GROUPS)
            corner_rows[at : at + 6, :] = rows
    glon_ref[...] = lon_rows[...].astype(BF16)
    gcor_ref[...] = corner_rows[...].astype(BF16)


def fine_backward_kernel(side, *refs):
    if side == 1:
        (g_ref, lat_ref, cot_ref, clat_ref, clon_ref, ccor_ref,
         xw_ref, qkv_ref, inv_ref, soft_ref, att_ref, w_ref, gain_ref, scale_ref,
         gq_ref, e_ref, normt_ref, wins, gatt) = refs
        lon_cot = clon_ref[...].astype(F32)
        corner_cot = ccor_ref[...].astype(F32)
    else:
        (g_ref, lat_ref, lon_ref, corner_ref, cot_ref, clat_ref, xw_ref, qkv_ref, inv_ref, soft_ref, att_ref, w_ref, gain_ref,
         scale_ref, gq1_ref, e1_ref, normt1_ref, att1_ref,
         gq_ref, e_ref, gw_ref, wins, gatt, normt_ref) = refs
        lon_in = lon_ref[...].astype(F32)
        corner_in = corner_ref[...].astype(F32)
    tile = g_ref[...].astype(F32).reshape(GROUPS, LON, D1)
    lat_rows = lat_ref[...].astype(F32).reshape(EDGE, LON, D1)
    cot_tile = cot_ref[...].astype(F32).reshape(GROUPS, LON, D1)
    cot_lat = clat_ref[...].astype(F32).reshape(EDGE, LON, D1)
    for group in range(GROUPS):
        source = lat_rows[group] if group < EDGE else tile[group - EDGE]
        win, row = group // 18, WIN * (group % 18)
        inside = group + EDGE < GROUPS
        cot = cot_tile[group + EDGE] if inside else cot_lat[group + EDGE - GROUPS]
        if side == 1:
            at = 6 * group if inside else 6 * (group + EDGE - GROUPS)
            halo = lon_cot[at : at + 6] if inside else corner_cot[at : at + 6]
            wins[win, row : row + 6, :] = source[6:12] + cot[18:24]
            wins[win, row + 6 : row + WIN, :] = source[12:18] + halo
        else:
            if group < EDGE:
                halo = corner_in[6 * group : 6 * group + 6]
            else:
                halo = lon_in[6 * (group - EDGE) : 6 * (group - EDGE) + 6]
            wins[win, row : row + 6, :] = halo + cot[6:12]
            wins[win, row + 6 : row + WIN, :] = source[0:6] + cot[12:18]
    normt_ref[...] = jnp.zeros_like(normt_ref)
    gq_ref[...] = jnp.zeros_like(gq_ref)

    def window(win, carry):
        cot = wins[win].astype(BF16)
        e_ref[win] = cot
        gatt[...] = dot(w_ref[:, 3 * D1 :], cot, 1, 1).astype(BF16)
        normed = (normalize(xw_ref[win].astype(F32))[0] * gain_ref[...]).astype(BF16)
        normt_ref[win, :, 0:TOK] = normed.T
        for head in range(H1):
            rows = slice(head * HEAD, head * HEAD + HEAD)
            krows = slice(D1 + head * HEAD, D1 + head * HEAD + HEAD)
            vrows = slice(2 * D1 + head * HEAD, 2 * D1 + head * HEAD + HEAD)
            soft_round = soft_ref[win, head]
            grads = head_back(
                gatt[rows, :], qkv_ref[win, rows, :], qkv_ref[win, krows, :], qkv_ref[win, vrows, :],
                soft_round.astype(F32), soft_round,
                inv_ref[win, head : head + 1, :], inv_ref[win, H1 + head : H1 + head + 1, :],
                scale_ref[head] / HEAD,
            )
            gq_ref[win, rows, 0:TOK] = grads[0].astype(BF16)
            gq_ref[win, krows, 0:TOK] = grads[1].astype(BF16)
            gq_ref[win, vrows, 0:TOK] = grads[2].astype(BF16)
        return carry

    lax.fori_loop(0, 2, window, 0)
    if side == 0:
        def paired(left, right):
            left, right = left.reshape(64, 8, D1), right.reshape(64, 8, D1)
            first = lax.broadcasted_iota(jnp.int32, (64, 8, D1), 1) < 4
            even = jnp.where(first, left, pltpu.roll(right, 4, 1))
            odd = jnp.where(first, pltpu.roll(left, 4, 1), right)
            return even.astype(BF16), odd.astype(BF16)

        sums = []
        for part in range(3):
            cols = slice(part * D1, part * D1 + D1)
            total = dot(normt_ref[0], gq_ref[0, cols, :], 1, 1) + dot(normt_ref[1], gq_ref[1, cols, :], 1, 1)
            total += dot(normt1_ref[0], gq1_ref[0, cols, :], 1, 1)
            sums.append(total + dot(normt1_ref[1], gq1_ref[1, cols, :], 1, 1))
        total = dot(att_ref[0], e_ref[0], 1, 0) + dot(att_ref[1], e_ref[1], 1, 0)
        sums.append(total + dot(att1_ref[0], e1_ref[0], 1, 0) + dot(att1_ref[1], e1_ref[1], 1, 0))
        for part in range(2):
            even, odd = paired(sums[2 * part], sums[2 * part + 1])
            gw_ref[:, 0, :, part * D1 : part * D1 + D1] = even
            gw_ref[:, 1, :, part * D1 : part * D1 + D1] = odd


def fine_input_kernel(
    gq0_ref, gq1_ref, e0_ref, e1_ref, xw0_ref, xw1_ref, w_ref, gain_ref,
    g0_ref, g1_ref, glat_ref, glon_ref, gcor_ref, lat_rows, lon_rows, corner_rows,
):
    for side, (gq_ref, e_ref, xw_ref, g_ref) in enumerate(
        ((gq0_ref, e0_ref, xw0_ref, g0_ref), (gq1_ref, e1_ref, xw1_ref, g1_ref))
    ):
        for win in range(2):
            turned = dot(w_ref[:, : 3 * D1], gq_ref[win], 1, 0)
            scaled = turned.T[:TOK] * gain_ref[...]
            normed, inverse = normalize(xw_ref[win].astype(F32))
            grad_in = e_ref[win].astype(F32) + norm_back(scaled, normed, inverse)
            g_ref[win] = grad_in.astype(BF16)
            if win == 1:
                lat_rows[108 * side : 108 * side + 108, :] = grad_in[108:TOK]
            if side == 1:
                for group in range(18):
                    rows = grad_in[WIN * group + 6 : WIN * group + WIN]
                    at = 6 * (group + 18 * win)
                    if at < 162:
                        lon_rows[at : at + 6, :] = rows
                    else:
                        corner_rows[at - 162 : at - 156, :] = rows
    glat_ref[...] = lat_rows[...].astype(BF16)
    glon_ref[...] = lon_rows[...].astype(BF16)
    gcor_ref[...] = corner_rows[...].astype(BF16)


def assemble_kernel(g0_ref, g1_ref, lat_ref, lon_ref, corner_ref, out_ref, full):
    first = [g0_ref[win].astype(F32) for win in range(2)]
    second = [g1_ref[win].astype(F32) for win in range(2)]
    lat_rows = lat_ref[...].astype(F32)
    lon_rows = lon_ref[...].astype(F32)
    corner_rows = corner_ref[...].astype(F32)
    for group in range(GROUPS):
        if group < EDGE:
            full[group, 0:6, :] = corner_rows[6 * group : 6 * group + 6]
            full[group, 6:18, :] = lat_rows[WIN * group : WIN * group + WIN]
            full[group, 18:24, :] = lat_rows[108 + WIN * group : 108 + WIN * group + 6]
        else:
            own = group - EDGE
            win, row = own // 18, WIN * (own % 18)
            full[group, 0:6, :] = lon_rows[6 * own : 6 * own + 6]
            full[group, 6:18, :] = first[win][row : row + WIN]
            full[group, 18:24, :] = second[win][row : row + 6]
    out_ref[...] = full[...].reshape(ROWS, D1).astype(BF16)


def call(kernel, outs, scratch, smem_from, args, name, flops, vmem):
    whole = pl.BlockSpec(memory_space=pltpu.VMEM)
    scalars = pl.BlockSpec(memory_space=pltpu.SMEM)
    return pl.pallas_call(
        kernel,
        out_shape=[jax.ShapeDtypeStruct(shape, kind) for shape, kind in outs],
        in_specs=[scalars if position in smem_from else whole for position in range(len(args))],
        out_specs=[whole] * len(outs),
        scratch_shapes=[pltpu.VMEM(shape, kind) for shape, kind in scratch],
        compiler_params=pltpu.CompilerParams(vmem_limit_bytes=vmem * MIB),
        cost_estimate=pl.CostEstimate(flops=flops, bytes_accessed=1 << 22, transcendentals=0),
        name=name,
    )(*args)


HALF = ((2, TOK, D1), BF16)
LAT_BLOCK = ((EDGE * LON, D1), BF16)
LON_BLOCK = ((162, D1), BF16)
CORNER = ((54, D1), BF16)
LON_ROWS = ((162, D1), F32)
CORNER_ROWS = ((54, D1), F32)


def edges(tile):
    return call(edges_kernel, [LAT_BLOCK, LON_BLOCK, CORNER], [LON_ROWS, CORNER_ROWS], (), (tile,), "edges", 2 * 10**9, 12)


def fine_forward(side, ins, weights, scalars):
    outs = [HALF] + ([((112, D1), BF16), LON_BLOCK, CORNER] if side == 0 else [((224, D1), BF16)])
    outs += [
        HALF,
        ((2, 3 * D1, TOK), BF16),
        ((2, 2 * H1, TOK), F32),
        ((2, H1, TOK, TOK), BF16),
        ((2, D1, TOK), BF16),
    ]
    scratch = [((2, TOK, D1), F32), ((3 * D1, TOK), F32), ((TOK, TOK), F32)]
    if side == 0:
        scratch += [LON_ROWS, CORNER_ROWS]
    args = (*ins, *weights, *scalars)
    smem = (len(args) - 2, len(args) - 1)
    kernel = functools.partial(fine_forward_kernel, side)
    out = call(kernel, outs, scratch, smem, args, "fine_forward_" + str(side), 10**10, 20)
    return out[:-5], out[-5:]


def coarse_both(ins, cot_coarse, mgain, mw, cw, gain, scales, last):
    outs = [((TOK, D2), BF16), ((ROWS, D1), BF16), LAT_BLOCK, LON_BLOCK, CORNER]
    scratch = [
        ((4, 2 * TOK + 112, 128), F32),
        ((4, 2 * TOK + 112, 128), F32),
        ((4, TOK, 128), F32),
        ((4, GROUPS, LON, 128), F32),
        ((TOK, 4 * D1), F32),
        ((TOK, 4 * D1), F32),
        ((TOK, 128), F32),
        ((3 * D2, TOK), F32),
        ((3 * D2, TOK), BF16),
        ((D2, TOK), BF16),
        ((D2, TOK), BF16),
        ((D2, TOK), F32),
        ((TOK, TOK), F32),
        LON_ROWS,
        CORNER_ROWS,
    ]
    args = (*ins, cot_coarse, mgain, mw, cw, gain, scales, last)
    return call(coarse_kernel, outs, scratch, (10, 11), args, "coarse_both", 2 * 10**10, 36)


def fine_backward(side, ins, saved, weights, gain, scales, other=()):
    outs = [((2, 3 * D1, 256), BF16), HALF]
    scratch = [((2, TOK, D1), F32), ((D1, TOK), BF16)]
    normt = ((2, D1, 256), BF16)
    if side == 1:
        outs.append(normt)
    else:
        outs.append(((64, 2, 8, 2 * D1), BF16))
        scratch.append(normt)
    args = (*ins, *saved, weights, gain, scales, *other)
    smem = (len(args) - len(other) - 1,)
    kernel = functools.partial(fine_backward_kernel, side)
    return call(kernel, outs, scratch, smem, args, "fine_backward_" + str(side), 10**10, 24)


def fine_input(args):
    outs = [HALF, HALF, LAT_BLOCK, LON_BLOCK, CORNER]
    scratch = [((EDGE * LON, D1), F32), LON_ROWS, CORNER_ROWS]
    return call(fine_input_kernel, outs, scratch, (), args, "fine_input", 6 * 10**9, 20)


def assemble(args):
    scratch = [((GROUPS, LON, D1), F32)]
    return call(assemble_kernel, [((ROWS, D1), BF16)], scratch, (), args, "assemble", 2 * 10**9, 12)[0]


def ring(axis_size, step):
    return [(i, (i + step) % axis_size) for i in range(axis_size)]


def moved(block, axis, step):
    return lax.ppermute(block, axis, ring(lax.axis_size(axis), step))


def moved_both(block, step):
    nlon, nlat = lax.axis_size("lon"), lax.axis_size("lat")
    route = [
        (i * nlat + j, ((i + step) % nlon) * nlat + (j + step) % nlat)
        for i in range(nlon)
        for j in range(nlat)
    ]
    return lax.ppermute(block, ("lon", "lat"), route)


def half_moved(tile, axis, dim, step):
    near, far = jnp.split(tile, 2, dim)
    if step < 0:
        return jnp.concatenate([far, moved(near, axis, step)], dim)
    return jnp.concatenate([moved(far, axis, step), near], dim)


def after(value, *others):
    return lax.optimization_barrier((value, *others))[0]


def share_sum(pieces):
    pieces = lax.all_to_all(pieces, ("lon", "lat"), 0, 0)
    total = jnp.sum(pieces.astype(F32), 0).reshape(2, 4, 2, D1)
    return total.transpose(1, 2, 0, 3).reshape(4, 4 * D1)


def on_device(
    grid_field, fine_weights, fine_gain, fine_scales, merge_gain, merge_weight, coarse_weights, coarse_gain,
    coarse_scales, cot_fine, cot_coarse,
):
    last = (lax.axis_index("lat") == lax.axis_size("lat") - 1).astype(jnp.int32).reshape(1)
    fine_gain = fine_gain.reshape(1, -1)
    tile = grid_field.transpose(1, 2, 0, 3).reshape(ROWS, D1)
    lat, lon, corner = edges(tile)
    lat, lon, corner = moved(lat, "lat", -1), moved(lon, "lon", -1), moved_both(corner, -1)
    cot_coarse = after(cot_coarse, lat).transpose(1, 2, 0, 3)
    cot_coarse = half_moved(cot_coarse, "lon", 2, -1)
    weights = (fine_weights[:, : 3 * D1].T, fine_weights, fine_gain)
    scalars = (fine_scales, last)
    (y0, ylat, ylon, ycor), saved0 = fine_forward(0, (tile, lat), weights, scalars)
    ylon, ycor = moved(ylon, "lon", -1), moved_both(ycor, -1)
    cot_coarse = half_moved(after(cot_coarse, y0), "lat", 0, -1).reshape(TOK, D2)
    (y1, ylat), saved1 = fine_forward(1, (tile, lat, lon, corner, ylat), weights, scalars)
    ylat, ylon, ycor, cot_coarse = lax.optimization_barrier((ylat, ylon, ycor, cot_coarse))
    ylat = moved(ylat, "lat", -1)
    cot_tile = after(cot_fine, y1).transpose(1, 2, 0, 3).reshape(ROWS, D1)
    cot_edges = edges(cot_tile)
    cot_edges = (moved(cot_edges[0], "lat", -1), moved(cot_edges[1], "lon", -1), moved_both(cot_edges[2], -1))
    coarse_out, grad, glat, glon, gcor = coarse_both(
        (y0, y1, ylat, ylon, ycor), cot_coarse, merge_gain.reshape(1, -1), merge_weight,
        coarse_weights, coarse_gain.reshape(1, -1), coarse_scales, last,
    )
    (glat, glon, gcor), cot_edges = lax.optimization_barrier(((glat, glon, gcor), cot_edges))
    glat, glon, gcor = moved(glat, "lat", 1), moved(glon, "lon", 1), moved_both(gcor, 1)
    coarse_out = half_moved(after(coarse_out, glat).reshape(LAT // 2, LEV, LON // 2, D2), "lon", 2, 1)
    gq1, e1, normt1 = fine_backward(
        1, (grad, glat, cot_tile, *cot_edges), saved1, fine_weights, fine_gain, fine_scales
    )
    gq1, coarse_out = lax.optimization_barrier((gq1, coarse_out))
    coarse_out = half_moved(coarse_out, "lat", 0, 1)
    gq0, e0, pieces = fine_backward(
        0, (grad, glat, glon, gcor, cot_tile, cot_edges[0]), saved0, fine_weights, fine_gain, fine_scales,
        (gq1, e1, normt1, saved1[4]),
    )
    gq0, coarse_out = lax.optimization_barrier((gq0, coarse_out))
    g0, g1, lat, lon, corner = fine_input(
        (gq0, gq1, e0, e1, saved0[0], saved1[0], fine_weights, fine_gain)
    )
    lat, lon, corner = moved(lat, "lat", 1), moved(lon, "lon", 1), moved_both(corner, 1)
    share = share_sum(after(pieces, gq0).reshape(128, 8, 2 * D1))
    grad_input = assemble((g0, g1, lat, lon, corner)).reshape(LAT, LEV, LON, D1)
    return coarse_out.transpose(2, 0, 1, 3), grad_input.transpose(2, 0, 1, 3), share


def solution(mesh):
    tile = P("lon", "lat", None, None)
    in_specs = (tile,) + (P(),) * 8 + (tile, tile)
    out_specs = (tile, tile, P(("lon", "lat"), None))
    return jax.shard_map(
        on_device, mesh=mesh, in_specs=in_specs, out_specs=out_specs, check_vma=False
    )
```

```python
import functools

import jax
import jax.numpy as jnp
from jax import lax
from jax.experimental import pallas as pl
from jax.experimental.pallas import tpu as pltpu
from jax.sharding import Mesh, PartitionSpec as P

F32 = jnp.float32
BF16 = jnp.bfloat16
EPS_NORM = 1e-05
EPS_HEAD = 1e-06
D1, D2, H1, H2 = 512, 1024, 8, 16
HEAD = 64
TOK = 216
LON, LAT, LEV = 24, 12, 3
GROUPS = LAT * LEV
EDGE = 9
ROWS = GROUPS * LON
WIN = 12
MIB = 1024 * 1024


def dot(left, right, left_dim, right_dim):
    return lax.dot_general(
        left, right, (((left_dim,), (right_dim,)), ((), ())), preferred_element_type=F32
    )


def mean_last(values):
    return jnp.mean(values, -1, keepdims=True)


def normalize(values):
    center = values - mean_last(values)
    inverse = lax.rsqrt(mean_last(center * center) + EPS_NORM)
    return center * inverse, inverse


def norm_back(scaled, normed, inverse):
    return inverse * (scaled - mean_last(scaled) - normed * mean_last(scaled * normed))


def keep_matrix(last_ref):
    half = TOK // 2
    keys = lax.broadcasted_iota(jnp.int32, (TOK, TOK), 0) >= half
    queries = lax.broadcasted_iota(jnp.int32, (TOK, TOK), 1) >= half
    apart = jnp.where(keys == queries, 0.0, 1.0)
    return 1.0 - apart * last_ref[0].astype(F32)


def unit_rows(values):
    inverse = lax.rsqrt(jnp.mean(values * values, 0, keepdims=True) + EPS_HEAD)
    return values * inverse, inverse


def probabilities(k_round, q_scaled, keep):
    raw = jnp.exp(dot(k_round, q_scaled, 0, 0)) * keep
    return raw * (1.0 / jnp.sum(raw, 0, keepdims=True))


def head_back(grad, q_scaled, k_round, v_round, soft, soft_round, q_inverse, k_inverse, scale):
    grad_probs = dot(v_round, grad, 0, 0)
    grad_value = dot(grad, soft_round, 1, 1)
    centered = grad_probs - jnp.sum(grad_probs * soft, 0, keepdims=True)
    grad_scores = (soft * centered).astype(BF16)
    grad_q = dot(k_round, grad_scores, 1, 0)
    grad_k = dot(q_scaled, grad_scores, 1, 1)
    q_wide = q_scaled.astype(F32)
    k_wide = k_round.astype(F32)
    q_mean = jnp.mean(grad_q * q_wide, 0, keepdims=True)
    grad_query = q_inverse * (grad_q * scale - q_wide * (q_mean * (1.0 / scale)))
    grad_key = k_inverse * (grad_k - k_wide * jnp.mean(grad_k * k_wide, 0, keepdims=True))
    return grad_query, grad_key, grad_value


def head_rows(part, width, head):
    return pl.ds(pl.multiple_of(part * width + head * HEAD, HEAD), HEAD)


def attention_forward(head, width, base, scale, keep, qkv):
    q_unit, q_inverse = unit_rows(qkv[base, :])
    k_unit, k_inverse = unit_rows(qkv[head_rows(1, width, head), :])
    q_scaled = (q_unit * scale).astype(BF16)
    k_round = k_unit.astype(BF16)
    v_round = qkv[head_rows(2, width, head), :].astype(BF16)
    return q_scaled, k_round, v_round, q_inverse, k_inverse, probabilities(k_round, q_scaled, keep)


def edges_kernel(x_ref, lat_ref, lon_ref, corner_ref, lat_rows, lon_rows, corner_rows):
    tile = x_ref[...].astype(F32).reshape(GROUPS, LON, D1)
    for group in range(GROUPS):
        rows = tile[group, 0:6]
        if group < EDGE:
            corner_rows[6 * group : 6 * group + 6, :] = rows
            lat_rows[18 * group : 18 * group + 18, :] = tile[group, 6:24]
        else:
            lon_rows[6 * (group - EDGE) : 6 * (group - EDGE) + 6, :] = rows
    lat_ref[...] = lat_rows[...].astype(BF16)
    lon_ref[...] = lon_rows[...].astype(BF16)
    corner_ref[...] = corner_rows[...].astype(BF16)


def fine_forward_kernel(side, *refs):
    if side == 0:
        (x_ref, lat_ref, wt_ref, w_ref, gain_ref, scale_ref, last_ref,
         y_ref, ylat_ref, ylon_ref, ycor_ref, xw_ref, qkv_ref, inv_ref, soft_ref, att_ref,
         wins, qkv, keep, lon_rows, corner_rows) = refs
    else:
        (x_ref, lat_ref, lon_ref, corner_ref, first_ref, wt_ref, w_ref, gain_ref, scale_ref, last_ref,
         y_ref, ylat_ref, xw_ref, qkv_ref, inv_ref, soft_ref, att_ref, wins, qkv, keep) = refs
    tile = x_ref[...].astype(F32).reshape(GROUPS, LON, D1)
    lat_rows = lat_ref[...].astype(F32)
    if side == 1:
        lon_in = lon_ref[...].astype(F32)
        corner_in = corner_ref[...].astype(F32)
    for group in range(GROUPS):
        if group + EDGE < GROUPS:
            source = tile[group + EDGE, 6:24]
        else:
            source = lat_rows[18 * (group + EDGE - GROUPS) : 18 * (group + EDGE - GROUPS) + 18]
        win, row = group // 18, WIN * (group % 18)
        if side == 0:
            wins[win, row : row + WIN, :] = source[0:12]
        else:
            wins[win, row : row + 6, :] = source[12:18]
            if group + EDGE < GROUPS:
                halo = lon_in[6 * group : 6 * group + 6]
            else:
                halo = corner_in[6 * (group + EDGE - GROUPS) : 6 * (group + EDGE - GROUPS) + 6]
            wins[win, row + 6 : row + WIN, :] = halo
    keep[...] = keep_matrix(last_ref)

    def window(win, carry):
        values = wins[win]
        xw_ref[win] = values.astype(BF16)
        normed = (normalize(values)[0] * gain_ref[...]).astype(BF16)
        for part in range(3):
            qkv[part * D1 : part * D1 + D1, :] = dot(
                wt_ref[part * D1 : part * D1 + D1, :], normed, 1, 1
            )
        use_keep = jnp.where(win >= 1, keep[...], 1.0)
        for head in range(H1):
            rows = slice(head * HEAD, head * HEAD + HEAD)
            krows = slice(D1 + head * HEAD, D1 + head * HEAD + HEAD)
            vrows = slice(2 * D1 + head * HEAD, 2 * D1 + head * HEAD + HEAD)
            q_scaled, k_round, v_round, q_inverse, k_inverse, soft = attention_forward(
                head, D1, rows, scale_ref[head] / HEAD, use_keep, qkv
            )
            qkv_ref[win, rows, :] = q_scaled
            qkv_ref[win, krows, :] = k_round
            qkv_ref[win, vrows, :] = v_round
            inv_ref[win, head : head + 1, :] = q_inverse
            inv_ref[win, H1 + head : H1 + head + 1, :] = k_inverse
            soft = soft.astype(BF16)
            soft_ref[win, head] = soft
            att_ref[win, rows, :] = dot(v_round, soft, 1, 0).astype(BF16)
        result = values + dot(att_ref[win], w_ref[:, 3 * D1 :], 0, 0)
        wins[win] = result
        y_ref[win] = result.astype(BF16)
        return carry

    lax.fori_loop(0, 2, window, 0)
    if side == 0:
        ylat_ref[...] = wins[0, 0:112, :].astype(BF16)
        for group in range(GROUPS):
            rows = wins[group // 18, WIN * (group % 18) : WIN * (group % 18) + 6, :]
            if group < EDGE:
                corner_rows[6 * group : 6 * group + 6, :] = rows
            else:
                lon_rows[6 * (group - EDGE) : 6 * (group - EDGE) + 6, :] = rows
        ylon_ref[...] = lon_rows[...].astype(BF16)
        ycor_ref[...] = corner_rows[...].astype(BF16)
    else:
        ylat_ref[0:112, :] = first_ref[...]
        ylat_ref[112:224, :] = wins[0, 0:112, :].astype(BF16)


def coarse_kernel(
    y0_ref, y1_ref, lat_ref, lon_ref, corner_ref, cotc_ref, mgain_ref, mw_ref, cw_ref, gain_ref,
    scale_ref, last_ref,
    out_ref, g_ref, glat_ref, glon_ref, gcor_ref,
    near, far, halo, cells, merged, mnorm, minv, qkv, gqkv, gatt, att, turned, keep, lat_out, lon_rows, corner_rows,
):
    for cut in range(4):
        lanes = slice(cut * 128, cut * 128 + 128)
        for win in range(2):
            near[cut, TOK * win : TOK * win + TOK, :] = y0_ref[win, :, lanes].astype(F32)
            far[cut, TOK * win : TOK * win + TOK, :] = y1_ref[win, :, lanes].astype(F32)
        near[cut, 2 * TOK :, :] = lat_ref[0:112, lanes].astype(F32)
        far[cut, 2 * TOK :, :] = lat_ref[112:224, lanes].astype(F32)
        halo[cut, 0:162, :] = lon_ref[:, lanes].astype(F32)
        halo[cut, 162:TOK, :] = corner_ref[:, lanes].astype(F32)
    for group in range(18):
        for part in range(4):
            cell = (2 * (group // LEV) + part % 2) * LEV + group % LEV
            source, odd, row = WIN * (cell + EDGE), part // 2, WIN * group
            for cut in range(4):
                lanes = slice(part * D1 + cut * 128, part * D1 + cut * 128 + 128)
                merged[row : row + 3, lanes] = near[cut, pl.ds(source + 6 + odd, 3, stride=2), :]
                merged[row + 3 : row + 9, lanes] = far[cut, pl.ds(source + odd, 6, stride=2), :]
                merged[row + 9 : row + WIN, lanes] = halo[cut, pl.ds(6 * cell + odd, 3, stride=2), :]
    for start in range(0, TOK, 72):
        normed, inverse = normalize(merged[start : start + 72, :])
        merged[start : start + 72, :] = normed
        minv[start : start + 72, :] = jnp.broadcast_to(inverse, (72, 128))
        mnorm[start : start + 72, :] = normed * mgain_ref[...]
    keep[...] = keep_matrix(last_ref)
    values = dot(mnorm[...].astype(BF16), mw_ref[...], 1, 0).astype(BF16).astype(F32)
    value_norm, value_inverse = normalize(values)
    normed = (value_norm * gain_ref[...]).astype(BF16)
    for start in range(0, 3 * D2, 512):
        qkv[start : start + 512, :] = dot(normed, cw_ref[:, start : start + 512], 1, 0).T
    for start in range(0, D2, 512):
        gatt[start : start + 512, :] = dot(
            cw_ref[start : start + 512, 3 * D2 :], cotc_ref[...], 1, 1
        ).astype(BF16)

    def heads(step, carry):
        for inner in range(4):
            head = step * 4 + inner
            rows = head_rows(0, D2, head)
            scale = scale_ref[head] / HEAD
            q_scaled, k_round, v_round, q_inverse, k_inverse, soft = attention_forward(
                head, D2, rows, scale, keep[...], qkv
            )
            soft_round = soft.astype(BF16)
            att[rows, :] = dot(v_round, soft_round, 1, 0).astype(BF16)
            grads = head_back(
                gatt[rows, :], q_scaled, k_round, v_round, soft, soft_round, q_inverse, k_inverse, scale
            )
            gqkv[rows, :] = grads[0].astype(BF16)
            gqkv[head_rows(1, D2, head), :] = grads[1].astype(BF16)
            gqkv[head_rows(2, D2, head), :] = grads[2].astype(BF16)
        return carry

    lax.fori_loop(0, H2 // 4, heads, 0)
    out_ref[...] = (values + dot(att[...], cw_ref[:, 3 * D2 :], 0, 0)).astype(BF16)
    for start in range(0, D2, 256):
        turned[start : start + 256, :] = dot(
            cw_ref[start : start + 256, : 3 * D2], gqkv[...], 1, 0
        )
    scaled = turned[...].T * gain_ref[...]
    grad_in = cotc_ref[...].astype(F32) + norm_back(scaled, value_norm, value_inverse)
    grad_in = grad_in.astype(BF16)
    for part in range(4):
        cols = slice(part * D1, part * D1 + D1)
        mnorm[:, cols] = dot(grad_in, mw_ref[cols, :], 1, 1) * mgain_ref[:, cols]
    for start in range(0, TOK, 72):
        mnorm[start : start + 72, :] = norm_back(
            mnorm[start : start + 72, :], merged[start : start + 72, :], minv[start : start + 72, 0:1]
        )
    for group in range(18):
        for part in range(4):
            target = (2 * (group // LEV) + part % 2) * LEV + group % LEV
            for cut in range(4):
                cells[cut, target, pl.ds(part // 2, WIN, stride=2), :] = mnorm[
                    WIN * group : WIN * group + WIN,
                    part * D1 + cut * 128 : part * D1 + cut * 128 + 128,
                ]
    done = jnp.concatenate([cells[cut] for cut in range(4)], -1)
    g_ref[...] = done.reshape(ROWS, D1).astype(BF16)
    for group in range(GROUPS):
        rows = done[group, 18:24]
        if group < GROUPS - EDGE:
            lon_rows[6 * group : 6 * group + 6, :] = rows
        else:
            at = 6 * (group + EDGE - GROUPS)
            corner_rows[at : at + 6, :] = rows
            lat_out[3 * at : 3 * at + 18, :] = done[group, 0:18]
    glat_ref[...] = lat_out[...].astype(BF16)
    glon_ref[...] = lon_rows[...].astype(BF16)
    gcor_ref[...] = corner_rows[...].astype(BF16)


def fine_backward_kernel(side, *refs):
    if side == 1:
        (g_ref, lat_ref, cot_ref, clat_ref, clon_ref, ccor_ref,
         xw_ref, qkv_ref, inv_ref, soft_ref, att_ref, w_ref, gain_ref, scale_ref,
         gq_ref, e_ref, normt_ref, wins, gatt) = refs
        lon_cot = clon_ref[...].astype(F32)
        corner_cot = ccor_ref[...].astype(F32)
    else:
        (g_ref, lat_ref, lon_ref, corner_ref, cot_ref, clat_ref, xw_ref, qkv_ref, inv_ref, soft_ref, att_ref, w_ref, gain_ref,
         scale_ref, gq1_ref, e1_ref, normt1_ref, att1_ref,
         gq_ref, e_ref, gw_ref, wins, gatt, normt_ref) = refs
        lon_in = lon_ref[...].astype(F32)
        corner_in = corner_ref[...].astype(F32)
    tile = g_ref[...].astype(F32).reshape(GROUPS, LON, D1)
    lat_rows = lat_ref[...].astype(F32)
    cot_tile = cot_ref[...].astype(F32).reshape(GROUPS, LON, D1)
    cot_lat = clat_ref[...].astype(F32)
    for group in range(GROUPS):
        source = lat_rows[18 * group : 18 * group + 18] if group < EDGE else tile[group - EDGE, 0:18]
        win, row = group // 18, WIN * (group % 18)
        inside = group + EDGE < GROUPS
        at = 18 * (group + EDGE - GROUPS)
        cot = cot_tile[group + EDGE, 6:24] if inside else cot_lat[at : at + 18]
        if side == 1:
            at = 6 * group if inside else 6 * (group + EDGE - GROUPS)
            halo = lon_cot[at : at + 6] if inside else corner_cot[at : at + 6]
            wins[win, row : row + 6, :] = source[6:12] + cot[12:18]
            wins[win, row + 6 : row + WIN, :] = source[12:18] + halo
        else:
            if group < EDGE:
                halo = corner_in[6 * group : 6 * group + 6]
            else:
                halo = lon_in[6 * (group - EDGE) : 6 * (group - EDGE) + 6]
            wins[win, row : row + 6, :] = halo + cot[0:6]
            wins[win, row + 6 : row + WIN, :] = source[0:6] + cot[6:12]
    normt_ref[...] = jnp.zeros_like(normt_ref)
    gq_ref[...] = jnp.zeros_like(gq_ref)

    def window(win, carry):
        cot = wins[win].astype(BF16)
        e_ref[win] = cot
        gatt[...] = dot(w_ref[:, 3 * D1 :], cot, 1, 1).astype(BF16)
        normed = (normalize(xw_ref[win].astype(F32))[0] * gain_ref[...]).astype(BF16)
        normt_ref[win, :, 0:TOK] = normed.T
        for head in range(H1):
            rows = slice(head * HEAD, head * HEAD + HEAD)
            krows = slice(D1 + head * HEAD, D1 + head * HEAD + HEAD)
            vrows = slice(2 * D1 + head * HEAD, 2 * D1 + head * HEAD + HEAD)
            soft_round = soft_ref[win, head]
            grads = head_back(
                gatt[rows, :], qkv_ref[win, rows, :], qkv_ref[win, krows, :], qkv_ref[win, vrows, :],
                soft_round.astype(F32), soft_round,
                inv_ref[win, head : head + 1, :], inv_ref[win, H1 + head : H1 + head + 1, :],
                scale_ref[head] / HEAD,
            )
            gq_ref[win, rows, 0:TOK] = grads[0].astype(BF16)
            gq_ref[win, krows, 0:TOK] = grads[1].astype(BF16)
            gq_ref[win, vrows, 0:TOK] = grads[2].astype(BF16)
        return carry

    lax.fori_loop(0, 2, window, 0)
    if side == 0:
        def paired(left, right):
            left, right = left.reshape(64, 8, D1), right.reshape(64, 8, D1)
            first = lax.broadcasted_iota(jnp.int32, (64, 8, D1), 1) < 4
            even = jnp.where(first, left, pltpu.roll(right, 4, 1))
            odd = jnp.where(first, pltpu.roll(left, 4, 1), right)
            return even.astype(BF16), odd.astype(BF16)

        sums = []
        for part in range(3):
            cols = slice(part * D1, part * D1 + D1)
            total = dot(normt_ref[0], gq_ref[0, cols, :], 1, 1) + dot(normt_ref[1], gq_ref[1, cols, :], 1, 1)
            total += dot(normt1_ref[0], gq1_ref[0, cols, :], 1, 1)
            sums.append(total + dot(normt1_ref[1], gq1_ref[1, cols, :], 1, 1))
        total = dot(att_ref[0], e_ref[0], 1, 0) + dot(att_ref[1], e_ref[1], 1, 0)
        sums.append(total + dot(att1_ref[0], e1_ref[0], 1, 0) + dot(att1_ref[1], e1_ref[1], 1, 0))
        for part in range(2):
            even, odd = paired(sums[2 * part], sums[2 * part + 1])
            gw_ref[:, 0, :, part * D1 : part * D1 + D1] = even
            gw_ref[:, 1, :, part * D1 : part * D1 + D1] = odd


def fine_input_kernel(
    gq0_ref, gq1_ref, e0_ref, e1_ref, xw0_ref, xw1_ref, w_ref, gain_ref,
    g0_ref, g1_ref, glat_ref, glon_ref, gcor_ref, lat_rows, lon_rows, corner_rows,
):
    for side, (gq_ref, e_ref, xw_ref, g_ref) in enumerate(
        ((gq0_ref, e0_ref, xw0_ref, g0_ref), (gq1_ref, e1_ref, xw1_ref, g1_ref))
    ):
        for win in range(2):
            turned = dot(w_ref[:, : 3 * D1], gq_ref[win], 1, 0)
            scaled = turned.T[:TOK] * gain_ref[...]
            normed, inverse = normalize(xw_ref[win].astype(F32))
            grad_in = e_ref[win].astype(F32) + norm_back(scaled, normed, inverse)
            g_ref[win] = grad_in.astype(BF16)
            if win == 1 and side == 0:
                lat_rows[0:108, :] = grad_in[108:TOK]
            if side == 1:
                for group in range(18):
                    rows = grad_in[WIN * group + 6 : WIN * group + WIN]
                    at = 6 * (group + 18 * win)
                    if at < 162:
                        lon_rows[at : at + 6, :] = rows
                    else:
                        corner_rows[at - 162 : at - 156, :] = rows
                        lat_rows[at - 54 : at - 48, :] = grad_in[WIN * group : WIN * group + 6]
    glat_ref[...] = lat_rows[...].astype(BF16)
    glon_ref[...] = lon_rows[...].astype(BF16)
    gcor_ref[...] = corner_rows[...].astype(BF16)


def assemble_kernel(g0_ref, g1_ref, lat_ref, lon_ref, corner_ref, out_ref, full):
    first = [g0_ref[win].astype(F32) for win in range(2)]
    second = [g1_ref[win].astype(F32) for win in range(2)]
    lat_rows = lat_ref[...].astype(F32)
    lon_rows = lon_ref[...].astype(F32)
    corner_rows = corner_ref[...].astype(F32)
    for group in range(GROUPS):
        if group < EDGE:
            full[group, 0:6, :] = corner_rows[6 * group : 6 * group + 6]
            full[group, 6:18, :] = lat_rows[WIN * group : WIN * group + WIN]
            full[group, 18:24, :] = lat_rows[108 + 6 * group : 108 + 6 * group + 6]
        else:
            own = group - EDGE
            win, row = own // 18, WIN * (own % 18)
            full[group, 0:6, :] = lon_rows[6 * own : 6 * own + 6]
            full[group, 6:18, :] = first[win][row : row + WIN]
            full[group, 18:24, :] = second[win][row : row + 6]
    out_ref[...] = full[...].reshape(ROWS, D1).astype(BF16)


def call(kernel, outs, scratch, smem_from, args, name, flops, vmem):
    whole = pl.BlockSpec(memory_space=pltpu.VMEM)
    scalars = pl.BlockSpec(memory_space=pltpu.SMEM)
    return pl.pallas_call(
        kernel,
        out_shape=[jax.ShapeDtypeStruct(shape, kind) for shape, kind in outs],
        in_specs=[scalars if position in smem_from else whole for position in range(len(args))],
        out_specs=[whole] * len(outs),
        scratch_shapes=[pltpu.VMEM(shape, kind) for shape, kind in scratch],
        compiler_params=pltpu.CompilerParams(vmem_limit_bytes=vmem * MIB),
        cost_estimate=pl.CostEstimate(flops=flops, bytes_accessed=1 << 22, transcendentals=0),
        name=name,
    )(*args)


HALF = ((2, TOK, D1), BF16)
LON_BLOCK = ((162, D1), BF16)
CORNER = ((54, D1), BF16)
LON_ROWS = ((162, D1), F32)
CORNER_ROWS = ((54, D1), F32)


def edges(tile):
    return call(edges_kernel, [LON_BLOCK, LON_BLOCK, CORNER], [LON_ROWS, LON_ROWS, CORNER_ROWS], (), (tile,), "edges", 2 * 10**9, 6)


def fine_forward(side, ins, weights, scalars):
    outs = [HALF] + ([((112, D1), BF16), LON_BLOCK, CORNER] if side == 0 else [((224, D1), BF16)])
    outs += [
        HALF,
        ((2, 3 * D1, TOK), BF16),
        ((2, 2 * H1, TOK), F32),
        ((2, H1, TOK, TOK), BF16),
        ((2, D1, TOK), BF16),
    ]
    scratch = [((2, TOK, D1), F32), ((3 * D1, TOK), F32), ((TOK, TOK), F32)]
    if side == 0:
        scratch += [LON_ROWS, CORNER_ROWS]
    args = (*ins, *weights, *scalars)
    smem = (len(args) - 2, len(args) - 1)
    kernel = functools.partial(fine_forward_kernel, side)
    out = call(kernel, outs, scratch, smem, args, "fine_forward_" + str(side), 10**10, 10)
    return out[:-5], out[-5:]


def coarse_both(ins, cot_coarse, mgain, mw, cw, gain, scales, last):
    outs = [((TOK, D2), BF16), ((ROWS, D1), BF16), LON_BLOCK, LON_BLOCK, CORNER]
    scratch = [
        ((4, 2 * TOK + 112, 128), F32),
        ((4, 2 * TOK + 112, 128), F32),
        ((4, TOK, 128), F32),
        ((4, GROUPS, LON, 128), F32),
        ((TOK, 4 * D1), F32),
        ((TOK, 4 * D1), F32),
        ((TOK, 128), F32),
        ((3 * D2, TOK), F32),
        ((3 * D2, TOK), BF16),
        ((D2, TOK), BF16),
        ((D2, TOK), BF16),
        ((D2, TOK), F32),
        ((TOK, TOK), F32),
        LON_ROWS,
        LON_ROWS,
        CORNER_ROWS,
    ]
    args = (*ins, cot_coarse, mgain, mw, cw, gain, scales, last)
    return call(coarse_kernel, outs, scratch, (10, 11), args, "coarse_both", 2 * 10**10, 22)


def fine_backward(side, ins, saved, weights, gain, scales, other=()):
    outs = [((2, 3 * D1, 256), BF16), HALF]
    scratch = [((2, TOK, D1), F32), ((D1, TOK), BF16)]
    normt = ((2, D1, 256), BF16)
    if side == 1:
        outs.append(normt)
    else:
        outs.append(((64, 2, 8, 2 * D1), BF16))
        scratch.append(normt)
    args = (*ins, *saved, weights, gain, scales, *other)
    smem = (len(args) - len(other) - 1,)
    kernel = functools.partial(fine_backward_kernel, side)
    return call(kernel, outs, scratch, smem, args, "fine_backward_" + str(side), 10**10, 14)


def fine_input(args):
    outs = [HALF, HALF, LON_BLOCK, LON_BLOCK, CORNER]
    scratch = [LON_ROWS, LON_ROWS, CORNER_ROWS]
    return call(fine_input_kernel, outs, scratch, (), args, "fine_input", 6 * 10**9, 8)


def assemble(args):
    scratch = [((GROUPS, LON, D1), F32)]
    return call(assemble_kernel, [((ROWS, D1), BF16)], scratch, (), args, "assemble", 2 * 10**9, 6)[0]


def ring(axis_size, step):
    return [(i, (i + step) % axis_size) for i in range(axis_size)]


def moved(block, axis, step):
    return lax.ppermute(block, axis, ring(lax.axis_size(axis), step))


def half_moved(tile, axis, dim, step):
    near, far = jnp.split(tile, 2, dim)
    if step < 0:
        return jnp.concatenate([far, moved(near, axis, step)], dim)
    return jnp.concatenate([moved(far, axis, step), near], dim)


def after(value, *others):
    return lax.optimization_barrier((value, *others))[0]


def share_sum(pieces):
    pieces = lax.all_to_all(pieces, ("lon", "lat"), 0, 0)
    total = jnp.sum(pieces.astype(F32), 0).reshape(2, 4, 2, D1)
    return total.transpose(1, 2, 0, 3).reshape(4, 4 * D1)


def on_device(
    grid_field, fine_weights, fine_gain, fine_scales, merge_gain, merge_weight, coarse_weights, coarse_gain,
    coarse_scales, cot_fine, cot_coarse,
):
    last = (lax.axis_index("lat") == lax.axis_size("lat") - 1).astype(jnp.int32).reshape(1)
    fine_gain = fine_gain.reshape(1, -1)
    tile = grid_field.transpose(1, 2, 0, 3).reshape(ROWS, D1)
    lat, lon, corner = edges(tile)
    lat, lon, corner = moved(lat, "lat", -1), moved(lon, "lon", -1), moved(corner, "lat", -1)
    corner = moved(corner, "lon", -1)
    cot_coarse = after(cot_coarse, lat).transpose(1, 2, 0, 3)
    cot_coarse = half_moved(cot_coarse, "lon", 2, -1)
    weights = (fine_weights[:, : 3 * D1].T, fine_weights, fine_gain)
    scalars = (fine_scales, last)
    (y0, ylat, ylon, ycor), saved0 = fine_forward(0, (tile, lat), weights, scalars)
    ylon, ycor = moved(ylon, "lon", -1), moved(ycor, "lon", -1)
    cot_coarse = half_moved(after(cot_coarse, y0), "lat", 0, -1).reshape(TOK, D2)
    (y1, ylat), saved1 = fine_forward(1, (tile, lat, lon, corner, ylat), weights, scalars)
    ylat, ylon, ycor, cot_coarse = lax.optimization_barrier((ylat, ylon, ycor, cot_coarse))
    ylat, ycor = moved(ylat, "lat", -1), moved(ycor, "lat", -1)
    cot_tile = after(cot_fine, y1).transpose(1, 2, 0, 3).reshape(ROWS, D1)
    cot_edges = edges(cot_tile)
    cot_lon, cot_corner = moved(cot_edges[1], "lon", -1), moved(cot_edges[2], "lon", -1)
    cot_lat = moved(cot_edges[0], "lat", -1)
    coarse_out, grad, glat, glon, gcor = coarse_both(
        (y0, y1, ylat, ylon, ycor), cot_coarse, merge_gain.reshape(1, -1), merge_weight,
        coarse_weights, coarse_gain.reshape(1, -1), coarse_scales, last,
    )
    glat, glon, gcor, cot_lat, cot_lon, cot_corner = lax.optimization_barrier(
        (glat, glon, gcor, cot_lat, cot_lon, cot_corner)
    )
    cot_corner = moved(cot_corner, "lat", -1)
    glat, glon, gcor = moved(glat, "lat", 1), moved(glon, "lon", 1), moved(gcor, "lat", 1)
    gcor = moved(gcor, "lon", 1)
    coarse_out = half_moved(after(coarse_out, glat).reshape(LAT // 2, LEV, LON // 2, D2), "lon", 2, 1)
    gq1, e1, normt1 = fine_backward(
        1, (grad, glat, cot_tile, cot_lat, cot_lon, cot_corner), saved1, fine_weights, fine_gain, fine_scales
    )
    gq1, coarse_out = lax.optimization_barrier((gq1, coarse_out))
    coarse_out = half_moved(coarse_out, "lat", 0, 1)
    gq0, e0, pieces = fine_backward(
        0, (grad, glat, glon, gcor, cot_tile, cot_lat), saved0, fine_weights, fine_gain, fine_scales,
        (gq1, e1, normt1, saved1[4]),
    )
    gq0, coarse_out = lax.optimization_barrier((gq0, coarse_out))
    g0, g1, lat, lon, corner = fine_input(
        (gq0, gq1, e0, e1, saved0[0], saved1[0], fine_weights, fine_gain)
    )
    lat, lon, corner = moved(lat, "lat", 1), moved(lon, "lon", 1), moved(corner, "lat", 1)
    corner = moved(corner, "lon", 1)
    share = share_sum(after(pieces, gq0).reshape(128, 8, 2 * D1))
    grad_input = assemble((g0, g1, lat, lon, corner)).reshape(LAT, LEV, LON, D1)
    return coarse_out.transpose(2, 0, 1, 3), grad_input.transpose(2, 0, 1, 3), share


def solution(mesh):
    tile = P("lon", "lat", None, None)
    in_specs = (tile,) + (P(),) * 8 + (tile, tile)
    out_specs = (tile, tile, P(("lon", "lat"), None))
    return jax.shard_map(
        on_device, mesh=mesh, in_specs=in_specs, out_specs=out_specs, check_vma=False
    )
```

```python
import functools

import jax
import jax.numpy as jnp
from jax import lax
from jax.experimental import pallas as pl
from jax.experimental.pallas import tpu as pltpu
from jax.sharding import Mesh, PartitionSpec as P

F32 = jnp.float32
BF16 = jnp.bfloat16
EPS_NORM = 1e-05
EPS_HEAD = 1e-06
D1, D2, H1, H2 = 512, 1024, 8, 16
HEAD = 64
TOK = 216
LON, LAT, LEV = 24, 12, 3
GROUPS = LAT * LEV
EDGE = 9
ROWS = GROUPS * LON
WIN = 12
MIB = 1024 * 1024


def dot(left, right, left_dim, right_dim):
    return lax.dot_general(
        left, right, (((left_dim,), (right_dim,)), ((), ())), preferred_element_type=F32
    )


def mean_last(values):
    return jnp.mean(values, -1, keepdims=True)


def normalize(values):
    center = values - mean_last(values)
    inverse = lax.rsqrt(mean_last(center * center) + EPS_NORM)
    return center * inverse, inverse


def norm_back(scaled, normed, inverse):
    return inverse * (scaled - mean_last(scaled) - normed * mean_last(scaled * normed))


def keep_matrix(last_ref):
    half = TOK // 2
    keys = lax.broadcasted_iota(jnp.int32, (TOK, TOK), 0) >= half
    queries = lax.broadcasted_iota(jnp.int32, (TOK, TOK), 1) >= half
    apart = jnp.where(keys == queries, 0.0, 1.0)
    return 1.0 - apart * last_ref[0].astype(F32)


def unit_rows(values):
    inverse = lax.rsqrt(jnp.mean(values * values, 0, keepdims=True) + EPS_HEAD)
    return values * inverse, inverse


def probabilities(k_round, q_scaled, keep):
    raw = jnp.exp(dot(k_round, q_scaled, 0, 0)) * keep
    return raw * (1.0 / jnp.sum(raw, 0, keepdims=True))


def head_back(grad, q_scaled, k_round, v_round, soft, soft_round, q_inverse, k_inverse, scale):
    grad_probs = dot(v_round, grad, 0, 0)
    grad_value = dot(grad, soft_round, 1, 1)
    centered = grad_probs - jnp.sum(grad_probs * soft, 0, keepdims=True)
    grad_scores = (soft * centered).astype(BF16)
    grad_q = dot(k_round, grad_scores, 1, 0)
    grad_k = dot(q_scaled, grad_scores, 1, 1)
    q_wide = q_scaled.astype(F32)
    k_wide = k_round.astype(F32)
    q_mean = jnp.mean(grad_q * q_wide, 0, keepdims=True)
    grad_query = q_inverse * (grad_q * scale - q_wide * (q_mean * (1.0 / scale)))
    grad_key = k_inverse * (grad_k - k_wide * jnp.mean(grad_k * k_wide, 0, keepdims=True))
    return grad_query, grad_key, grad_value


def head_rows(part, width, head):
    return pl.ds(pl.multiple_of(part * width + head * HEAD, HEAD), HEAD)


def attention_forward(head, width, base, scale, keep, qkv):
    q_unit, q_inverse = unit_rows(qkv[base, :])
    k_unit, k_inverse = unit_rows(qkv[head_rows(1, width, head), :])
    q_scaled = (q_unit * scale).astype(BF16)
    k_round = k_unit.astype(BF16)
    v_round = qkv[head_rows(2, width, head), :].astype(BF16)
    return q_scaled, k_round, v_round, q_inverse, k_inverse, probabilities(k_round, q_scaled, keep)


def edges_kernel(x_ref, lat_ref, lon_ref, corner_ref, lon_rows, corner_rows):
    tile = x_ref[...].astype(F32).reshape(GROUPS, LON, D1)
    lat_ref[...] = tile[:EDGE].reshape(EDGE * LON, D1).astype(BF16)
    for group in range(GROUPS):
        rows = tile[group, 0:6]
        if group < EDGE:
            corner_rows[6 * group : 6 * group + 6, :] = rows
        else:
            lon_rows[6 * (group - EDGE) : 6 * (group - EDGE) + 6, :] = rows
    lon_ref[...] = lon_rows[...].astype(BF16)
    corner_ref[...] = corner_rows[...].astype(BF16)


def fine_forward_kernel(side, *refs):
    if side == 0:
        (x_ref, lat_ref, wt_ref, w_ref, gain_ref, scale_ref, last_ref,
         y_ref, ylat_ref, ylon_ref, ycor_ref, xw_ref, qkv_ref, inv_ref, soft_ref, att_ref,
         wins, qkv, keep, lon_rows, corner_rows) = refs
    else:
        (x_ref, lat_ref, lon_ref, corner_ref, first_ref, wt_ref, w_ref, gain_ref, scale_ref, last_ref,
         y_ref, ylat_ref, xw_ref, qkv_ref, inv_ref, soft_ref, att_ref, wins, qkv, keep) = refs
    tile = x_ref[...].astype(F32).reshape(GROUPS, LON, D1)
    lat_rows = lat_ref[...].astype(F32).reshape(EDGE, LON, D1)
    if side == 1:
        lon_in = lon_ref[...].astype(F32)
        corner_in = corner_ref[...].astype(F32)
    for group in range(GROUPS):
        source = tile[group + EDGE] if group + EDGE < GROUPS else lat_rows[group + EDGE - GROUPS]
        win, row = group // 18, WIN * (group % 18)
        if side == 0:
            wins[win, row : row + WIN, :] = source[6:18]
        else:
            wins[win, row : row + 6, :] = source[18:24]
            if group + EDGE < GROUPS:
                halo = lon_in[6 * group : 6 * group + 6]
            else:
                halo = corner_in[6 * (group + EDGE - GROUPS) : 6 * (group + EDGE - GROUPS) + 6]
            wins[win, row + 6 : row + WIN, :] = halo
    keep[...] = keep_matrix(last_ref)

    def window(win, carry):
        values = wins[win]
        xw_ref[win] = values.astype(BF16)
        normed = (normalize(values)[0] * gain_ref[...]).astype(BF16)
        for part in range(3):
            qkv[part * D1 : part * D1 + D1, :] = dot(
                wt_ref[part * D1 : part * D1 + D1, :], normed, 1, 1
            )
        use_keep = jnp.where(win >= 1, keep[...], 1.0)
        for head in range(H1):
            rows = slice(head * HEAD, head * HEAD + HEAD)
            krows = slice(D1 + head * HEAD, D1 + head * HEAD + HEAD)
            vrows = slice(2 * D1 + head * HEAD, 2 * D1 + head * HEAD + HEAD)
            q_scaled, k_round, v_round, q_inverse, k_inverse, soft = attention_forward(
                head, D1, rows, scale_ref[head] / HEAD, use_keep, qkv
            )
            qkv_ref[win, rows, :] = q_scaled
            qkv_ref[win, krows, :] = k_round
            qkv_ref[win, vrows, :] = v_round
            inv_ref[win, head : head + 1, :] = q_inverse
            inv_ref[win, H1 + head : H1 + head + 1, :] = k_inverse
            soft = soft.astype(BF16)
            soft_ref[win, head] = soft
            att_ref[win, rows, :] = dot(v_round, soft, 1, 0).astype(BF16)
        result = values + dot(att_ref[win], w_ref[:, 3 * D1 :], 0, 0)
        wins[win] = result
        y_ref[win] = result.astype(BF16)
        return carry

    lax.fori_loop(0, 2, window, 0)
    if side == 0:
        ylat_ref[...] = wins[0, 0:112, :].astype(BF16)
        for group in range(GROUPS):
            rows = wins[group // 18, WIN * (group % 18) : WIN * (group % 18) + 6, :]
            if group < EDGE:
                corner_rows[6 * group : 6 * group + 6, :] = rows
            else:
                lon_rows[6 * (group - EDGE) : 6 * (group - EDGE) + 6, :] = rows
        ylon_ref[...] = lon_rows[...].astype(BF16)
        ycor_ref[...] = corner_rows[...].astype(BF16)
    else:
        ylat_ref[0:112, :] = first_ref[...]
        ylat_ref[112:224, :] = wins[0, 0:112, :].astype(BF16)


def coarse_kernel(
    y0_ref, y1_ref, lat_ref, lon_ref, corner_ref, cotc_ref, mgain_ref, mw_ref, cw_ref, gain_ref,
    scale_ref, last_ref,
    out_ref, g_ref, glat_ref, glon_ref, gcor_ref,
    near, far, halo, cells, merged, mnorm, minv, qkv, gqkv, gatt, att, turned, keep, lon_rows, corner_rows, cot_rows,
):
    for group in range(18):
        cot_rows[WIN * group : WIN * group + WIN, :] = cotc_ref[group].astype(F32)
    cot = cot_rows[...].astype(BF16)
    for cut in range(4):
        lanes = slice(cut * 128, cut * 128 + 128)
        for win in range(2):
            near[cut, TOK * win : TOK * win + TOK, :] = y0_ref[win, :, lanes].astype(F32)
            far[cut, TOK * win : TOK * win + TOK, :] = y1_ref[win, :, lanes].astype(F32)
        near[cut, 2 * TOK :, :] = lat_ref[0:112, lanes].astype(F32)
        far[cut, 2 * TOK :, :] = lat_ref[112:224, lanes].astype(F32)
        halo[cut, 0:162, :] = lon_ref[:, lanes].astype(F32)
        halo[cut, 162:TOK, :] = corner_ref[:, lanes].astype(F32)
    for group in range(18):
        for part in range(4):
            cell = (2 * (group // LEV) + part % 2) * LEV + group % LEV
            source, odd, row = WIN * (cell + EDGE), part // 2, WIN * group
            for cut in range(4):
                lanes = slice(part * D1 + cut * 128, part * D1 + cut * 128 + 128)
                merged[row : row + 3, lanes] = near[cut, pl.ds(source + 6 + odd, 3, stride=2), :]
                merged[row + 3 : row + 9, lanes] = far[cut, pl.ds(source + odd, 6, stride=2), :]
                merged[row + 9 : row + WIN, lanes] = halo[cut, pl.ds(6 * cell + odd, 3, stride=2), :]
    for start in range(0, TOK, 72):
        normed, inverse = normalize(merged[start : start + 72, :])
        merged[start : start + 72, :] = normed
        minv[start : start + 72, :] = jnp.broadcast_to(inverse, (72, 128))
        mnorm[start : start + 72, :] = normed * mgain_ref[...]
    keep[...] = keep_matrix(last_ref)
    values = dot(mnorm[...].astype(BF16), mw_ref[...], 1, 0).astype(BF16).astype(F32)
    value_norm, value_inverse = normalize(values)
    normed = (value_norm * gain_ref[...]).astype(BF16)
    for start in range(0, 3 * D2, 512):
        qkv[start : start + 512, :] = dot(normed, cw_ref[:, start : start + 512], 1, 0).T
    for start in range(0, D2, 512):
        gatt[start : start + 512, :] = dot(
            cw_ref[start : start + 512, 3 * D2 :], cot, 1, 1
        ).astype(BF16)

    def heads(step, carry):
        for inner in range(4):
            head = step * 4 + inner
            rows = head_rows(0, D2, head)
            scale = scale_ref[head] / HEAD
            q_scaled, k_round, v_round, q_inverse, k_inverse, soft = attention_forward(
                head, D2, rows, scale, keep[...], qkv
            )
            soft_round = soft.astype(BF16)
            att[rows, :] = dot(v_round, soft_round, 1, 0).astype(BF16)
            grads = head_back(
                gatt[rows, :], q_scaled, k_round, v_round, soft, soft_round, q_inverse, k_inverse, scale
            )
            gqkv[rows, :] = grads[0].astype(BF16)
            gqkv[head_rows(1, D2, head), :] = grads[1].astype(BF16)
            gqkv[head_rows(2, D2, head), :] = grads[2].astype(BF16)
        return carry

    lax.fori_loop(0, H2 // 4, heads, 0)
    result = values + dot(att[...], cw_ref[:, 3 * D2 :], 0, 0)
    for group in range(18):
        out_ref[group] = result[WIN * group : WIN * group + WIN].astype(BF16)
    for start in range(0, D2, 256):
        turned[start : start + 256, :] = dot(
            cw_ref[start : start + 256, : 3 * D2], gqkv[...], 1, 0
        )
    scaled = turned[...].T * gain_ref[...]
    grad_in = cot_rows[...] + norm_back(scaled, value_norm, value_inverse)
    grad_in = grad_in.astype(BF16)
    for part in range(4):
        cols = slice(part * D1, part * D1 + D1)
        mnorm[:, cols] = dot(grad_in, mw_ref[cols, :], 1, 1) * mgain_ref[:, cols]
    for start in range(0, TOK, 72):
        mnorm[start : start + 72, :] = norm_back(
            mnorm[start : start + 72, :], merged[start : start + 72, :], minv[start : start + 72, 0:1]
        )
    for group in range(18):
        for part in range(4):
            target = (2 * (group // LEV) + part % 2) * LEV + group % LEV
            for cut in range(4):
                cells[cut, target, pl.ds(part // 2, WIN, stride=2), :] = mnorm[
                    WIN * group : WIN * group + WIN,
                    part * D1 + cut * 128 : part * D1 + cut * 128 + 128,
                ]
    done = jnp.concatenate([cells[cut] for cut in range(4)], -1)
    g_ref[...] = done.reshape(ROWS, D1).astype(BF16)
    glat_ref[...] = done[GROUPS - EDGE :].reshape(EDGE * LON, D1).astype(BF16)
    for group in range(GROUPS):
        rows = done[group, 18:24]
        if group < GROUPS - EDGE:
            lon_rows[6 * group : 6 * group + 6, :] = rows
        else:
            at = 6 * (group + EDGE - GROUPS)
            corner_rows[at : at + 6, :] = rows
    glon_ref[...] = lon_rows[...].astype(BF16)
    gcor_ref[...] = corner_rows[...].astype(BF16)


def fine_backward_kernel(side, *refs):
    if side == 1:
        (g_ref, lat_ref, cot_ref, clat_ref, clon_ref, ccor_ref,
         xw_ref, qkv_ref, inv_ref, soft_ref, att_ref, w_ref, gain_ref, scale_ref,
         gq_ref, e_ref, normt_ref, wins, gatt) = refs
        lon_cot = clon_ref[...].astype(F32)
        corner_cot = ccor_ref[...].astype(F32)
    else:
        (g_ref, lat_ref, lon_ref, corner_ref, cot_ref, clat_ref, xw_ref, qkv_ref, inv_ref, soft_ref, att_ref, w_ref, gain_ref,
         scale_ref, gq1_ref, e1_ref, normt1_ref, att1_ref,
         gq_ref, e_ref, gw_ref, wins, gatt, normt_ref) = refs
        lon_in = lon_ref[...].astype(F32)
        corner_in = corner_ref[...].astype(F32)
    tile = g_ref[...].astype(F32).reshape(GROUPS, LON, D1)
    lat_rows = lat_ref[...].astype(F32).reshape(EDGE, LON, D1)
    cot_tile = cot_ref[...].astype(F32).reshape(GROUPS, LON, D1)
    cot_lat = clat_ref[...].astype(F32).reshape(EDGE, LON, D1)
    for group in range(GROUPS):
        source = lat_rows[group] if group < EDGE else tile[group - EDGE]
        win, row = group // 18, WIN * (group % 18)
        inside = group + EDGE < GROUPS
        cot = cot_tile[group + EDGE] if inside else cot_lat[group + EDGE - GROUPS]
        if side == 1:
            at = 6 * group if inside else 6 * (group + EDGE - GROUPS)
            halo = lon_cot[at : at + 6] if inside else corner_cot[at : at + 6]
            wins[win, row : row + 6, :] = source[6:12] + cot[18:24]
            wins[win, row + 6 : row + WIN, :] = source[12:18] + halo
        else:
            if group < EDGE:
                halo = corner_in[6 * group : 6 * group + 6]
            else:
                halo = lon_in[6 * (group - EDGE) : 6 * (group - EDGE) + 6]
            wins[win, row : row + 6, :] = halo + cot[6:12]
            wins[win, row + 6 : row + WIN, :] = source[0:6] + cot[12:18]
    normt_ref[...] = jnp.zeros_like(normt_ref)
    gq_ref[...] = jnp.zeros_like(gq_ref)

    def window(win, carry):
        cot = wins[win].astype(BF16)
        e_ref[win] = cot
        gatt[...] = dot(w_ref[:, 3 * D1 :], cot, 1, 1).astype(BF16)
        normed = (normalize(xw_ref[win].astype(F32))[0] * gain_ref[...]).astype(BF16)
        normt_ref[win, :, 0:TOK] = normed.T
        for head in range(H1):
            rows = slice(head * HEAD, head * HEAD + HEAD)
            krows = slice(D1 + head * HEAD, D1 + head * HEAD + HEAD)
            vrows = slice(2 * D1 + head * HEAD, 2 * D1 + head * HEAD + HEAD)
            soft_round = soft_ref[win, head]
            grads = head_back(
                gatt[rows, :], qkv_ref[win, rows, :], qkv_ref[win, krows, :], qkv_ref[win, vrows, :],
                soft_round.astype(F32), soft_round,
                inv_ref[win, head : head + 1, :], inv_ref[win, H1 + head : H1 + head + 1, :],
                scale_ref[head] / HEAD,
            )
            gq_ref[win, rows, 0:TOK] = grads[0].astype(BF16)
            gq_ref[win, krows, 0:TOK] = grads[1].astype(BF16)
            gq_ref[win, vrows, 0:TOK] = grads[2].astype(BF16)
        return carry

    lax.fori_loop(0, 2, window, 0)
    if side == 0:
        def paired(left, right):
            left, right = left.reshape(64, 8, D1), right.reshape(64, 8, D1)
            first = lax.broadcasted_iota(jnp.int32, (64, 8, D1), 1) < 4
            even = jnp.where(first, left, pltpu.roll(right, 4, 1))
            odd = jnp.where(first, pltpu.roll(left, 4, 1), right)
            return even.astype(BF16), odd.astype(BF16)

        sums = []
        for part in range(3):
            cols = slice(part * D1, part * D1 + D1)
            total = dot(normt_ref[0], gq_ref[0, cols, :], 1, 1) + dot(normt_ref[1], gq_ref[1, cols, :], 1, 1)
            total += dot(normt1_ref[0], gq1_ref[0, cols, :], 1, 1)
            sums.append(total + dot(normt1_ref[1], gq1_ref[1, cols, :], 1, 1))
        total = dot(att_ref[0], e_ref[0], 1, 0) + dot(att_ref[1], e_ref[1], 1, 0)
        sums.append(total + dot(att1_ref[0], e1_ref[0], 1, 0) + dot(att1_ref[1], e1_ref[1], 1, 0))
        for part in range(2):
            even, odd = paired(sums[2 * part], sums[2 * part + 1])
            gw_ref[:, 0, :, part * D1 : part * D1 + D1] = even
            gw_ref[:, 1, :, part * D1 : part * D1 + D1] = odd


def fine_input_kernel(
    gq0_ref, gq1_ref, e0_ref, e1_ref, xw0_ref, xw1_ref, w_ref, gain_ref,
    g0_ref, g1_ref, glat_ref, glon_ref, gcor_ref, lat_rows, lon_rows, corner_rows,
):
    for side, (gq_ref, e_ref, xw_ref, g_ref) in enumerate(
        ((gq0_ref, e0_ref, xw0_ref, g0_ref), (gq1_ref, e1_ref, xw1_ref, g1_ref))
    ):
        for win in range(2):
            turned = dot(w_ref[:, : 3 * D1], gq_ref[win], 1, 0)
            scaled = turned.T[:TOK] * gain_ref[...]
            normed, inverse = normalize(xw_ref[win].astype(F32))
            grad_in = e_ref[win].astype(F32) + norm_back(scaled, normed, inverse)
            g_ref[win] = grad_in.astype(BF16)
            if win == 1:
                lat_rows[108 * side : 108 * side + 108, :] = grad_in[108:TOK]
            if side == 1:
                for group in range(18):
                    rows = grad_in[WIN * group + 6 : WIN * group + WIN]
                    at = 6 * (group + 18 * win)
                    if at < 162:
                        lon_rows[at : at + 6, :] = rows
                    else:
                        corner_rows[at - 162 : at - 156, :] = rows
    glat_ref[...] = lat_rows[...].astype(BF16)
    glon_ref[...] = lon_rows[...].astype(BF16)
    gcor_ref[...] = corner_rows[...].astype(BF16)


def assemble_kernel(g0_ref, g1_ref, lat_ref, lon_ref, corner_ref, out_ref, full):
    first = [g0_ref[win].astype(F32) for win in range(2)]
    second = [g1_ref[win].astype(F32) for win in range(2)]
    lat_rows = lat_ref[...].astype(F32)
    lon_rows = lon_ref[...].astype(F32)
    corner_rows = corner_ref[...].astype(F32)
    for group in range(GROUPS):
        if group < EDGE:
            full[group, 0:6, :] = corner_rows[6 * group : 6 * group + 6]
            full[group, 6:18, :] = lat_rows[WIN * group : WIN * group + WIN]
            full[group, 18:24, :] = lat_rows[108 + WIN * group : 108 + WIN * group + 6]
        else:
            own = group - EDGE
            win, row = own // 18, WIN * (own % 18)
            full[group, 0:6, :] = lon_rows[6 * own : 6 * own + 6]
            full[group, 6:18, :] = first[win][row : row + WIN]
            full[group, 18:24, :] = second[win][row : row + 6]
    out_ref[...] = full[...].reshape(ROWS, D1).astype(BF16)


def call(kernel, outs, scratch, smem_from, args, name, flops, vmem):
    whole = pl.BlockSpec(memory_space=pltpu.VMEM)
    scalars = pl.BlockSpec(memory_space=pltpu.SMEM)
    return pl.pallas_call(
        kernel,
        out_shape=[jax.ShapeDtypeStruct(shape, kind) for shape, kind in outs],
        in_specs=[scalars if position in smem_from else whole for position in range(len(args))],
        out_specs=[whole] * len(outs),
        scratch_shapes=[pltpu.VMEM(shape, kind) for shape, kind in scratch],
        compiler_params=pltpu.CompilerParams(vmem_limit_bytes=vmem * MIB),
        cost_estimate=pl.CostEstimate(flops=flops, bytes_accessed=1 << 22, transcendentals=0),
        name=name,
    )(*args)


HALF = ((2, TOK, D1), BF16)
LAT_BLOCK = ((EDGE * LON, D1), BF16)
LON_BLOCK = ((162, D1), BF16)
CORNER = ((54, D1), BF16)
LON_ROWS = ((162, D1), F32)
CORNER_ROWS = ((54, D1), F32)


def edges(tile):
    return call(edges_kernel, [LAT_BLOCK, LON_BLOCK, CORNER], [LON_ROWS, CORNER_ROWS], (), (tile,), "edges", 2 * 10**9, 6)


def fine_forward(side, ins, weights, scalars):
    outs = [HALF] + ([((112, D1), BF16), LON_BLOCK, CORNER] if side == 0 else [((224, D1), BF16)])
    outs += [
        HALF,
        ((2, 3 * D1, TOK), BF16),
        ((2, 2 * H1, TOK), F32),
        ((2, H1, TOK, TOK), BF16),
        ((2, D1, TOK), BF16),
    ]
    scratch = [((2, TOK, D1), F32), ((3 * D1, TOK), F32), ((TOK, TOK), F32)]
    if side == 0:
        scratch += [LON_ROWS, CORNER_ROWS]
    args = (*ins, *weights, *scalars)
    smem = (len(args) - 2, len(args) - 1)
    kernel = functools.partial(fine_forward_kernel, side)
    out = call(kernel, outs, scratch, smem, args, "fine_forward_" + str(side), 10**10, 10)
    return out[:-5], out[-5:]


def coarse_both(ins, cot_coarse, mgain, mw, cw, gain, scales, last):
    outs = [((18, WIN, D2), BF16), ((ROWS, D1), BF16), LAT_BLOCK, LON_BLOCK, CORNER]
    scratch = [
        ((4, 2 * TOK + 112, 128), F32),
        ((4, 2 * TOK + 112, 128), F32),
        ((4, TOK, 128), F32),
        ((4, GROUPS, LON, 128), F32),
        ((TOK, 4 * D1), F32),
        ((TOK, 4 * D1), F32),
        ((TOK, 128), F32),
        ((3 * D2, TOK), F32),
        ((3 * D2, TOK), BF16),
        ((D2, TOK), BF16),
        ((D2, TOK), BF16),
        ((D2, TOK), F32),
        ((TOK, TOK), F32),
        LON_ROWS,
        CORNER_ROWS,
        ((TOK, D2), F32),
    ]
    args = (*ins, cot_coarse, mgain, mw, cw, gain, scales, last)
    return call(coarse_kernel, outs, scratch, (10, 11), args, "coarse_both", 2 * 10**10, 22)


def fine_backward(side, ins, saved, weights, gain, scales, other=()):
    outs = [((2, 3 * D1, 256), BF16), HALF]
    scratch = [((2, TOK, D1), F32), ((D1, TOK), BF16)]
    normt = ((2, D1, 256), BF16)
    if side == 1:
        outs.append(normt)
    else:
        outs.append(((64, 2, 8, 2 * D1), BF16))
        scratch.append(normt)
    args = (*ins, *saved, weights, gain, scales, *other)
    smem = (len(args) - len(other) - 1,)
    kernel = functools.partial(fine_backward_kernel, side)
    return call(kernel, outs, scratch, smem, args, "fine_backward_" + str(side), 10**10, 14)


def fine_input(args):
    outs = [HALF, HALF, LAT_BLOCK, LON_BLOCK, CORNER]
    scratch = [((EDGE * LON, D1), F32), LON_ROWS, CORNER_ROWS]
    return call(fine_input_kernel, outs, scratch, (), args, "fine_input", 6 * 10**9, 8)


def assemble(args):
    scratch = [((GROUPS, LON, D1), F32)]
    return call(assemble_kernel, [((ROWS, D1), BF16)], scratch, (), args, "assemble", 2 * 10**9, 6)[0]


def ring(axis_size, step):
    return [(i, (i + step) % axis_size) for i in range(axis_size)]


def moved(block, axis, step):
    return lax.ppermute(block, axis, ring(lax.axis_size(axis), step))


def moved_both(block, step):
    nlon, nlat = lax.axis_size("lon"), lax.axis_size("lat")
    route = [
        (i * nlat + j, ((i + step) % nlon) * nlat + (j + step) % nlat)
        for i in range(nlon)
        for j in range(nlat)
    ]
    return lax.ppermute(block, ("lon", "lat"), route)


def half_moved(tile, axis, dim, step):
    near, far = jnp.split(tile, 2, dim)
    if step < 0:
        return jnp.concatenate([far, moved(near, axis, step)], dim)
    return jnp.concatenate([moved(far, axis, step), near], dim)


def after(value, *others):
    return lax.optimization_barrier((value, *others))[0]


def share_sum(pieces):
    pieces = lax.all_to_all(pieces, ("lon", "lat"), 0, 0)
    total = jnp.sum(pieces.astype(F32), 0).reshape(2, 4, 2, D1)
    return total.transpose(1, 2, 0, 3).reshape(4, 4 * D1)


def on_device(
    grid_field, fine_weights, fine_gain, fine_scales, merge_gain, merge_weight, coarse_weights, coarse_gain,
    coarse_scales, cot_fine, cot_coarse,
):
    last = (lax.axis_index("lat") == lax.axis_size("lat") - 1).astype(jnp.int32).reshape(1)
    fine_gain = fine_gain.reshape(1, -1)
    tile = grid_field.transpose(1, 2, 0, 3).reshape(ROWS, D1)
    lat, lon, corner = edges(tile)
    lat, lon, corner = moved(lat, "lat", -1), moved(lon, "lon", -1), moved_both(corner, -1)
    cot_coarse = after(cot_coarse, lat).transpose(1, 2, 0, 3)
    cot_coarse = half_moved(cot_coarse, "lon", 2, -1)
    weights = (fine_weights[:, : 3 * D1].T, fine_weights, fine_gain)
    scalars = (fine_scales, last)
    (y0, ylat, ylon, ycor), saved0 = fine_forward(0, (tile, lat), weights, scalars)
    ylon, ycor = moved(ylon, "lon", -1), moved_both(ycor, -1)
    cot_coarse = half_moved(after(cot_coarse, y0), "lat", 0, -1).reshape(18, WIN, D2)
    (y1, ylat), saved1 = fine_forward(1, (tile, lat, lon, corner, ylat), weights, scalars)
    ylat, ylon, ycor, cot_coarse = lax.optimization_barrier((ylat, ylon, ycor, cot_coarse))
    ylat = moved(ylat, "lat", -1)
    cot_tile = after(cot_fine, y1).transpose(1, 2, 0, 3).reshape(ROWS, D1)
    cot_edges = edges(cot_tile)
    cot_edges = (moved(cot_edges[0], "lat", -1), moved(cot_edges[1], "lon", -1), moved_both(cot_edges[2], -1))
    coarse_out, grad, glat, glon, gcor = coarse_both(
        (y0, y1, ylat, ylon, ycor), cot_coarse, merge_gain.reshape(1, -1), merge_weight,
        coarse_weights, coarse_gain.reshape(1, -1), coarse_scales, last,
    )
    (glat, glon, gcor), cot_edges = lax.optimization_barrier(((glat, glon, gcor), cot_edges))
    glat, glon, gcor = moved(glat, "lat", 1), moved(glon, "lon", 1), moved_both(gcor, 1)
    coarse_out = half_moved(after(coarse_out, glat).reshape(LAT // 2, LEV, LON // 2, D2), "lon", 2, 1)
    gq1, e1, normt1 = fine_backward(
        1, (grad, glat, cot_tile, *cot_edges), saved1, fine_weights, fine_gain, fine_scales
    )
    gq1, coarse_out = lax.optimization_barrier((gq1, coarse_out))
    coarse_out = half_moved(coarse_out, "lat", 0, 1)
    gq0, e0, pieces = fine_backward(
        0, (grad, glat, glon, gcor, cot_tile, cot_edges[0]), saved0, fine_weights, fine_gain, fine_scales,
        (gq1, e1, normt1, saved1[4]),
    )
    gq0, coarse_out = lax.optimization_barrier((gq0, coarse_out))
    g0, g1, lat, lon, corner = fine_input(
        (gq0, gq1, e0, e1, saved0[0], saved1[0], fine_weights, fine_gain)
    )
    lat, lon, corner = moved(lat, "lat", 1), moved(lon, "lon", 1), moved_both(corner, 1)
    share = share_sum(after(pieces, lat).reshape(128, 8, 2 * D1))
    grad_input = assemble((g0, g1, lat, lon, corner)).reshape(LAT, LEV, LON, D1)
    return coarse_out.transpose(2, 0, 1, 3), grad_input.transpose(2, 0, 1, 3), share


def solution(mesh):
    tile = P("lon", "lat", None, None)
    in_specs = (tile,) + (P(),) * 8 + (tile, tile)
    out_specs = (tile, tile, P(("lon", "lat"), None))
    return jax.shard_map(
        on_device, mesh=mesh, in_specs=in_specs, out_specs=out_specs, check_vma=False
    )
```

```python
import functools

import jax
import jax.numpy as jnp
from jax import lax
from jax.experimental import pallas as pl
from jax.experimental.pallas import tpu as pltpu
from jax.sharding import Mesh, PartitionSpec as P

LAT_AXES = ("chip", "core")
F32 = jnp.float32
BF16 = jnp.bfloat16
EPS_NORM = 1e-05
EPS_HEAD = 1e-06
D1, D2, H1, H2 = 512, 1024, 8, 16
HEAD = 64
TOK = 216
LON, LAT, LEV = 24, 12, 3
GROUPS = LAT * LEV
EDGE = 9
ROWS = GROUPS * LON
WIN = 12
MIB = 1024 * 1024


def dot(left, right, left_dim, right_dim):
    return lax.dot_general(
        left, right, (((left_dim,), (right_dim,)), ((), ())), preferred_element_type=F32
    )


def mean_last(values):
    return jnp.mean(values, -1, keepdims=True)


def normalize(values):
    center = values - mean_last(values)
    inverse = lax.rsqrt(mean_last(center * center) + EPS_NORM)
    return center * inverse, inverse


def norm_back(scaled, normed, inverse):
    return inverse * (scaled - mean_last(scaled) - normed * mean_last(scaled * normed))


def keep_matrix(last_ref):
    half = TOK // 2
    keys = lax.broadcasted_iota(jnp.int32, (TOK, TOK), 0) >= half
    queries = lax.broadcasted_iota(jnp.int32, (TOK, TOK), 1) >= half
    apart = jnp.where(keys == queries, 0.0, 1.0)
    return 1.0 - apart * last_ref[0].astype(F32)


def unit_rows(values):
    inverse = lax.rsqrt(jnp.mean(values * values, 0, keepdims=True) + EPS_HEAD)
    return values * inverse, inverse


def probabilities(k_round, q_scaled, keep):
    raw = jnp.exp(dot(k_round, q_scaled, 0, 0)) * keep
    return raw * (1.0 / jnp.sum(raw, 0, keepdims=True))


def head_back(grad, q_scaled, k_round, v_round, soft, soft_round, q_inverse, k_inverse, scale):
    grad_probs = dot(v_round, grad, 0, 0)
    grad_value = dot(grad, soft_round, 1, 1)
    centered = grad_probs - jnp.sum(grad_probs * soft, 0, keepdims=True)
    grad_scores = (soft * centered).astype(BF16)
    grad_q = dot(k_round, grad_scores, 1, 0)
    grad_k = dot(q_scaled, grad_scores, 1, 1)
    q_wide = q_scaled.astype(F32)
    k_wide = k_round.astype(F32)
    q_mean = jnp.mean(grad_q * q_wide, 0, keepdims=True)
    grad_query = q_inverse * (grad_q * scale - q_wide * (q_mean * (1.0 / scale)))
    grad_key = k_inverse * (grad_k - k_wide * jnp.mean(grad_k * k_wide, 0, keepdims=True))
    return grad_query, grad_key, grad_value


def head_rows(part, width, head):
    return pl.ds(pl.multiple_of(part * width + head * HEAD, HEAD), HEAD)


def attention_forward(head, width, base, scale, keep, qkv):
    q_unit, q_inverse = unit_rows(qkv[base, :])
    k_unit, k_inverse = unit_rows(qkv[head_rows(1, width, head), :])
    q_scaled = (q_unit * scale).astype(BF16)
    k_round = k_unit.astype(BF16)
    v_round = qkv[head_rows(2, width, head), :].astype(BF16)
    return q_scaled, k_round, v_round, q_inverse, k_inverse, probabilities(k_round, q_scaled, keep)


def edges_kernel(x_ref, lat_ref, lon_ref, corner_ref, lon_rows, corner_rows):
    tile = x_ref[...].astype(F32).reshape(GROUPS, LON, D1)
    lat_ref[...] = tile[:EDGE].reshape(EDGE * LON, D1).astype(BF16)
    for group in range(GROUPS):
        rows = tile[group, 0:6]
        if group < EDGE:
            corner_rows[6 * group : 6 * group + 6, :] = rows
        else:
            lon_rows[6 * (group - EDGE) : 6 * (group - EDGE) + 6, :] = rows
    lon_ref[...] = lon_rows[...].astype(BF16)
    corner_ref[...] = corner_rows[...].astype(BF16)


def turn_kernel(w_ref, wt_ref):
    for part in range(3):
        cols = slice(part * D1, part * D1 + D1)
        wt_ref[cols, :] = w_ref[:, cols].T


def fine_forward_kernel(side, *refs):
    if side == 0:
        (x_ref, lat_ref, wt_ref, w_ref, gain_ref, scale_ref, last_ref,
         y_ref, ylat_ref, ylon_ref, ycor_ref, xw_ref, qkv_ref, inv_ref, soft_ref, att_ref,
         wins, qkv, keep, lon_rows, corner_rows) = refs
    else:
        (x_ref, lat_ref, lon_ref, corner_ref, first_ref, wt_ref, w_ref, gain_ref, scale_ref, last_ref,
         y_ref, ylat_ref, xw_ref, qkv_ref, inv_ref, soft_ref, att_ref, wins, qkv, keep) = refs
    tile = x_ref[...].astype(F32).reshape(GROUPS, LON, D1)
    lat_rows = lat_ref[...].astype(F32).reshape(EDGE, LON, D1)
    if side == 1:
        lon_in = lon_ref[...].astype(F32)
        corner_in = corner_ref[...].astype(F32)
    for group in range(GROUPS):
        source = tile[group + EDGE] if group + EDGE < GROUPS else lat_rows[group + EDGE - GROUPS]
        win, row = group // 18, WIN * (group % 18)
        if side == 0:
            wins[win, row : row + WIN, :] = source[6:18]
        else:
            wins[win, row : row + 6, :] = source[18:24]
            if group + EDGE < GROUPS:
                halo = lon_in[6 * group : 6 * group + 6]
            else:
                halo = corner_in[6 * (group + EDGE - GROUPS) : 6 * (group + EDGE - GROUPS) + 6]
            wins[win, row + 6 : row + WIN, :] = halo
    keep[...] = keep_matrix(last_ref)

    def window(win, carry):
        values = wins[win]
        xw_ref[win] = values.astype(BF16)
        normed = (normalize(values)[0] * gain_ref[...]).astype(BF16)
        for part in range(3):
            qkv[part * D1 : part * D1 + D1, :] = dot(
                wt_ref[part * D1 : part * D1 + D1, :], normed, 1, 1
            )
        use_keep = jnp.where(win >= 1, keep[...], 1.0)
        for head in range(H1):
            rows = slice(head * HEAD, head * HEAD + HEAD)
            krows = slice(D1 + head * HEAD, D1 + head * HEAD + HEAD)
            vrows = slice(2 * D1 + head * HEAD, 2 * D1 + head * HEAD + HEAD)
            q_scaled, k_round, v_round, q_inverse, k_inverse, soft = attention_forward(
                head, D1, rows, scale_ref[head] / HEAD, use_keep, qkv
            )
            qkv_ref[win, rows, :] = q_scaled
            qkv_ref[win, krows, :] = k_round
            qkv_ref[win, vrows, :] = v_round
            inv_ref[win, head : head + 1, :] = q_inverse
            inv_ref[win, H1 + head : H1 + head + 1, :] = k_inverse
            soft = soft.astype(BF16)
            soft_ref[win, head] = soft
            att_ref[win, rows, :] = dot(v_round, soft, 1, 0).astype(BF16)
        result = values + dot(att_ref[win], w_ref[:, 3 * D1 :], 0, 0)
        wins[win] = result
        y_ref[win] = result.astype(BF16)
        return carry

    lax.fori_loop(0, 2, window, 0)
    if side == 0:
        ylat_ref[...] = wins[0, 0:112, :].astype(BF16)
        for group in range(GROUPS):
            rows = wins[group // 18, WIN * (group % 18) : WIN * (group % 18) + 6, :]
            if group < EDGE:
                corner_rows[6 * group : 6 * group + 6, :] = rows
            else:
                lon_rows[6 * (group - EDGE) : 6 * (group - EDGE) + 6, :] = rows
        ylon_ref[...] = lon_rows[...].astype(BF16)
        ycor_ref[...] = corner_rows[...].astype(BF16)
    else:
        ylat_ref[0:112, :] = first_ref[...]
        ylat_ref[112:224, :] = wins[0, 0:112, :].astype(BF16)


def coarse_kernel(
    y0_ref, y1_ref, lat_ref, lon_ref, corner_ref, cotc_ref, mgain_ref, mw_ref, cw_ref, gain_ref,
    scale_ref, last_ref,
    out_ref, g_ref, glat_ref, glon_ref, gcor_ref,
    near, far, halo, cells, merged, mnorm, minv, qkv, gqkv, gatt, att, turned, keep, lon_rows, corner_rows, cot_rows,
):
    for group in range(18):
        cot_rows[WIN * group : WIN * group + WIN, :] = cotc_ref[group].astype(F32)
    cot = cot_rows[...].astype(BF16)
    for cut in range(4):
        lanes = slice(cut * 128, cut * 128 + 128)
        for win in range(2):
            near[cut, TOK * win : TOK * win + TOK, :] = y0_ref[win, :, lanes].astype(F32)
            far[cut, TOK * win : TOK * win + TOK, :] = y1_ref[win, :, lanes].astype(F32)
        near[cut, 2 * TOK :, :] = lat_ref[0:112, lanes].astype(F32)
        far[cut, 2 * TOK :, :] = lat_ref[112:224, lanes].astype(F32)
        halo[cut, 0:162, :] = lon_ref[:, lanes].astype(F32)
        halo[cut, 162:TOK, :] = corner_ref[:, lanes].astype(F32)
    for group in range(18):
        for part in range(4):
            cell = (2 * (group // LEV) + part % 2) * LEV + group % LEV
            source, odd, row = WIN * (cell + EDGE), part // 2, WIN * group
            for cut in range(4):
                lanes = slice(part * D1 + cut * 128, part * D1 + cut * 128 + 128)
                merged[row : row + 3, lanes] = near[cut, pl.ds(source + 6 + odd, 3, stride=2), :]
                merged[row + 3 : row + 9, lanes] = far[cut, pl.ds(source + odd, 6, stride=2), :]
                merged[row + 9 : row + WIN, lanes] = halo[cut, pl.ds(6 * cell + odd, 3, stride=2), :]
    for start in range(0, TOK, 72):
        normed, inverse = normalize(merged[start : start + 72, :])
        merged[start : start + 72, :] = normed
        minv[start : start + 72, :] = jnp.broadcast_to(inverse, (72, 128))
        mnorm[start : start + 72, :] = normed * mgain_ref[...]
    keep[...] = keep_matrix(last_ref)
    values = dot(mnorm[...].astype(BF16), mw_ref[...], 1, 0).astype(BF16).astype(F32)
    value_norm, value_inverse = normalize(values)
    normed = (value_norm * gain_ref[...]).astype(BF16)
    for start in range(0, 3 * D2, 512):
        qkv[start : start + 512, :] = dot(normed, cw_ref[:, start : start + 512], 1, 0).T
    for start in range(0, D2, 512):
        gatt[start : start + 512, :] = dot(
            cw_ref[start : start + 512, 3 * D2 :], cot, 1, 1
        ).astype(BF16)

    def heads(step, carry):
        for inner in range(4):
            head = step * 4 + inner
            rows = head_rows(0, D2, head)
            scale = scale_ref[head] / HEAD
            q_scaled, k_round, v_round, q_inverse, k_inverse, soft = attention_forward(
                head, D2, rows, scale, keep[...], qkv
            )
            soft_round = soft.astype(BF16)
            att[rows, :] = dot(v_round, soft_round, 1, 0).astype(BF16)
            grads = head_back(
                gatt[rows, :], q_scaled, k_round, v_round, soft, soft_round, q_inverse, k_inverse, scale
            )
            gqkv[rows, :] = grads[0].astype(BF16)
            gqkv[head_rows(1, D2, head), :] = grads[1].astype(BF16)
            gqkv[head_rows(2, D2, head), :] = grads[2].astype(BF16)
        return carry

    lax.fori_loop(0, H2 // 4, heads, 0)
    result = values + dot(att[...], cw_ref[:, 3 * D2 :], 0, 0)
    for group in range(18):
        out_ref[group] = result[WIN * group : WIN * group + WIN].astype(BF16)
    for start in range(0, D2, 256):
        turned[start : start + 256, :] = dot(
            cw_ref[start : start + 256, : 3 * D2], gqkv[...], 1, 0
        )
    scaled = turned[...].T * gain_ref[...]
    grad_in = cot_rows[...] + norm_back(scaled, value_norm, value_inverse)
    grad_in = grad_in.astype(BF16)
    for part in range(4):
        cols = slice(part * D1, part * D1 + D1)
        mnorm[:, cols] = dot(grad_in, mw_ref[cols, :], 1, 1) * mgain_ref[:, cols]
    for start in range(0, TOK, 72):
        mnorm[start : start + 72, :] = norm_back(
            mnorm[start : start + 72, :], merged[start : start + 72, :], minv[start : start + 72, 0:1]
        )
    for group in range(18):
        for part in range(4):
            target = (2 * (group // LEV) + part % 2) * LEV + group % LEV
            for cut in range(4):
                cells[cut, target, pl.ds(part // 2, WIN, stride=2), :] = mnorm[
                    WIN * group : WIN * group + WIN,
                    part * D1 + cut * 128 : part * D1 + cut * 128 + 128,
                ]
    done = jnp.concatenate([cells[cut] for cut in range(4)], -1)
    g_ref[...] = done.reshape(ROWS, D1).astype(BF16)
    glat_ref[...] = done[GROUPS - EDGE :].reshape(EDGE * LON, D1).astype(BF16)
    for group in range(GROUPS):
        rows = done[group, 18:24]
        if group < GROUPS - EDGE:
            lon_rows[6 * group : 6 * group + 6, :] = rows
        else:
            at = 6 * (group + EDGE - GROUPS)
            corner_rows[at : at + 6, :] = rows
    glon_ref[...] = lon_rows[...].astype(BF16)
    gcor_ref[...] = corner_rows[...].astype(BF16)


def fine_backward_kernel(side, *refs):
    if side == 1:
        (g_ref, lat_ref, cot_ref, clat_ref, clon_ref, ccor_ref,
         xw_ref, qkv_ref, inv_ref, soft_ref, att_ref, w_ref, gain_ref, scale_ref,
         gq_ref, e_ref, normt_ref, wins, gatt) = refs
        lon_cot = clon_ref[...].astype(F32)
        corner_cot = ccor_ref[...].astype(F32)
    else:
        (g_ref, lat_ref, lon_ref, corner_ref, cot_ref, clat_ref, xw_ref, qkv_ref, inv_ref, soft_ref, att_ref, w_ref, gain_ref,
         scale_ref, core_ref, gq1_ref, e1_ref, normt1_ref, att1_ref,
         gq_ref, e_ref, keep_ref, send_ref, wins, gatt, normt_ref) = refs
        lon_in = lon_ref[...].astype(F32)
        corner_in = corner_ref[...].astype(F32)
    tile = g_ref[...].astype(F32).reshape(GROUPS, LON, D1)
    lat_rows = lat_ref[...].astype(F32).reshape(EDGE, LON, D1)
    cot_tile = cot_ref[...].astype(F32).reshape(GROUPS, LON, D1)
    cot_lat = clat_ref[...].astype(F32).reshape(EDGE, LON, D1)
    for group in range(GROUPS):
        source = lat_rows[group] if group < EDGE else tile[group - EDGE]
        win, row = group // 18, WIN * (group % 18)
        inside = group + EDGE < GROUPS
        cot = cot_tile[group + EDGE] if inside else cot_lat[group + EDGE - GROUPS]
        if side == 1:
            at = 6 * group if inside else 6 * (group + EDGE - GROUPS)
            halo = lon_cot[at : at + 6] if inside else corner_cot[at : at + 6]
            wins[win, row : row + 6, :] = source[6:12] + cot[18:24]
            wins[win, row + 6 : row + WIN, :] = source[12:18] + halo
        else:
            if group < EDGE:
                halo = corner_in[6 * group : 6 * group + 6]
            else:
                halo = lon_in[6 * (group - EDGE) : 6 * (group - EDGE) + 6]
            wins[win, row : row + 6, :] = halo + cot[6:12]
            wins[win, row + 6 : row + WIN, :] = source[0:6] + cot[12:18]
    normt_ref[...] = jnp.zeros_like(normt_ref)
    gq_ref[...] = jnp.zeros_like(gq_ref)

    def window(win, carry):
        cot = wins[win].astype(BF16)
        e_ref[win] = cot
        gatt[...] = dot(w_ref[:, 3 * D1 :], cot, 1, 1).astype(BF16)
        normed = (normalize(xw_ref[win].astype(F32))[0] * gain_ref[...]).astype(BF16)
        normt_ref[win, :, 0:TOK] = normed.T
        for head in range(H1):
            rows = slice(head * HEAD, head * HEAD + HEAD)
            krows = slice(D1 + head * HEAD, D1 + head * HEAD + HEAD)
            vrows = slice(2 * D1 + head * HEAD, 2 * D1 + head * HEAD + HEAD)
            soft_round = soft_ref[win, head]
            grads = head_back(
                gatt[rows, :], qkv_ref[win, rows, :], qkv_ref[win, krows, :], qkv_ref[win, vrows, :],
                soft_round.astype(F32), soft_round,
                inv_ref[win, head : head + 1, :], inv_ref[win, H1 + head : H1 + head + 1, :],
                scale_ref[head] / HEAD,
            )
            gq_ref[win, rows, 0:TOK] = grads[0].astype(BF16)
            gq_ref[win, krows, 0:TOK] = grads[1].astype(BF16)
            gq_ref[win, vrows, 0:TOK] = grads[2].astype(BF16)
        return carry

    lax.fori_loop(0, 2, window, 0)
    if side == 0:
        sums = []
        for part in range(3):
            cols = slice(part * D1, part * D1 + D1)
            total = dot(normt_ref[0], gq_ref[0, cols, :], 1, 1) + dot(normt_ref[1], gq_ref[1, cols, :], 1, 1)
            total += dot(normt1_ref[0], gq1_ref[0, cols, :], 1, 1)
            sums.append(total + dot(normt1_ref[1], gq1_ref[1, cols, :], 1, 1))
        total = dot(att_ref[0], e_ref[0], 1, 0) + dot(att_ref[1], e_ref[1], 1, 0)
        sums.append(total + dot(att1_ref[0], e1_ref[0], 1, 0) + dot(att1_ref[1], e1_ref[1], 1, 0))
        for part in range(2):
            cols = slice(part * D1, part * D1 + D1)
            first = core_ref[0] == 0
            keep_ref[:, cols] = jnp.where(first, sums[part], sums[2 + part]).astype(BF16)
            send_ref[:, cols] = jnp.where(first, sums[2 + part], sums[part]).astype(BF16)


def fine_input_kernel(
    gq0_ref, gq1_ref, e0_ref, e1_ref, xw0_ref, xw1_ref, w_ref, gain_ref,
    g0_ref, g1_ref, glat_ref, glon_ref, gcor_ref, lat_rows, lon_rows, corner_rows,
):
    for side, (gq_ref, e_ref, xw_ref, g_ref) in enumerate(
        ((gq0_ref, e0_ref, xw0_ref, g0_ref), (gq1_ref, e1_ref, xw1_ref, g1_ref))
    ):
        for win in range(2):
            turned = dot(w_ref[:, : 3 * D1], gq_ref[win], 1, 0)
            scaled = turned.T[:TOK] * gain_ref[...]
            normed, inverse = normalize(xw_ref[win].astype(F32))
            grad_in = e_ref[win].astype(F32) + norm_back(scaled, normed, inverse)
            g_ref[win] = grad_in.astype(BF16)
            if win == 1:
                lat_rows[108 * side : 108 * side + 108, :] = grad_in[108:TOK]
            if side == 1:
                for group in range(18):
                    rows = grad_in[WIN * group + 6 : WIN * group + WIN]
                    at = 6 * (group + 18 * win)
                    if at < 162:
                        lon_rows[at : at + 6, :] = rows
                    else:
                        corner_rows[at - 162 : at - 156, :] = rows
    glat_ref[...] = lat_rows[...].astype(BF16)
    glon_ref[...] = lon_rows[...].astype(BF16)
    gcor_ref[...] = corner_rows[...].astype(BF16)


def assemble_kernel(g0_ref, g1_ref, lat_ref, lon_ref, corner_ref, out_ref, full):
    first = [g0_ref[win].astype(F32) for win in range(2)]
    second = [g1_ref[win].astype(F32) for win in range(2)]
    lat_rows = lat_ref[...].astype(F32)
    lon_rows = lon_ref[...].astype(F32)
    corner_rows = corner_ref[...].astype(F32)
    for group in range(GROUPS):
        if group < EDGE:
            full[group, 0:6, :] = corner_rows[6 * group : 6 * group + 6]
            full[group, 6:18, :] = lat_rows[WIN * group : WIN * group + WIN]
            full[group, 18:24, :] = lat_rows[108 + WIN * group : 108 + WIN * group + 6]
        else:
            own = group - EDGE
            win, row = own // 18, WIN * (own % 18)
            full[group, 0:6, :] = lon_rows[6 * own : 6 * own + 6]
            full[group, 6:18, :] = first[win][row : row + WIN]
            full[group, 18:24, :] = second[win][row : row + 6]
    out_ref[...] = full[...].reshape(ROWS, D1).astype(BF16)


def call(kernel, outs, scratch, smem_from, args, name, flops, vmem):
    whole = pl.BlockSpec(memory_space=pltpu.VMEM)
    scalars = pl.BlockSpec(memory_space=pltpu.SMEM)
    return pl.pallas_call(
        kernel,
        out_shape=[jax.ShapeDtypeStruct(shape, kind) for shape, kind in outs],
        in_specs=[scalars if position in smem_from else whole for position in range(len(args))],
        out_specs=[whole] * len(outs),
        scratch_shapes=[pltpu.VMEM(shape, kind) for shape, kind in scratch],
        compiler_params=pltpu.CompilerParams(vmem_limit_bytes=vmem * MIB),
        cost_estimate=pl.CostEstimate(flops=flops, bytes_accessed=1 << 22, transcendentals=0),
        name=name,
    )(*args)


HALF = ((2, TOK, D1), BF16)
LAT_BLOCK = ((EDGE * LON, D1), BF16)
LON_BLOCK = ((162, D1), BF16)
CORNER = ((54, D1), BF16)
LON_ROWS = ((162, D1), F32)
CORNER_ROWS = ((54, D1), F32)


def edges(tile):
    return call(edges_kernel, [LAT_BLOCK, LON_BLOCK, CORNER], [LON_ROWS, CORNER_ROWS], (), (tile,), "edges", 2 * 10**9, 6)


def turn(weights):
    return call(turn_kernel, [((3 * D1, D1), BF16)], [], (), (weights,), "turn", 10**9, 6)[0]


def fine_forward(side, ins, weights, scalars):
    outs = [HALF] + ([((112, D1), BF16), LON_BLOCK, CORNER] if side == 0 else [((224, D1), BF16)])
    outs += [
        HALF,
        ((2, 3 * D1, TOK), BF16),
        ((2, 2 * H1, TOK), F32),
        ((2, H1, TOK, TOK), BF16),
        ((2, D1, TOK), BF16),
    ]
    scratch = [((2, TOK, D1), F32), ((3 * D1, TOK), F32), ((TOK, TOK), F32)]
    if side == 0:
        scratch += [LON_ROWS, CORNER_ROWS]
    args = (*ins, *weights, *scalars)
    smem = (len(args) - 2, len(args) - 1)
    kernel = functools.partial(fine_forward_kernel, side)
    out = call(kernel, outs, scratch, smem, args, "fine_forward_" + str(side), 10**10, 10)
    return out[:-5], out[-5:]


def coarse_both(ins, cot_coarse, mgain, mw, cw, gain, scales, last):
    outs = [((18, WIN, D2), BF16), ((ROWS, D1), BF16), LAT_BLOCK, LON_BLOCK, CORNER]
    scratch = [
        ((4, 2 * TOK + 112, 128), F32),
        ((4, 2 * TOK + 112, 128), F32),
        ((4, TOK, 128), F32),
        ((4, GROUPS, LON, 128), F32),
        ((TOK, 4 * D1), F32),
        ((TOK, 4 * D1), F32),
        ((TOK, 128), F32),
        ((3 * D2, TOK), F32),
        ((3 * D2, TOK), BF16),
        ((D2, TOK), BF16),
        ((D2, TOK), BF16),
        ((D2, TOK), F32),
        ((TOK, TOK), F32),
        LON_ROWS,
        CORNER_ROWS,
        ((TOK, D2), F32),
    ]
    args = (*ins, cot_coarse, mgain, mw, cw, gain, scales, last)
    return call(coarse_kernel, outs, scratch, (10, 11), args, "coarse_both", 2 * 10**10, 22)


def fine_backward(side, ins, saved, weights, gain, scales, core=(), other=()):
    outs = [((2, 3 * D1, 256), BF16), HALF]
    scratch = [((2, TOK, D1), F32), ((D1, TOK), BF16)]
    normt = ((2, D1, 256), BF16)
    if side == 1:
        outs.append(normt)
    else:
        outs += [((D1, 2 * D1), BF16)] * 2
        scratch.append(normt)
    args = (*ins, *saved, weights, gain, scales, *core, *other)
    scalars = len(args) - len(other) - len(core) - 1
    smem = tuple(range(scalars, scalars + 1 + len(core)))
    kernel = functools.partial(fine_backward_kernel, side)
    return call(kernel, outs, scratch, smem, args, "fine_backward_" + str(side), 10**10, 14)


def fine_input(args):
    outs = [HALF, HALF, LAT_BLOCK, LON_BLOCK, CORNER]
    scratch = [((EDGE * LON, D1), F32), LON_ROWS, CORNER_ROWS]
    return call(fine_input_kernel, outs, scratch, (), args, "fine_input", 6 * 10**9, 8)


def assemble(args):
    scratch = [((GROUPS, LON, D1), F32)]
    return call(assemble_kernel, [((ROWS, D1), BF16)], scratch, (), args, "assemble", 2 * 10**9, 6)[0]


def ring(axis_size, step):
    return [(i, (i + step) % axis_size) for i in range(axis_size)]


def moved(block, axis, step):
    return lax.ppermute(block, axis, ring(lax.axis_size(axis), step))


def moved_both(block, step):
    nlon, nlat = lax.axis_size("lon"), lax.axis_size(LAT_AXES)
    route = [
        (i * nlat + j, ((i + step) % nlon) * nlat + (j + step) % nlat)
        for i in range(nlon)
        for j in range(nlat)
    ]
    return lax.ppermute(block, ("lon", *LAT_AXES), route)


def half_moved(tile, axis, dim, step):
    near, far = jnp.split(tile, 2, dim)
    if step < 0:
        return jnp.concatenate([far, moved(near, axis, step)], dim)
    return jnp.concatenate([moved(far, axis, step), near], dim)


def after(value, *others):
    return lax.optimization_barrier((value, *others))[0]


def share_sum(part, core):
    pieces = lax.all_to_all(part.reshape(64, 8, 2 * D1), ("lon", "chip"), 0, 0)
    total = jnp.sum(pieces.astype(F32), 0)
    first = core == 0
    mine = jnp.where(first, total[:4], total[4:])
    other = lax.ppermute(jnp.where(first, total[4:], total[:4]), "core", [(0, 1), (1, 0)])
    return jnp.concatenate([jnp.where(first, mine, other), jnp.where(first, other, mine)], 1)


def on_device(
    grid_field, fine_weights, fine_gain, fine_scales, merge_gain, merge_weight, coarse_weights, coarse_gain,
    coarse_scales, cot_fine, cot_coarse,
):
    core = lax.axis_index("core").astype(jnp.int32).reshape(1)
    last = (lax.axis_index(LAT_AXES) == lax.axis_size(LAT_AXES) - 1).astype(jnp.int32).reshape(1)
    fine_gain = fine_gain.reshape(1, -1)
    tile = grid_field.transpose(1, 2, 0, 3).reshape(ROWS, D1)
    lat, lon, corner = edges(tile)
    lat, lon, corner = moved(lat, LAT_AXES, -1), moved(lon, "lon", -1), moved_both(corner, -1)
    cot_coarse = after(cot_coarse, lat).transpose(1, 2, 0, 3)
    cot_coarse = half_moved(cot_coarse, "lon", 2, -1)
    weights = (turn(fine_weights), fine_weights, fine_gain)
    scalars = (fine_scales, last)
    (y0, ylat, ylon, ycor), saved0 = fine_forward(0, (tile, lat), weights, scalars)
    ylon, ycor = moved(ylon, "lon", -1), moved_both(ycor, -1)
    cot_coarse = half_moved(after(cot_coarse, y0), LAT_AXES, 0, -1).reshape(18, WIN, D2)
    (y1, ylat), saved1 = fine_forward(1, (tile, lat, lon, corner, ylat), weights, scalars)
    ylat, ylon, ycor, cot_coarse = lax.optimization_barrier((ylat, ylon, ycor, cot_coarse))
    ylat = moved(ylat, LAT_AXES, -1)
    cot_tile = after(cot_fine, y1).transpose(1, 2, 0, 3).reshape(ROWS, D1)
    cot_edges = edges(cot_tile)
    cot_edges = (moved(cot_edges[0], LAT_AXES, -1), moved(cot_edges[1], "lon", -1), moved_both(cot_edges[2], -1))
    coarse_out, grad, glat, glon, gcor = coarse_both(
        (y0, y1, ylat, ylon, ycor), cot_coarse, merge_gain.reshape(1, -1), merge_weight,
        coarse_weights, coarse_gain.reshape(1, -1), coarse_scales, last,
    )
    (glat, glon, gcor), cot_edges = lax.optimization_barrier(((glat, glon, gcor), cot_edges))
    glat, glon, gcor = moved(glat, LAT_AXES, 1), moved(glon, "lon", 1), moved_both(gcor, 1)
    coarse_out = half_moved(after(coarse_out, glat).reshape(LAT // 2, LEV, LON // 2, D2), "lon", 2, 1)
    gq1, e1, normt1 = fine_backward(
        1, (grad, glat, cot_tile, *cot_edges), saved1, fine_weights, fine_gain, fine_scales
    )
    gq1, coarse_out = lax.optimization_barrier((gq1, coarse_out))
    own, other = jnp.split(coarse_out, 2, 0)
    other = moved(other, LAT_AXES, 1)
    gq0, e0, keep, send = fine_backward(
        0, (grad, glat, glon, gcor, cot_tile, cot_edges[0]), saved0, fine_weights, fine_gain, fine_scales,
        (core,), (gq1, e1, normt1, saved1[4]),
    )
    sent = lax.ppermute(send, "core", [(0, 1), (1, 0)])
    g0, g1, lat, lon, corner = fine_input(
        (gq0, gq1, e0, e1, saved0[0], saved1[0], fine_weights, fine_gain)
    )
    lat, lon, corner = moved(lat, LAT_AXES, 1), moved(lon, "lon", 1), moved_both(corner, 1)
    sent, keep, g0, other = lax.optimization_barrier((sent, keep, g0, other))
    part = (keep.astype(F32) + sent.astype(F32)).astype(BF16)
    share = share_sum(part, core[0])
    grad_input = assemble((g0, g1, lat, lon, corner)).reshape(LAT, LEV, LON, D1)
    coarse_out = jnp.concatenate([other, own], 0)
    return coarse_out.transpose(2, 0, 1, 3), grad_input.transpose(2, 0, 1, 3), share


def solution(mesh):
    split = Mesh(mesh.devices.reshape(mesh.devices.shape[0], -1, 2), ("lon", *LAT_AXES))
    tile = P("lon", LAT_AXES, None, None)
    in_specs = (tile,) + (P(),) * 8 + (tile, tile)
    out_specs = (tile, tile, P(("lon", *LAT_AXES), None))
    return jax.shard_map(
        on_device, mesh=split, in_specs=in_specs, out_specs=out_specs, check_vma=False
    )
```

```python
import functools

import jax
import jax.numpy as jnp
from jax import lax
from jax.experimental import pallas as pl
from jax.experimental.pallas import tpu as pltpu
from jax.sharding import Mesh, PartitionSpec as P

LAT_AXES = ("chip", "core")
F32 = jnp.float32
BF16 = jnp.bfloat16
EPS_NORM = 1e-05
EPS_HEAD = 1e-06
D1, D2, H1, H2 = 512, 1024, 8, 16
HEAD = 64
TOK = 216
LON, LAT, LEV = 24, 12, 3
GROUPS = LAT * LEV
EDGE = 9
ROWS = GROUPS * LON
WIN = 12
MIB = 1024 * 1024


def dot(left, right, left_dim, right_dim):
    return lax.dot_general(
        left, right, (((left_dim,), (right_dim,)), ((), ())), preferred_element_type=F32
    )


def mean_last(values):
    return jnp.mean(values, -1, keepdims=True)


def normalize(values):
    center = values - mean_last(values)
    inverse = lax.rsqrt(mean_last(center * center) + EPS_NORM)
    return center * inverse, inverse


def norm_back(scaled, normed, inverse):
    return inverse * (scaled - mean_last(scaled) - normed * mean_last(scaled * normed))


def keep_matrix(last_ref):
    half = TOK // 2
    keys = lax.broadcasted_iota(jnp.int32, (TOK, TOK), 0) >= half
    queries = lax.broadcasted_iota(jnp.int32, (TOK, TOK), 1) >= half
    apart = jnp.where(keys == queries, 0.0, 1.0)
    return 1.0 - apart * last_ref[0].astype(F32)


def unit_rows(values):
    inverse = lax.rsqrt(jnp.mean(values * values, 0, keepdims=True) + EPS_HEAD)
    return values * inverse, inverse


def probabilities(k_round, q_scaled, keep):
    raw = jnp.exp(dot(k_round, q_scaled, 0, 0)) * keep
    return raw * (1.0 / jnp.sum(raw, 0, keepdims=True))


def head_back(grad, q_scaled, k_round, v_round, soft, soft_round, q_inverse, k_inverse, scale):
    grad_probs = dot(v_round, grad, 0, 0)
    grad_value = dot(grad, soft_round, 1, 1)
    centered = grad_probs - jnp.sum(grad_probs * soft, 0, keepdims=True)
    grad_scores = (soft * centered).astype(BF16)
    grad_q = dot(k_round, grad_scores, 1, 0)
    grad_k = dot(q_scaled, grad_scores, 1, 1)
    q_wide = q_scaled.astype(F32)
    k_wide = k_round.astype(F32)
    q_mean = jnp.mean(grad_q * q_wide, 0, keepdims=True)
    grad_query = q_inverse * (grad_q * scale - q_wide * (q_mean * (1.0 / scale)))
    grad_key = k_inverse * (grad_k - k_wide * jnp.mean(grad_k * k_wide, 0, keepdims=True))
    return grad_query, grad_key, grad_value


def head_rows(part, width, head):
    return pl.ds(pl.multiple_of(part * width + head * HEAD, HEAD), HEAD)


def attention_forward(head, width, base, scale, keep, qkv):
    q_unit, q_inverse = unit_rows(qkv[base, :])
    k_unit, k_inverse = unit_rows(qkv[head_rows(1, width, head), :])
    q_scaled = (q_unit * scale).astype(BF16)
    k_round = k_unit.astype(BF16)
    v_round = qkv[head_rows(2, width, head), :].astype(BF16)
    return q_scaled, k_round, v_round, q_inverse, k_inverse, probabilities(k_round, q_scaled, keep)


def edges_kernel(x_ref, lat_ref, lon_ref, corner_ref, lon_rows, corner_rows):
    tile = x_ref[...].astype(F32).reshape(GROUPS, LON, D1)
    lat_ref[...] = tile[:EDGE].reshape(EDGE * LON, D1).astype(BF16)
    for group in range(GROUPS):
        rows = tile[group, 0:6]
        if group < EDGE:
            corner_rows[6 * group : 6 * group + 6, :] = rows
        else:
            lon_rows[6 * (group - EDGE) : 6 * (group - EDGE) + 6, :] = rows
    lon_ref[...] = lon_rows[...].astype(BF16)
    corner_ref[...] = corner_rows[...].astype(BF16)


def turn_kernel(w_ref, wt_ref):
    for part in range(3):
        cols = slice(part * D1, part * D1 + D1)
        wt_ref[cols, :] = w_ref[:, cols].T


def fine_forward_kernel(side, *refs):
    if side == 0:
        (x_ref, lat_ref, wt_ref, w_ref, gain_ref, scale_ref, last_ref,
         y_ref, ylat_ref, ylon_ref, ycor_ref, xw_ref, qkv_ref, inv_ref, soft_ref, att_ref,
         wins, qkv, keep, lon_rows, corner_rows) = refs
    else:
        (x_ref, lat_ref, lon_ref, corner_ref, first_ref, wt_ref, w_ref, gain_ref, scale_ref, last_ref,
         y_ref, ylat_ref, xw_ref, qkv_ref, inv_ref, soft_ref, att_ref, wins, qkv, keep) = refs
    tile = x_ref[...].astype(F32).reshape(GROUPS, LON, D1)
    lat_rows = lat_ref[...].astype(F32).reshape(EDGE, LON, D1)
    if side == 1:
        lon_in = lon_ref[...].astype(F32)
        corner_in = corner_ref[...].astype(F32)
    for group in range(GROUPS):
        source = tile[group + EDGE] if group + EDGE < GROUPS else lat_rows[group + EDGE - GROUPS]
        win, row = group // 18, WIN * (group % 18)
        if side == 0:
            wins[win, row : row + WIN, :] = source[6:18]
        else:
            wins[win, row : row + 6, :] = source[18:24]
            if group + EDGE < GROUPS:
                halo = lon_in[6 * group : 6 * group + 6]
            else:
                halo = corner_in[6 * (group + EDGE - GROUPS) : 6 * (group + EDGE - GROUPS) + 6]
            wins[win, row + 6 : row + WIN, :] = halo
    keep[...] = keep_matrix(last_ref)

    def window(win, carry):
        values = wins[win]
        xw_ref[win] = values.astype(BF16)
        normed = (normalize(values)[0] * gain_ref[...]).astype(BF16)
        for part in range(3):
            qkv[part * D1 : part * D1 + D1, :] = dot(
                wt_ref[part * D1 : part * D1 + D1, :], normed, 1, 1
            )
        use_keep = jnp.where(win >= 1, keep[...], 1.0)
        for head in range(H1):
            rows = slice(head * HEAD, head * HEAD + HEAD)
            krows = slice(D1 + head * HEAD, D1 + head * HEAD + HEAD)
            vrows = slice(2 * D1 + head * HEAD, 2 * D1 + head * HEAD + HEAD)
            q_scaled, k_round, v_round, q_inverse, k_inverse, soft = attention_forward(
                head, D1, rows, scale_ref[head] / HEAD, use_keep, qkv
            )
            qkv_ref[win, rows, :] = q_scaled
            qkv_ref[win, krows, :] = k_round
            qkv_ref[win, vrows, :] = v_round
            inv_ref[win, head : head + 1, :] = q_inverse
            inv_ref[win, H1 + head : H1 + head + 1, :] = k_inverse
            soft = soft.astype(BF16)
            soft_ref[win, head] = soft
            att_ref[win, rows, :] = dot(v_round, soft, 1, 0).astype(BF16)
        result = values + dot(att_ref[win], w_ref[:, 3 * D1 :], 0, 0)
        wins[win] = result
        y_ref[win] = result.astype(BF16)
        return carry

    lax.fori_loop(0, 2, window, 0)
    if side == 0:
        ylat_ref[...] = wins[0, 0:112, :].astype(BF16)
        for group in range(GROUPS):
            rows = wins[group // 18, WIN * (group % 18) : WIN * (group % 18) + 6, :]
            if group < EDGE:
                corner_rows[6 * group : 6 * group + 6, :] = rows
            else:
                lon_rows[6 * (group - EDGE) : 6 * (group - EDGE) + 6, :] = rows
        ylon_ref[...] = lon_rows[...].astype(BF16)
        ycor_ref[...] = corner_rows[...].astype(BF16)
    else:
        ylat_ref[0:112, :] = first_ref[...]
        ylat_ref[112:224, :] = wins[0, 0:112, :].astype(BF16)


def coarse_kernel(
    y0_ref, y1_ref, lat_ref, lon_ref, corner_ref, cotc_ref, mgain_ref, mw_ref, cw_ref, gain_ref,
    scale_ref, last_ref,
    att, val_ref, g_ref, glat_ref, glon_ref, gcor_ref,
    near, far, halo, cells, merged, mnorm, minv, qkv, gqkv, gatt, turned, keep, lon_rows, corner_rows, cot_rows,
):
    for group in range(18):
        cot_rows[WIN * group : WIN * group + WIN, :] = cotc_ref[group].astype(F32)
    cot = cot_rows[...].astype(BF16)
    for cut in range(4):
        lanes = slice(cut * 128, cut * 128 + 128)
        for win in range(2):
            near[cut, TOK * win : TOK * win + TOK, :] = y0_ref[win, :, lanes].astype(F32)
            far[cut, TOK * win : TOK * win + TOK, :] = y1_ref[win, :, lanes].astype(F32)
        near[cut, 2 * TOK :, :] = lat_ref[0:112, lanes].astype(F32)
        far[cut, 2 * TOK :, :] = lat_ref[112:224, lanes].astype(F32)
        halo[cut, 0:162, :] = lon_ref[:, lanes].astype(F32)
        halo[cut, 162:TOK, :] = corner_ref[:, lanes].astype(F32)
    for group in range(18):
        for part in range(4):
            cell = (2 * (group // LEV) + part % 2) * LEV + group % LEV
            source, odd, row = WIN * (cell + EDGE), part // 2, WIN * group
            for cut in range(4):
                lanes = slice(part * D1 + cut * 128, part * D1 + cut * 128 + 128)
                merged[row : row + 3, lanes] = near[cut, pl.ds(source + 6 + odd, 3, stride=2), :]
                merged[row + 3 : row + 9, lanes] = far[cut, pl.ds(source + odd, 6, stride=2), :]
                merged[row + 9 : row + WIN, lanes] = halo[cut, pl.ds(6 * cell + odd, 3, stride=2), :]
    for start in range(0, TOK, 72):
        normed, inverse = normalize(merged[start : start + 72, :])
        merged[start : start + 72, :] = normed
        minv[start : start + 72, :] = jnp.broadcast_to(inverse, (72, 128))
        mnorm[start : start + 72, :] = normed * mgain_ref[...]
    keep[...] = keep_matrix(last_ref)
    values = dot(mnorm[...].astype(BF16), mw_ref[...], 1, 0).astype(BF16).astype(F32)
    value_norm, value_inverse = normalize(values)
    normed = (value_norm * gain_ref[...]).astype(BF16)
    for start in range(0, 3 * D2, 512):
        qkv[start : start + 512, :] = dot(normed, cw_ref[:, start : start + 512], 1, 0).T
    for start in range(0, D2, 512):
        gatt[start : start + 512, :] = dot(
            cw_ref[start : start + 512, 3 * D2 :], cot, 1, 1
        ).astype(BF16)

    def heads(step, carry):
        for inner in range(4):
            head = step * 4 + inner
            rows = head_rows(0, D2, head)
            scale = scale_ref[head] / HEAD
            q_scaled, k_round, v_round, q_inverse, k_inverse, soft = attention_forward(
                head, D2, rows, scale, keep[...], qkv
            )
            soft_round = soft.astype(BF16)
            att[rows, :] = dot(v_round, soft_round, 1, 0).astype(BF16)
            grads = head_back(
                gatt[rows, :], q_scaled, k_round, v_round, soft, soft_round, q_inverse, k_inverse, scale
            )
            gqkv[rows, :] = grads[0].astype(BF16)
            gqkv[head_rows(1, D2, head), :] = grads[1].astype(BF16)
            gqkv[head_rows(2, D2, head), :] = grads[2].astype(BF16)
        return carry

    lax.fori_loop(0, H2 // 4, heads, 0)
    val_ref[...] = values.astype(BF16)
    for start in range(0, D2, 256):
        turned[start : start + 256, :] = dot(
            cw_ref[start : start + 256, : 3 * D2], gqkv[...], 1, 0
        )
    scaled = turned[...].T * gain_ref[...]
    grad_in = cot_rows[...] + norm_back(scaled, value_norm, value_inverse)
    grad_in = grad_in.astype(BF16)
    for part in range(4):
        cols = slice(part * D1, part * D1 + D1)
        mnorm[:, cols] = dot(grad_in, mw_ref[cols, :], 1, 1) * mgain_ref[:, cols]
    for start in range(0, TOK, 72):
        mnorm[start : start + 72, :] = norm_back(
            mnorm[start : start + 72, :], merged[start : start + 72, :], minv[start : start + 72, 0:1]
        )
    for group in range(18):
        for part in range(4):
            target = (2 * (group // LEV) + part % 2) * LEV + group % LEV
            for cut in range(4):
                cells[cut, target, pl.ds(part // 2, WIN, stride=2), :] = mnorm[
                    WIN * group : WIN * group + WIN,
                    part * D1 + cut * 128 : part * D1 + cut * 128 + 128,
                ]
    done = jnp.concatenate([cells[cut] for cut in range(4)], -1)
    g_ref[...] = done.reshape(ROWS, D1).astype(BF16)
    glat_ref[...] = done[GROUPS - EDGE :].reshape(EDGE * LON, D1).astype(BF16)
    for group in range(GROUPS):
        rows = done[group, 18:24]
        if group < GROUPS - EDGE:
            lon_rows[6 * group : 6 * group + 6, :] = rows
        else:
            at = 6 * (group + EDGE - GROUPS)
            corner_rows[at : at + 6, :] = rows
    glon_ref[...] = lon_rows[...].astype(BF16)
    gcor_ref[...] = corner_rows[...].astype(BF16)


def coarse_out_kernel(att_ref, val_ref, cw_ref, out_ref):
    result = val_ref[...].astype(F32) + dot(att_ref[...], cw_ref[:, 3 * D2 :], 0, 0)
    for group in range(18):
        out_ref[group] = result[WIN * group : WIN * group + WIN].astype(BF16)


def normed_kernel(xw0_ref, xw1_ref, gain_ref, normt0_ref, normt1_ref):
    for xw_ref, normt_ref in ((xw0_ref, normt0_ref), (xw1_ref, normt1_ref)):
        normt_ref[...] = jnp.zeros_like(normt_ref)
        for win in range(2):
            normed = (normalize(xw_ref[win].astype(F32))[0] * gain_ref[...]).astype(BF16)
            normt_ref[win, :, 0:TOK] = normed.T


def fine_backward_kernel(side, *refs):
    if side == 1:
        (g_ref, lat_ref, cot_ref, clat_ref, clon_ref, ccor_ref,
         qkv_ref, inv_ref, soft_ref, att_ref, w_ref, scale_ref, gq_ref, e_ref, wins, gatt) = refs
        lon_cot = clon_ref[...].astype(F32)
        corner_cot = ccor_ref[...].astype(F32)
    else:
        (g_ref, lat_ref, lon_ref, corner_ref, cot_ref, clat_ref, qkv_ref, inv_ref, soft_ref, att_ref, w_ref,
         scale_ref, core_ref, gq1_ref, e1_ref, att1_ref, normt_ref, normt1_ref,
         gq_ref, e_ref, keep_ref, send_ref, wins, gatt) = refs
        lon_in = lon_ref[...].astype(F32)
        corner_in = corner_ref[...].astype(F32)
    tile = g_ref[...].astype(F32).reshape(GROUPS, LON, D1)
    lat_rows = lat_ref[...].astype(F32).reshape(EDGE, LON, D1)
    cot_tile = cot_ref[...].astype(F32).reshape(GROUPS, LON, D1)
    cot_lat = clat_ref[...].astype(F32).reshape(EDGE, LON, D1)
    for group in range(GROUPS):
        source = lat_rows[group] if group < EDGE else tile[group - EDGE]
        win, row = group // 18, WIN * (group % 18)
        inside = group + EDGE < GROUPS
        cot = cot_tile[group + EDGE] if inside else cot_lat[group + EDGE - GROUPS]
        if side == 1:
            at = 6 * group if inside else 6 * (group + EDGE - GROUPS)
            halo = lon_cot[at : at + 6] if inside else corner_cot[at : at + 6]
            wins[win, row : row + 6, :] = source[6:12] + cot[18:24]
            wins[win, row + 6 : row + WIN, :] = source[12:18] + halo
        else:
            if group < EDGE:
                halo = corner_in[6 * group : 6 * group + 6]
            else:
                halo = lon_in[6 * (group - EDGE) : 6 * (group - EDGE) + 6]
            wins[win, row : row + 6, :] = halo + cot[6:12]
            wins[win, row + 6 : row + WIN, :] = source[0:6] + cot[12:18]
    gq_ref[...] = jnp.zeros_like(gq_ref)

    def window(win, carry):
        cot = wins[win].astype(BF16)
        e_ref[win] = cot
        gatt[...] = dot(w_ref[:, 3 * D1 :], cot, 1, 1).astype(BF16)
        for head in range(H1):
            rows = slice(head * HEAD, head * HEAD + HEAD)
            krows = slice(D1 + head * HEAD, D1 + head * HEAD + HEAD)
            vrows = slice(2 * D1 + head * HEAD, 2 * D1 + head * HEAD + HEAD)
            soft_round = soft_ref[win, head]
            grads = head_back(
                gatt[rows, :], qkv_ref[win, rows, :], qkv_ref[win, krows, :], qkv_ref[win, vrows, :],
                soft_round.astype(F32), soft_round,
                inv_ref[win, head : head + 1, :], inv_ref[win, H1 + head : H1 + head + 1, :],
                scale_ref[head] / HEAD,
            )
            gq_ref[win, rows, 0:TOK] = grads[0].astype(BF16)
            gq_ref[win, krows, 0:TOK] = grads[1].astype(BF16)
            gq_ref[win, vrows, 0:TOK] = grads[2].astype(BF16)
        return carry

    lax.fori_loop(0, 2, window, 0)
    if side == 0:
        sums = []
        for part in range(3):
            cols = slice(part * D1, part * D1 + D1)
            total = dot(normt_ref[0], gq_ref[0, cols, :], 1, 1) + dot(normt_ref[1], gq_ref[1, cols, :], 1, 1)
            total += dot(normt1_ref[0], gq1_ref[0, cols, :], 1, 1)
            sums.append(total + dot(normt1_ref[1], gq1_ref[1, cols, :], 1, 1))
        total = dot(att_ref[0], e_ref[0], 1, 0) + dot(att_ref[1], e_ref[1], 1, 0)
        sums.append(total + dot(att1_ref[0], e1_ref[0], 1, 0) + dot(att1_ref[1], e1_ref[1], 1, 0))
        for part in range(2):
            cols = slice(part * D1, part * D1 + D1)
            first = core_ref[0] == 0
            keep_ref[:, cols] = jnp.where(first, sums[part], sums[2 + part]).astype(BF16)
            send_ref[:, cols] = jnp.where(first, sums[2 + part], sums[part]).astype(BF16)


def fine_input_kernel(
    gq0_ref, gq1_ref, e0_ref, e1_ref, xw0_ref, xw1_ref, w_ref, gain_ref,
    g0_ref, g1_ref, glat_ref, glon_ref, gcor_ref, lat_rows, lon_rows, corner_rows,
):
    for side, (gq_ref, e_ref, xw_ref, g_ref) in enumerate(
        ((gq0_ref, e0_ref, xw0_ref, g0_ref), (gq1_ref, e1_ref, xw1_ref, g1_ref))
    ):
        for win in range(2):
            turned = dot(w_ref[:, : 3 * D1], gq_ref[win], 1, 0)
            scaled = turned.T[:TOK] * gain_ref[...]
            normed, inverse = normalize(xw_ref[win].astype(F32))
            grad_in = e_ref[win].astype(F32) + norm_back(scaled, normed, inverse)
            g_ref[win] = grad_in.astype(BF16)
            if win == 1:
                lat_rows[108 * side : 108 * side + 108, :] = grad_in[108:TOK]
            if side == 1:
                for group in range(18):
                    rows = grad_in[WIN * group + 6 : WIN * group + WIN]
                    at = 6 * (group + 18 * win)
                    if at < 162:
                        lon_rows[at : at + 6, :] = rows
                    else:
                        corner_rows[at - 162 : at - 156, :] = rows
    glat_ref[...] = lat_rows[...].astype(BF16)
    glon_ref[...] = lon_rows[...].astype(BF16)
    gcor_ref[...] = corner_rows[...].astype(BF16)


def assemble_kernel(g0_ref, g1_ref, lat_ref, lon_ref, corner_ref, out_ref, full):
    first = [g0_ref[win].astype(F32) for win in range(2)]
    second = [g1_ref[win].astype(F32) for win in range(2)]
    lat_rows = lat_ref[...].astype(F32)
    lon_rows = lon_ref[...].astype(F32)
    corner_rows = corner_ref[...].astype(F32)
    for group in range(GROUPS):
        if group < EDGE:
            full[group, 0:6, :] = corner_rows[6 * group : 6 * group + 6]
            full[group, 6:18, :] = lat_rows[WIN * group : WIN * group + WIN]
            full[group, 18:24, :] = lat_rows[108 + WIN * group : 108 + WIN * group + 6]
        else:
            own = group - EDGE
            win, row = own // 18, WIN * (own % 18)
            full[group, 0:6, :] = lon_rows[6 * own : 6 * own + 6]
            full[group, 6:18, :] = first[win][row : row + WIN]
            full[group, 18:24, :] = second[win][row : row + 6]
    out_ref[...] = full[...].reshape(ROWS, D1).astype(BF16)


def call(kernel, outs, scratch, smem_from, args, name, flops, vmem):
    whole = pl.BlockSpec(memory_space=pltpu.VMEM)
    scalars = pl.BlockSpec(memory_space=pltpu.SMEM)
    return pl.pallas_call(
        kernel,
        out_shape=[jax.ShapeDtypeStruct(shape, kind) for shape, kind in outs],
        in_specs=[scalars if position in smem_from else whole for position in range(len(args))],
        out_specs=[whole] * len(outs),
        scratch_shapes=[pltpu.VMEM(shape, kind) for shape, kind in scratch],
        compiler_params=pltpu.CompilerParams(vmem_limit_bytes=vmem * MIB),
        cost_estimate=pl.CostEstimate(flops=flops, bytes_accessed=1 << 22, transcendentals=0),
        name=name,
    )(*args)


HALF = ((2, TOK, D1), BF16)
LAT_BLOCK = ((EDGE * LON, D1), BF16)
LON_BLOCK = ((162, D1), BF16)
CORNER = ((54, D1), BF16)
LON_ROWS = ((162, D1), F32)
CORNER_ROWS = ((54, D1), F32)


def edges(tile):
    return call(edges_kernel, [LAT_BLOCK, LON_BLOCK, CORNER], [LON_ROWS, CORNER_ROWS], (), (tile,), "edges", 2 * 10**9, 6)


def turn(weights):
    return call(turn_kernel, [((3 * D1, D1), BF16)], [], (), (weights,), "turn", 10**9, 6)[0]


def fine_forward(side, ins, weights, scalars):
    outs = [HALF] + ([((112, D1), BF16), LON_BLOCK, CORNER] if side == 0 else [((224, D1), BF16)])
    outs += [
        HALF,
        ((2, 3 * D1, TOK), BF16),
        ((2, 2 * H1, TOK), F32),
        ((2, H1, TOK, TOK), BF16),
        ((2, D1, TOK), BF16),
    ]
    scratch = [((2, TOK, D1), F32), ((3 * D1, TOK), F32), ((TOK, TOK), F32)]
    if side == 0:
        scratch += [LON_ROWS, CORNER_ROWS]
    args = (*ins, *weights, *scalars)
    smem = (len(args) - 2, len(args) - 1)
    kernel = functools.partial(fine_forward_kernel, side)
    out = call(kernel, outs, scratch, smem, args, "fine_forward_" + str(side), 10**10, 10)
    return out[:-5], out[-5:]


def coarse_both(ins, cot_coarse, mgain, mw, cw, gain, scales, last):
    outs = [((D2, TOK), BF16), ((TOK, D2), BF16), ((ROWS, D1), BF16), LAT_BLOCK, LON_BLOCK, CORNER]
    scratch = [
        ((4, 2 * TOK + 112, 128), F32),
        ((4, 2 * TOK + 112, 128), F32),
        ((4, TOK, 128), F32),
        ((4, GROUPS, LON, 128), F32),
        ((TOK, 4 * D1), F32),
        ((TOK, 4 * D1), F32),
        ((TOK, 128), F32),
        ((3 * D2, TOK), F32),
        ((3 * D2, TOK), BF16),
        ((D2, TOK), BF16),
        ((D2, TOK), F32),
        ((TOK, TOK), F32),
        LON_ROWS,
        CORNER_ROWS,
        ((TOK, D2), F32),
    ]
    args = (*ins, cot_coarse, mgain, mw, cw, gain, scales, last)
    return call(coarse_kernel, outs, scratch, (10, 11), args, "coarse_both", 2 * 10**10, 22)


def coarse_result(att, values, weights):
    return call(
        coarse_out_kernel, [((18, WIN, D2), BF16)], [], (), (att, values, weights), "coarse_out", 10**9, 16
    )[0]


def normed_turned(xw0, xw1, gain):
    outs = [((2, D1, 256), BF16)] * 2
    return call(normed_kernel, outs, [], (), (xw0, xw1, gain), "normed", 10**9, 8)


def fine_backward(side, ins, saved, weights, scales, core=(), other=()):
    outs = [((2, 3 * D1, 256), BF16), HALF]
    scratch = [((2, TOK, D1), F32), ((D1, TOK), BF16)]
    if side == 0:
        outs += [((D1, 2 * D1), BF16)] * 2
    args = (*ins, *saved, weights, scales, *core, *other)
    scalars = len(args) - len(other) - len(core) - 1
    smem = tuple(range(scalars, scalars + 1 + len(core)))
    kernel = functools.partial(fine_backward_kernel, side)
    return call(kernel, outs, scratch, smem, args, "fine_backward_" + str(side), 10**10, 14)


def fine_input(args):
    outs = [HALF, HALF, LAT_BLOCK, LON_BLOCK, CORNER]
    scratch = [((EDGE * LON, D1), F32), LON_ROWS, CORNER_ROWS]
    return call(fine_input_kernel, outs, scratch, (), args, "fine_input", 6 * 10**9, 8)


def assemble(args):
    scratch = [((GROUPS, LON, D1), F32)]
    return call(assemble_kernel, [((ROWS, D1), BF16)], scratch, (), args, "assemble", 2 * 10**9, 6)[0]


def ring(axis_size, step):
    return [(i, (i + step) % axis_size) for i in range(axis_size)]


def moved(block, axis, step):
    return lax.ppermute(block, axis, ring(lax.axis_size(axis), step))


def moved_both(block, step):
    nlon, nlat = lax.axis_size("lon"), lax.axis_size(LAT_AXES)
    route = [
        (i * nlat + j, ((i + step) % nlon) * nlat + (j + step) % nlat)
        for i in range(nlon)
        for j in range(nlat)
    ]
    return lax.ppermute(block, ("lon", *LAT_AXES), route)


def half_moved(tile, axis, dim, step):
    near, far = jnp.split(tile, 2, dim)
    if step < 0:
        return jnp.concatenate([far, moved(near, axis, step)], dim)
    return jnp.concatenate([moved(far, axis, step), near], dim)


def after(value, *others):
    return lax.optimization_barrier((value, *others))[0]


def share_sum(part, core):
    pieces = lax.all_to_all(part.reshape(64, 8, 2 * D1), ("lon", "chip"), 0, 0)
    total = jnp.sum(pieces.astype(F32), 0)
    first = core == 0
    mine = jnp.where(first, total[:4], total[4:])
    other = lax.ppermute(jnp.where(first, total[4:], total[:4]), "core", [(0, 1), (1, 0)])
    return jnp.concatenate([jnp.where(first, mine, other), jnp.where(first, other, mine)], 1)


def on_device(
    grid_field, fine_weights, fine_gain, fine_scales, merge_gain, merge_weight, coarse_weights, coarse_gain,
    coarse_scales, cot_fine, cot_coarse,
):
    core = lax.axis_index("core").astype(jnp.int32).reshape(1)
    last = (lax.axis_index(LAT_AXES) == lax.axis_size(LAT_AXES) - 1).astype(jnp.int32).reshape(1)
    fine_gain = fine_gain.reshape(1, -1)
    tile = grid_field.transpose(1, 2, 0, 3).reshape(ROWS, D1)
    lat, lon, corner = edges(tile)
    lat, lon, corner = moved(lat, LAT_AXES, -1), moved(lon, "lon", -1), moved_both(corner, -1)
    cot_coarse = after(cot_coarse, lat).transpose(1, 2, 0, 3)
    cot_coarse = half_moved(cot_coarse, "lon", 2, -1)
    weights = (turn(fine_weights), fine_weights, fine_gain)
    scalars = (fine_scales, last)
    (y0, ylat, ylon, ycor), saved0 = fine_forward(0, (tile, lat), weights, scalars)
    ylon, ycor = moved(ylon, "lon", -1), moved_both(ycor, -1)
    cot_coarse = half_moved(after(cot_coarse, y0), LAT_AXES, 0, -1).reshape(18, WIN, D2)
    (y1, ylat), saved1 = fine_forward(1, (tile, lat, lon, corner, ylat), weights, scalars)
    ylat, ylon, ycor, cot_coarse = lax.optimization_barrier((ylat, ylon, ycor, cot_coarse))
    ylat = moved(ylat, LAT_AXES, -1)
    cot_tile = after(cot_fine, y1).transpose(1, 2, 0, 3).reshape(ROWS, D1)
    cot_edges = edges(cot_tile)
    cot_edges = (moved(cot_edges[0], LAT_AXES, -1), moved(cot_edges[1], "lon", -1), moved_both(cot_edges[2], -1))
    att, values, grad, glat, glon, gcor = coarse_both(
        (y0, y1, ylat, ylon, ycor), cot_coarse, merge_gain.reshape(1, -1), merge_weight,
        coarse_weights, coarse_gain.reshape(1, -1), coarse_scales, last,
    )
    (glat, glon, gcor), cot_edges = lax.optimization_barrier(((glat, glon, gcor), cot_edges))
    glat, glon, gcor = moved(glat, LAT_AXES, 1), moved(glon, "lon", 1), moved_both(gcor, 1)
    coarse_out = coarse_result(att, values, coarse_weights)
    normt0, normt1 = normed_turned(saved0[0], saved1[0], after(fine_gain, att))
    coarse_out, glat, normt0, normt1 = lax.optimization_barrier((coarse_out, glat, normt0, normt1))
    coarse_out = half_moved(coarse_out.reshape(LAT // 2, LEV, LON // 2, D2), "lon", 2, 1)
    gq1, e1 = fine_backward(1, (grad, glat, cot_tile, *cot_edges), saved1[1:], fine_weights, fine_scales)
    own, other = jnp.split(coarse_out, 2, 0)
    other = moved(other, LAT_AXES, 1)
    gq0, e0, keep, send = fine_backward(
        0, (grad, glat, glon, gcor, cot_tile, cot_edges[0]), saved0[1:], fine_weights, fine_scales,
        (core,), (gq1, e1, saved1[4], normt0, normt1),
    )
    sent = lax.ppermute(send, "core", [(0, 1), (1, 0)])
    g0, g1, lat, lon, corner = fine_input(
        (gq0, gq1, e0, e1, saved0[0], saved1[0], fine_weights, fine_gain)
    )
    lat, lon, corner = moved(lat, LAT_AXES, 1), moved(lon, "lon", 1), moved_both(corner, 1)
    sent, keep, g0 = lax.optimization_barrier((sent, keep, g0))
    part = (keep.astype(F32) + sent.astype(F32)).astype(BF16)
    share = share_sum(part, core[0])
    grad_input = assemble((g0, g1, lat, lon, corner)).reshape(LAT, LEV, LON, D1)
    coarse_out = jnp.concatenate([after(other, corner), own], 0)
    return coarse_out.transpose(2, 0, 1, 3), grad_input.transpose(2, 0, 1, 3), share


def solution(mesh):
    split = Mesh(mesh.devices.reshape(mesh.devices.shape[0], -1, 2), ("lon", *LAT_AXES))
    tile = P("lon", LAT_AXES, None, None)
    in_specs = (tile,) + (P(),) * 8 + (tile, tile)
    out_specs = (tile, tile, P(("lon", *LAT_AXES), None))
    return jax.shard_map(
        on_device, mesh=split, in_specs=in_specs, out_specs=out_specs, check_vma=False
    )
```

```python
import functools

import jax
import jax.numpy as jnp
from jax import lax
from jax.experimental import pallas as pl
from jax.experimental.pallas import tpu as pltpu
from jax.sharding import Mesh, PartitionSpec as P

LAT_AXES = ("chip", "core")
F32 = jnp.float32
BF16 = jnp.bfloat16
EPS_NORM = 1e-05
EPS_HEAD = 1e-06
D1, D2, H1, H2 = 512, 1024, 8, 16
HEAD = 64
TOK = 216
LON, LAT, LEV = 24, 12, 3
GROUPS = LAT * LEV
EDGE = 9
ROWS = GROUPS * LON
WIN = 12
FINE_BATCH, COARSE_BATCH, BACK_BATCH = 8, 4, 8
MIB = 1024 * 1024


def dot(left, right, left_dim, right_dim):
    return lax.dot_general(
        left, right, (((left_dim,), (right_dim,)), ((), ())), preferred_element_type=F32
    )


def mean_last(values):
    return jnp.mean(values, -1, keepdims=True)


def normalize(values):
    center = values - mean_last(values)
    inverse = lax.rsqrt(mean_last(center * center) + EPS_NORM)
    return center * inverse, inverse


def norm_back(scaled, normed, inverse):
    return inverse * (scaled - mean_last(scaled) - normed * mean_last(scaled * normed))


def keep_matrix(last_ref):
    half = TOK // 2
    keys = lax.broadcasted_iota(jnp.int32, (TOK, TOK), 0) >= half
    queries = lax.broadcasted_iota(jnp.int32, (TOK, TOK), 1) >= half
    apart = jnp.where(keys == queries, 0.0, 1.0)
    return 1.0 - apart * last_ref[0].astype(F32)


def unit_rows(values):
    inverse = lax.rsqrt(jnp.mean(values * values, 0, keepdims=True) + EPS_HEAD)
    return values * inverse, inverse


def softmax_rows(scores, keep):
    raw = jnp.exp(scores) * keep
    return raw * (1.0 / jnp.sum(raw, 0, keepdims=True))


def heads_back(grads, parts, softs, rounds, inverses, scales):
    grad_probs = [dot(part[2], grad, 0, 0) for part, grad in zip(parts, grads)]
    grad_values = [dot(grad, soft, 1, 1) for grad, soft in zip(grads, rounds)]
    grad_scores = [
        (soft * (probs - jnp.sum(probs * soft, 0, keepdims=True))).astype(BF16)
        for probs, soft in zip(grad_probs, softs)
    ]
    grad_q = [dot(part[1], scores, 1, 0) for part, scores in zip(parts, grad_scores)]
    grad_k = [dot(part[0], scores, 1, 1) for part, scores in zip(parts, grad_scores)]
    results = []
    for index, part in enumerate(parts):
        scale, (q_inverse, k_inverse) = scales[index], inverses[index]
        q_wide, k_wide = part[0].astype(F32), part[1].astype(F32)
        q_mean = jnp.mean(grad_q[index] * q_wide, 0, keepdims=True)
        k_mean = jnp.mean(grad_k[index] * k_wide, 0, keepdims=True)
        results.append((
            q_inverse * (grad_q[index] * scale - q_wide * (q_mean * (1.0 / scale))),
            k_inverse * (grad_k[index] - k_wide * k_mean),
            grad_values[index],
        ))
    return results


def head_rows(part, width, head):
    if isinstance(head, int):
        return slice(part * width + head * HEAD, part * width + head * HEAD + HEAD)
    return pl.ds(pl.multiple_of(part * width + head * HEAD, HEAD), HEAD)


def head_parts(head, width, scale, qkv):
    q_unit, q_inverse = unit_rows(qkv[head_rows(0, width, head), :])
    k_unit, k_inverse = unit_rows(qkv[head_rows(1, width, head), :])
    v_round = qkv[head_rows(2, width, head), :].astype(BF16)
    return (q_unit * scale).astype(BF16), k_unit.astype(BF16), v_round, q_inverse, k_inverse


def edges_kernel(x_ref, lat_ref, lon_ref, corner_ref, lon_rows, corner_rows):
    tile = x_ref[...].astype(F32).reshape(GROUPS, LON, D1)
    lat_ref[...] = tile[:EDGE].reshape(EDGE * LON, D1).astype(BF16)
    for group in range(GROUPS):
        rows = tile[group, 0:6]
        if group < EDGE:
            corner_rows[6 * group : 6 * group + 6, :] = rows
        else:
            lon_rows[6 * (group - EDGE) : 6 * (group - EDGE) + 6, :] = rows
    lon_ref[...] = lon_rows[...].astype(BF16)
    corner_ref[...] = corner_rows[...].astype(BF16)


def turn_kernel(w_ref, wt_ref):
    for part in range(3):
        cols = slice(part * D1, part * D1 + D1)
        wt_ref[cols, :] = w_ref[:, cols].T


def fine_forward_kernel(side, *refs):
    if side == 0:
        (x_ref, lat_ref, wt_ref, w_ref, gain_ref, scale_ref, last_ref,
         y_ref, ylat_ref, ylon_ref, ycor_ref, xw_ref, qkv_ref, inv_ref, soft_ref, att_ref,
         wins, qkv, keep, lon_rows, corner_rows) = refs
    else:
        (x_ref, lat_ref, lon_ref, corner_ref, first_ref, wt_ref, w_ref, gain_ref, scale_ref, last_ref,
         y_ref, ylat_ref, xw_ref, qkv_ref, inv_ref, soft_ref, att_ref, wins, qkv, keep) = refs
    tile = x_ref[...].astype(F32).reshape(GROUPS, LON, D1)
    lat_rows = lat_ref[...].astype(F32).reshape(EDGE, LON, D1)
    if side == 1:
        lon_in = lon_ref[...].astype(F32)
        corner_in = corner_ref[...].astype(F32)
    for group in range(GROUPS):
        source = tile[group + EDGE] if group + EDGE < GROUPS else lat_rows[group + EDGE - GROUPS]
        win, row = group // 18, WIN * (group % 18)
        if side == 0:
            wins[win, row : row + WIN, :] = source[6:18]
        else:
            wins[win, row : row + 6, :] = source[18:24]
            if group + EDGE < GROUPS:
                halo = lon_in[6 * group : 6 * group + 6]
            else:
                halo = corner_in[6 * (group + EDGE - GROUPS) : 6 * (group + EDGE - GROUPS) + 6]
            wins[win, row + 6 : row + WIN, :] = halo
    keep[...] = keep_matrix(last_ref)

    def window(win, carry):
        values = wins[win]
        xw_ref[win] = values.astype(BF16)
        normed = (normalize(values)[0] * gain_ref[...]).astype(BF16)
        for part in range(3):
            qkv[part * D1 : part * D1 + D1, :] = dot(
                wt_ref[part * D1 : part * D1 + D1, :], normed, 1, 1
            )
        use_keep = jnp.where(win >= 1, keep[...], 1.0)
        for start in range(0, H1, FINE_BATCH):
            batch = range(start, start + FINE_BATCH)
            parts = []
            for head in batch:
                q_scaled, k_round, v_round, q_inverse, k_inverse = head_parts(
                    head, D1, scale_ref[head] / HEAD, qkv
                )
                qkv_ref[win, head_rows(0, D1, head), :] = q_scaled
                qkv_ref[win, head_rows(1, D1, head), :] = k_round
                qkv_ref[win, head_rows(2, D1, head), :] = v_round
                inv_ref[win, head : head + 1, :] = q_inverse
                inv_ref[win, H1 + head : H1 + head + 1, :] = k_inverse
                parts.append((q_scaled, k_round, v_round))
            scores = [dot(k_round, q_scaled, 0, 0) for q_scaled, k_round, _ in parts]
            softs = [softmax_rows(score, use_keep).astype(BF16) for score in scores]
            for head, soft, part in zip(batch, softs, parts):
                soft_ref[win, head] = soft
                att_ref[win, head_rows(0, D1, head), :] = dot(part[2], soft, 1, 0).astype(BF16)
        result = values + dot(att_ref[win], w_ref[:, 3 * D1 :], 0, 0)
        wins[win] = result
        y_ref[win] = result.astype(BF16)
        return carry

    lax.fori_loop(0, 2, window, 0)
    if side == 0:
        ylat_ref[...] = wins[0, 0:112, :].astype(BF16)
        for group in range(GROUPS):
            rows = wins[group // 18, WIN * (group % 18) : WIN * (group % 18) + 6, :]
            if group < EDGE:
                corner_rows[6 * group : 6 * group + 6, :] = rows
            else:
                lon_rows[6 * (group - EDGE) : 6 * (group - EDGE) + 6, :] = rows
        ylon_ref[...] = lon_rows[...].astype(BF16)
        ycor_ref[...] = corner_rows[...].astype(BF16)
    else:
        ylat_ref[0:112, :] = first_ref[...]
        ylat_ref[112:224, :] = wins[0, 0:112, :].astype(BF16)


def coarse_kernel(
    y0_ref, y1_ref, lat_ref, lon_ref, corner_ref, cotc_ref, mgain_ref, mw_ref, cw_ref, gain_ref,
    scale_ref, last_ref,
    att, val_ref, g_ref, glat_ref, glon_ref, gcor_ref,
    near, far, halo, cells, merged, mnorm, minv, qkv, gqkv, gatt, turned, keep, lon_rows, corner_rows, cot_rows,
):
    for group in range(18):
        cot_rows[WIN * group : WIN * group + WIN, :] = cotc_ref[group].astype(F32)
    cot = cot_rows[...].astype(BF16)
    for cut in range(4):
        lanes = slice(cut * 128, cut * 128 + 128)
        for win in range(2):
            near[cut, TOK * win : TOK * win + TOK, :] = y0_ref[win, :, lanes].astype(F32)
            far[cut, TOK * win : TOK * win + TOK, :] = y1_ref[win, :, lanes].astype(F32)
        near[cut, 2 * TOK :, :] = lat_ref[0:112, lanes].astype(F32)
        far[cut, 2 * TOK :, :] = lat_ref[112:224, lanes].astype(F32)
        halo[cut, 0:162, :] = lon_ref[:, lanes].astype(F32)
        halo[cut, 162:TOK, :] = corner_ref[:, lanes].astype(F32)
    for group in range(18):
        for part in range(4):
            cell = (2 * (group // LEV) + part % 2) * LEV + group % LEV
            source, odd, row = WIN * (cell + EDGE), part // 2, WIN * group
            for cut in range(4):
                lanes = slice(part * D1 + cut * 128, part * D1 + cut * 128 + 128)
                merged[row : row + 3, lanes] = near[cut, pl.ds(source + 6 + odd, 3, stride=2), :]
                merged[row + 3 : row + 9, lanes] = far[cut, pl.ds(source + odd, 6, stride=2), :]
                merged[row + 9 : row + WIN, lanes] = halo[cut, pl.ds(6 * cell + odd, 3, stride=2), :]
    for start in range(0, TOK, 72):
        normed, inverse = normalize(merged[start : start + 72, :])
        merged[start : start + 72, :] = normed
        minv[start : start + 72, :] = jnp.broadcast_to(inverse, (72, 128))
        mnorm[start : start + 72, :] = normed * mgain_ref[...]
    keep[...] = keep_matrix(last_ref)
    values = dot(mnorm[...].astype(BF16), mw_ref[...], 1, 0).astype(BF16).astype(F32)
    value_norm, value_inverse = normalize(values)
    normed = (value_norm * gain_ref[...]).astype(BF16)
    for start in range(0, 3 * D2, 512):
        qkv[start : start + 512, :] = dot(normed, cw_ref[:, start : start + 512], 1, 0).T
    for start in range(0, D2, 512):
        gatt[start : start + 512, :] = dot(
            cw_ref[start : start + 512, 3 * D2 :], cot, 1, 1
        ).astype(BF16)

    def heads(step, carry):
        batch = [step * COARSE_BATCH + inner for inner in range(COARSE_BATCH)]
        scales = [scale_ref[head] / HEAD for head in batch]
        parts = [head_parts(head, D2, scale, qkv) for head, scale in zip(batch, scales)]
        scores = [dot(part[1], part[0], 0, 0) for part in parts]
        softs = [softmax_rows(score, keep[...]) for score in scores]
        rounds = [soft.astype(BF16) for soft in softs]
        for head, soft, part in zip(batch, rounds, parts):
            att[head_rows(0, D2, head), :] = dot(part[2], soft, 1, 0).astype(BF16)
        grads = [gatt[head_rows(0, D2, head), :] for head in batch]
        results = heads_back(grads, parts, softs, rounds, [part[3:] for part in parts], scales)
        for head, result in zip(batch, results):
            for part in range(3):
                gqkv[head_rows(part, D2, head), :] = result[part].astype(BF16)
        return carry

    lax.fori_loop(0, H2 // COARSE_BATCH, heads, 0)
    val_ref[...] = values.astype(BF16)
    for start in range(0, D2, 256):
        turned[start : start + 256, :] = dot(
            cw_ref[start : start + 256, : 3 * D2], gqkv[...], 1, 0
        )
    scaled = turned[...].T * gain_ref[...]
    grad_in = cot_rows[...] + norm_back(scaled, value_norm, value_inverse)
    grad_in = grad_in.astype(BF16)
    for part in range(4):
        cols = slice(part * D1, part * D1 + D1)
        mnorm[:, cols] = dot(grad_in, mw_ref[cols, :], 1, 1) * mgain_ref[:, cols]
    for start in range(0, TOK, 72):
        mnorm[start : start + 72, :] = norm_back(
            mnorm[start : start + 72, :], merged[start : start + 72, :], minv[start : start + 72, 0:1]
        )
    for group in range(18):
        for part in range(4):
            target = (2 * (group // LEV) + part % 2) * LEV + group % LEV
            for cut in range(4):
                cells[cut, target, pl.ds(part // 2, WIN, stride=2), :] = mnorm[
                    WIN * group : WIN * group + WIN,
                    part * D1 + cut * 128 : part * D1 + cut * 128 + 128,
                ]
    done = jnp.concatenate([cells[cut] for cut in range(4)], -1)
    g_ref[...] = done.reshape(ROWS, D1).astype(BF16)
    glat_ref[...] = done[GROUPS - EDGE :].reshape(EDGE * LON, D1).astype(BF16)
    for group in range(GROUPS):
        rows = done[group, 18:24]
        if group < GROUPS - EDGE:
            lon_rows[6 * group : 6 * group + 6, :] = rows
        else:
            at = 6 * (group + EDGE - GROUPS)
            corner_rows[at : at + 6, :] = rows
    glon_ref[...] = lon_rows[...].astype(BF16)
    gcor_ref[...] = corner_rows[...].astype(BF16)


def coarse_out_kernel(att_ref, val_ref, cw_ref, out_ref):
    result = val_ref[...].astype(F32) + dot(att_ref[...], cw_ref[:, 3 * D2 :], 0, 0)
    for group in range(18):
        out_ref[group] = result[WIN * group : WIN * group + WIN].astype(BF16)


def normed_kernel(xw0_ref, xw1_ref, gain_ref, normt0_ref, normt1_ref):
    for xw_ref, normt_ref in ((xw0_ref, normt0_ref), (xw1_ref, normt1_ref)):
        normt_ref[...] = jnp.zeros_like(normt_ref)
        for win in range(2):
            normed = (normalize(xw_ref[win].astype(F32))[0] * gain_ref[...]).astype(BF16)
            normt_ref[win, :, 0:TOK] = normed.T


def fine_backward_kernel(side, *refs):
    if side == 1:
        (g_ref, lat_ref, cot_ref, clat_ref, clon_ref, ccor_ref,
         qkv_ref, inv_ref, soft_ref, att_ref, w_ref, scale_ref, gq_ref, e_ref, wins, gatt) = refs
        lon_cot = clon_ref[...].astype(F32)
        corner_cot = ccor_ref[...].astype(F32)
    else:
        (g_ref, lat_ref, lon_ref, corner_ref, cot_ref, clat_ref, qkv_ref, inv_ref, soft_ref, att_ref, w_ref,
         scale_ref, core_ref, gq1_ref, e1_ref, att1_ref, normt_ref, normt1_ref,
         gq_ref, e_ref, keep_ref, send_ref, wins, gatt) = refs
        lon_in = lon_ref[...].astype(F32)
        corner_in = corner_ref[...].astype(F32)
    tile = g_ref[...].astype(F32).reshape(GROUPS, LON, D1)
    lat_rows = lat_ref[...].astype(F32).reshape(EDGE, LON, D1)
    cot_tile = cot_ref[...].astype(F32).reshape(GROUPS, LON, D1)
    cot_lat = clat_ref[...].astype(F32).reshape(EDGE, LON, D1)
    for group in range(GROUPS):
        source = lat_rows[group] if group < EDGE else tile[group - EDGE]
        win, row = group // 18, WIN * (group % 18)
        inside = group + EDGE < GROUPS
        cot = cot_tile[group + EDGE] if inside else cot_lat[group + EDGE - GROUPS]
        if side == 1:
            at = 6 * group if inside else 6 * (group + EDGE - GROUPS)
            halo = lon_cot[at : at + 6] if inside else corner_cot[at : at + 6]
            wins[win, row : row + 6, :] = source[6:12] + cot[18:24]
            wins[win, row + 6 : row + WIN, :] = source[12:18] + halo
        else:
            if group < EDGE:
                halo = corner_in[6 * group : 6 * group + 6]
            else:
                halo = lon_in[6 * (group - EDGE) : 6 * (group - EDGE) + 6]
            wins[win, row : row + 6, :] = halo + cot[6:12]
            wins[win, row + 6 : row + WIN, :] = source[0:6] + cot[12:18]
    gq_ref[...] = jnp.zeros_like(gq_ref)

    def window(win, carry):
        cot = wins[win].astype(BF16)
        e_ref[win] = cot
        gatt[...] = dot(w_ref[:, 3 * D1 :], cot, 1, 1).astype(BF16)
        for start in range(0, H1, BACK_BATCH):
            batch = range(start, start + BACK_BATCH)
            rounds = [soft_ref[win, head] for head in batch]
            results = heads_back(
                [gatt[head_rows(0, D1, head), :] for head in batch],
                [[qkv_ref[win, head_rows(part, D1, head), :] for part in range(3)] for head in batch],
                [soft.astype(F32) for soft in rounds],
                rounds,
                [(inv_ref[win, head : head + 1, :], inv_ref[win, H1 + head : H1 + head + 1, :]) for head in batch],
                [scale_ref[head] / HEAD for head in batch],
            )
            for head, result in zip(batch, results):
                for part in range(3):
                    gq_ref[win, head_rows(part, D1, head), 0:TOK] = result[part].astype(BF16)
        return carry

    lax.fori_loop(0, 2, window, 0)
    if side == 0:
        sums = []
        for part in range(3):
            cols = slice(part * D1, part * D1 + D1)
            total = dot(normt_ref[0], gq_ref[0, cols, :], 1, 1) + dot(normt_ref[1], gq_ref[1, cols, :], 1, 1)
            total += dot(normt1_ref[0], gq1_ref[0, cols, :], 1, 1)
            sums.append(total + dot(normt1_ref[1], gq1_ref[1, cols, :], 1, 1))
        total = dot(att_ref[0], e_ref[0], 1, 0) + dot(att_ref[1], e_ref[1], 1, 0)
        sums.append(total + dot(att1_ref[0], e1_ref[0], 1, 0) + dot(att1_ref[1], e1_ref[1], 1, 0))
        for part in range(2):
            cols = slice(part * D1, part * D1 + D1)
            first = core_ref[0] == 0
            keep_ref[:, cols] = jnp.where(first, sums[part], sums[2 + part]).astype(BF16)
            send_ref[:, cols] = jnp.where(first, sums[2 + part], sums[part]).astype(BF16)


def fine_input_kernel(
    gq0_ref, gq1_ref, e0_ref, e1_ref, xw0_ref, xw1_ref, w_ref, gain_ref,
    g0_ref, g1_ref, glat_ref, glon_ref, gcor_ref, lat_rows, lon_rows, corner_rows,
):
    for side, (gq_ref, e_ref, xw_ref, g_ref) in enumerate(
        ((gq0_ref, e0_ref, xw0_ref, g0_ref), (gq1_ref, e1_ref, xw1_ref, g1_ref))
    ):
        for win in range(2):
            turned = dot(w_ref[:, : 3 * D1], gq_ref[win], 1, 0)
            scaled = turned.T[:TOK] * gain_ref[...]
            normed, inverse = normalize(xw_ref[win].astype(F32))
            grad_in = e_ref[win].astype(F32) + norm_back(scaled, normed, inverse)
            g_ref[win] = grad_in.astype(BF16)
            if win == 1:
                lat_rows[108 * side : 108 * side + 108, :] = grad_in[108:TOK]
            if side == 1:
                for group in range(18):
                    rows = grad_in[WIN * group + 6 : WIN * group + WIN]
                    at = 6 * (group + 18 * win)
                    if at < 162:
                        lon_rows[at : at + 6, :] = rows
                    else:
                        corner_rows[at - 162 : at - 156, :] = rows
    glat_ref[...] = lat_rows[...].astype(BF16)
    glon_ref[...] = lon_rows[...].astype(BF16)
    gcor_ref[...] = corner_rows[...].astype(BF16)


def assemble_kernel(g0_ref, g1_ref, lat_ref, lon_ref, corner_ref, out_ref, full):
    first = [g0_ref[win].astype(F32) for win in range(2)]
    second = [g1_ref[win].astype(F32) for win in range(2)]
    lat_rows = lat_ref[...].astype(F32)
    lon_rows = lon_ref[...].astype(F32)
    corner_rows = corner_ref[...].astype(F32)
    for group in range(GROUPS):
        if group < EDGE:
            full[group, 0:6, :] = corner_rows[6 * group : 6 * group + 6]
            full[group, 6:18, :] = lat_rows[WIN * group : WIN * group + WIN]
            full[group, 18:24, :] = lat_rows[108 + WIN * group : 108 + WIN * group + 6]
        else:
            own = group - EDGE
            win, row = own // 18, WIN * (own % 18)
            full[group, 0:6, :] = lon_rows[6 * own : 6 * own + 6]
            full[group, 6:18, :] = first[win][row : row + WIN]
            full[group, 18:24, :] = second[win][row : row + 6]
    out_ref[...] = full[...].reshape(ROWS, D1).astype(BF16)


def call(kernel, outs, scratch, smem_from, args, name, flops, vmem):
    whole = pl.BlockSpec(memory_space=pltpu.VMEM)
    scalars = pl.BlockSpec(memory_space=pltpu.SMEM)
    return pl.pallas_call(
        kernel,
        out_shape=[jax.ShapeDtypeStruct(shape, kind) for shape, kind in outs],
        in_specs=[scalars if position in smem_from else whole for position in range(len(args))],
        out_specs=[whole] * len(outs),
        scratch_shapes=[pltpu.VMEM(shape, kind) for shape, kind in scratch],
        compiler_params=pltpu.CompilerParams(vmem_limit_bytes=vmem * MIB),
        cost_estimate=pl.CostEstimate(flops=flops, bytes_accessed=1 << 22, transcendentals=0),
        name=name,
    )(*args)


HALF = ((2, TOK, D1), BF16)
LAT_BLOCK = ((EDGE * LON, D1), BF16)
LON_BLOCK = ((162, D1), BF16)
CORNER = ((54, D1), BF16)
LON_ROWS = ((162, D1), F32)
CORNER_ROWS = ((54, D1), F32)


def edges(tile):
    return call(edges_kernel, [LAT_BLOCK, LON_BLOCK, CORNER], [LON_ROWS, CORNER_ROWS], (), (tile,), "edges", 2 * 10**9, 6)


def turn(weights):
    return call(turn_kernel, [((3 * D1, D1), BF16)], [], (), (weights,), "turn", 10**9, 6)[0]


def fine_forward(side, ins, weights, scalars):
    outs = [HALF] + ([((112, D1), BF16), LON_BLOCK, CORNER] if side == 0 else [((224, D1), BF16)])
    outs += [
        HALF,
        ((2, 3 * D1, TOK), BF16),
        ((2, 2 * H1, TOK), F32),
        ((2, H1, TOK, TOK), BF16),
        ((2, D1, TOK), BF16),
    ]
    scratch = [((2, TOK, D1), F32), ((3 * D1, TOK), F32), ((TOK, TOK), F32)]
    if side == 0:
        scratch += [LON_ROWS, CORNER_ROWS]
    args = (*ins, *weights, *scalars)
    smem = (len(args) - 2, len(args) - 1)
    kernel = functools.partial(fine_forward_kernel, side)
    out = call(kernel, outs, scratch, smem, args, "fine_forward_" + str(side), 10**10, 10)
    return out[:-5], out[-5:]


def coarse_both(ins, cot_coarse, mgain, mw, cw, gain, scales, last):
    outs = [((D2, TOK), BF16), ((TOK, D2), BF16), ((ROWS, D1), BF16), LAT_BLOCK, LON_BLOCK, CORNER]
    scratch = [
        ((4, 2 * TOK + 112, 128), F32),
        ((4, 2 * TOK + 112, 128), F32),
        ((4, TOK, 128), F32),
        ((4, GROUPS, LON, 128), F32),
        ((TOK, 4 * D1), F32),
        ((TOK, 4 * D1), F32),
        ((TOK, 128), F32),
        ((3 * D2, TOK), F32),
        ((3 * D2, TOK), BF16),
        ((D2, TOK), BF16),
        ((D2, TOK), F32),
        ((TOK, TOK), F32),
        LON_ROWS,
        CORNER_ROWS,
        ((TOK, D2), F32),
    ]
    args = (*ins, cot_coarse, mgain, mw, cw, gain, scales, last)
    return call(coarse_kernel, outs, scratch, (10, 11), args, "coarse_both", 2 * 10**10, 22)


def coarse_result(att, values, weights):
    return call(
        coarse_out_kernel, [((18, WIN, D2), BF16)], [], (), (att, values, weights), "coarse_out", 10**9, 16
    )[0]


def normed_turned(xw0, xw1, gain):
    outs = [((2, D1, 256), BF16)] * 2
    return call(normed_kernel, outs, [], (), (xw0, xw1, gain), "normed", 10**9, 8)


def fine_backward(side, ins, saved, weights, scales, core=(), other=()):
    outs = [((2, 3 * D1, 256), BF16), HALF]
    scratch = [((2, TOK, D1), F32), ((D1, TOK), BF16)]
    if side == 0:
        outs += [((D1, 2 * D1), BF16)] * 2
    args = (*ins, *saved, weights, scales, *core, *other)
    scalars = len(args) - len(other) - len(core) - 1
    smem = tuple(range(scalars, scalars + 1 + len(core)))
    kernel = functools.partial(fine_backward_kernel, side)
    return call(kernel, outs, scratch, smem, args, "fine_backward_" + str(side), 10**10, 14)


def fine_input(args):
    outs = [HALF, HALF, LAT_BLOCK, LON_BLOCK, CORNER]
    scratch = [((EDGE * LON, D1), F32), LON_ROWS, CORNER_ROWS]
    return call(fine_input_kernel, outs, scratch, (), args, "fine_input", 6 * 10**9, 8)


def assemble(args):
    scratch = [((GROUPS, LON, D1), F32)]
    return call(assemble_kernel, [((ROWS, D1), BF16)], scratch, (), args, "assemble", 2 * 10**9, 6)[0]


def ring(axis_size, step):
    return [(i, (i + step) % axis_size) for i in range(axis_size)]


def moved(block, axis, step):
    return lax.ppermute(block, axis, ring(lax.axis_size(axis), step))


def moved_both(block, step):
    nlon, nlat = lax.axis_size("lon"), lax.axis_size(LAT_AXES)
    route = [
        (i * nlat + j, ((i + step) % nlon) * nlat + (j + step) % nlat)
        for i in range(nlon)
        for j in range(nlat)
    ]
    return lax.ppermute(block, ("lon", *LAT_AXES), route)


def half_moved(tile, axis, dim, step):
    near, far = jnp.split(tile, 2, dim)
    if step < 0:
        return jnp.concatenate([far, moved(near, axis, step)], dim)
    return jnp.concatenate([moved(far, axis, step), near], dim)


def after(value, *others):
    return lax.optimization_barrier((value, *others))[0]


def chip_sum(part):
    pieces = lax.all_to_all(part.reshape(64, 8, 2 * D1), ("lon", "chip"), 0, 0)
    return jnp.sum(pieces.astype(F32), 0)


def own_rows(total, core):
    first = core == 0
    mine = jnp.where(first, total[:4], total[4:])
    other = lax.ppermute(jnp.where(first, total[4:], total[:4]), "core", [(0, 1), (1, 0)])
    return jnp.concatenate([jnp.where(first, mine, other), jnp.where(first, other, mine)], 1)


def on_device(
    grid_field, fine_weights, fine_gain, fine_scales, merge_gain, merge_weight, coarse_weights, coarse_gain,
    coarse_scales, cot_fine, cot_coarse,
):
    core = lax.axis_index("core").astype(jnp.int32).reshape(1)
    last = (lax.axis_index(LAT_AXES) == lax.axis_size(LAT_AXES) - 1).astype(jnp.int32).reshape(1)
    fine_gain = fine_gain.reshape(1, -1)
    tile = grid_field.transpose(1, 2, 0, 3).reshape(ROWS, D1)
    lat, lon, corner = edges(tile)
    lat, lon, corner = moved(lat, LAT_AXES, -1), moved(lon, "lon", -1), moved_both(corner, -1)
    cot_coarse = after(cot_coarse, lat).transpose(1, 2, 0, 3)
    cot_coarse = half_moved(cot_coarse, "lon", 2, -1)
    weights = (turn(fine_weights), fine_weights, fine_gain)
    scalars = (fine_scales, last)
    (y0, ylat, ylon, ycor), saved0 = fine_forward(0, (tile, lat), weights, scalars)
    ylon, ycor = moved(ylon, "lon", -1), moved_both(ycor, -1)
    cot_coarse = half_moved(after(cot_coarse, y0), LAT_AXES, 0, -1).reshape(18, WIN, D2)
    (y1, ylat), saved1 = fine_forward(1, (tile, lat, lon, corner, ylat), weights, scalars)
    ylat, ylon, ycor, cot_coarse = lax.optimization_barrier((ylat, ylon, ycor, cot_coarse))
    ylat = moved(ylat, LAT_AXES, -1)
    cot_tile = after(cot_fine, y1).transpose(1, 2, 0, 3).reshape(ROWS, D1)
    cot_edges = edges(cot_tile)
    cot_edges = (moved(cot_edges[0], LAT_AXES, -1), moved(cot_edges[1], "lon", -1), moved_both(cot_edges[2], -1))
    att, values, grad, glat, glon, gcor = coarse_both(
        (y0, y1, ylat, ylon, ycor), cot_coarse, merge_gain.reshape(1, -1), merge_weight,
        coarse_weights, coarse_gain.reshape(1, -1), coarse_scales, last,
    )
    (glat, glon, gcor), cot_edges = lax.optimization_barrier(((glat, glon, gcor), cot_edges))
    glat, glon, gcor = moved(glat, LAT_AXES, 1), moved(glon, "lon", 1), moved_both(gcor, 1)
    coarse_out = coarse_result(att, values, coarse_weights)
    normt0, normt1 = normed_turned(saved0[0], saved1[0], after(fine_gain, att))
    coarse_out, glat, normt0, normt1 = lax.optimization_barrier((coarse_out, glat, normt0, normt1))
    coarse_out = half_moved(coarse_out.reshape(LAT // 2, LEV, LON // 2, D2), "lon", 2, 1)
    gq1, e1 = fine_backward(1, (grad, glat, cot_tile, *cot_edges), saved1[1:], fine_weights, fine_scales)
    own, other = jnp.split(coarse_out, 2, 0)
    other = moved(other, LAT_AXES, 1)
    gq0, e0, keep, send = fine_backward(
        0, (grad, glat, glon, gcor, cot_tile, cot_edges[0]), saved0[1:], fine_weights, fine_scales,
        (core,), (gq1, e1, saved1[4], normt0, normt1),
    )
    sent = lax.ppermute(send, "core", [(0, 1), (1, 0)])
    g0, g1, lat, lon, corner = fine_input(
        (gq0, gq1, e0, e1, saved0[0], saved1[0], fine_weights, fine_gain)
    )
    lat, lon, corner = moved(lat, LAT_AXES, 1), moved(lon, "lon", 1), moved_both(corner, 1)
    sent, keep, g0 = lax.optimization_barrier((sent, keep, g0))
    part = (keep.astype(F32) + sent.astype(F32)).astype(BF16)
    total = chip_sum(part)
    share = own_rows(total, core[0])
    lat, lon, corner, other = (after(block, total) for block in (lat, lon, corner, other))
    grad_input = assemble((g0, g1, lat, lon, corner)).reshape(LAT, LEV, LON, D1)
    coarse_out = jnp.concatenate([other, own], 0)
    return coarse_out.transpose(2, 0, 1, 3), grad_input.transpose(2, 0, 1, 3), share


def solution(mesh):
    split = Mesh(mesh.devices.reshape(mesh.devices.shape[0], -1, 2), ("lon", *LAT_AXES))
    tile = P("lon", LAT_AXES, None, None)
    in_specs = (tile,) + (P(),) * 8 + (tile, tile)
    out_specs = (tile, tile, P(("lon", *LAT_AXES), None))
    return jax.shard_map(
        on_device, mesh=split, in_specs=in_specs, out_specs=out_specs, check_vma=False
    )
```

```python
import functools

import jax
import jax.numpy as jnp
from jax import lax
from jax.experimental import pallas as pl
from jax.experimental.pallas import tpu as pltpu
from jax.sharding import Mesh, PartitionSpec as P

LAT_AXES = ("chip", "core")
F32 = jnp.float32
BF16 = jnp.bfloat16
EPS_NORM = 1e-05
EPS_HEAD = 1e-06
D1, D2, H1, H2 = 512, 1024, 8, 16
HEAD = 64
TOK = 216
LON, LAT, LEV = 24, 12, 3
GROUPS = LAT * LEV
EDGE = 9
ROWS = GROUPS * LON
WIN = 12
FINE_BATCH, COARSE_BATCH, BACK_BATCH = 8, 4, 8
MIB = 1024 * 1024


def dot(left, right, left_dim, right_dim):
    return lax.dot_general(
        left, right, (((left_dim,), (right_dim,)), ((), ())), preferred_element_type=F32
    )


def mean_last(values):
    return jnp.mean(values, -1, keepdims=True)


def normalize(values):
    center = values - mean_last(values)
    inverse = lax.rsqrt(mean_last(center * center) + EPS_NORM)
    return center * inverse, inverse


def norm_back(scaled, normed, inverse):
    return inverse * (scaled - mean_last(scaled) - normed * mean_last(scaled * normed))


def keep_matrix(last_ref):
    half = TOK // 2
    keys = lax.broadcasted_iota(jnp.int32, (TOK, TOK), 0) >= half
    queries = lax.broadcasted_iota(jnp.int32, (TOK, TOK), 1) >= half
    apart = jnp.where(keys == queries, 0.0, 1.0)
    return 1.0 - apart * last_ref[0].astype(F32)


def unit_rows(values):
    inverse = lax.rsqrt(jnp.mean(values * values, 0, keepdims=True) + EPS_HEAD)
    return values * inverse, inverse


def softmax_rows(scores, keep):
    raw = jnp.exp(scores) * keep
    return raw * (1.0 / jnp.sum(raw, 0, keepdims=True))


def heads_back(grads, parts, softs, rounds, inverses, scales):
    grad_probs = [dot(part[2], grad, 0, 0) for part, grad in zip(parts, grads)]
    grad_values = [dot(grad, soft, 1, 1) for grad, soft in zip(grads, rounds)]
    grad_scores = [
        (soft * (probs - jnp.sum(probs * soft, 0, keepdims=True))).astype(BF16)
        for probs, soft in zip(grad_probs, softs)
    ]
    grad_q = [dot(part[1], scores, 1, 0) for part, scores in zip(parts, grad_scores)]
    grad_k = [dot(part[0], scores, 1, 1) for part, scores in zip(parts, grad_scores)]
    results = []
    for index, part in enumerate(parts):
        scale, (q_inverse, k_inverse) = scales[index], inverses[index]
        q_wide, k_wide = part[0].astype(F32), part[1].astype(F32)
        q_mean = jnp.mean(grad_q[index] * q_wide, 0, keepdims=True)
        k_mean = jnp.mean(grad_k[index] * k_wide, 0, keepdims=True)
        results.append((
            q_inverse * (grad_q[index] * scale - q_wide * (q_mean * (1.0 / scale))),
            k_inverse * (grad_k[index] - k_wide * k_mean),
            grad_values[index],
        ))
    return results


def head_rows(part, width, head):
    if isinstance(head, int):
        return slice(part * width + head * HEAD, part * width + head * HEAD + HEAD)
    return pl.ds(pl.multiple_of(part * width + head * HEAD, HEAD), HEAD)


def head_parts(head, width, scale, qkv):
    q_unit, q_inverse = unit_rows(qkv[head_rows(0, width, head), :])
    k_unit, k_inverse = unit_rows(qkv[head_rows(1, width, head), :])
    v_round = qkv[head_rows(2, width, head), :].astype(BF16)
    return (q_unit * scale).astype(BF16), k_unit.astype(BF16), v_round, q_inverse, k_inverse


def edges_kernel(x_ref, lat_ref, lon_ref, corner_ref, lon_rows, corner_rows):
    tile = x_ref[...].astype(F32).reshape(GROUPS, LON, D1)
    lat_ref[...] = tile[:EDGE].reshape(EDGE * LON, D1).astype(BF16)
    for group in range(GROUPS):
        rows = tile[group, 0:6]
        if group < EDGE:
            corner_rows[6 * group : 6 * group + 6, :] = rows
        else:
            lon_rows[6 * (group - EDGE) : 6 * (group - EDGE) + 6, :] = rows
    lon_ref[...] = lon_rows[...].astype(BF16)
    corner_ref[...] = corner_rows[...].astype(BF16)


def turn_kernel(w_ref, wt_ref):
    for part in range(3):
        cols = slice(part * D1, part * D1 + D1)
        wt_ref[cols, :] = w_ref[:, cols].T


def fine_forward_kernel(side, *refs):
    if side == 0:
        (x_ref, lat_ref, wt_ref, w_ref, gain_ref, scale_ref, last_ref,
         y_ref, ylat_ref, ylon_ref, ycor_ref, xw_ref, qkv_ref, inv_ref, soft_ref, att_ref,
         wins, qkv, keep, lon_rows, corner_rows) = refs
    else:
        (x_ref, lat_ref, lon_ref, corner_ref, first_ref, wt_ref, w_ref, gain_ref, scale_ref, last_ref,
         y_ref, ylat_ref, xw_ref, qkv_ref, inv_ref, soft_ref, att_ref, wins, qkv, keep) = refs
    tile = x_ref[...].astype(F32).reshape(GROUPS, LON, D1)
    lat_rows = lat_ref[...].astype(F32).reshape(EDGE, LON, D1)
    if side == 1:
        lon_in = lon_ref[...].astype(F32)
        corner_in = corner_ref[...].astype(F32)
    for group in range(GROUPS):
        source = tile[group + EDGE] if group + EDGE < GROUPS else lat_rows[group + EDGE - GROUPS]
        win, row = group // 18, WIN * (group % 18)
        if side == 0:
            wins[win, row : row + WIN, :] = source[6:18]
        else:
            wins[win, row : row + 6, :] = source[18:24]
            if group + EDGE < GROUPS:
                halo = lon_in[6 * group : 6 * group + 6]
            else:
                halo = corner_in[6 * (group + EDGE - GROUPS) : 6 * (group + EDGE - GROUPS) + 6]
            wins[win, row + 6 : row + WIN, :] = halo
    keep[...] = keep_matrix(last_ref)

    def window(win, carry):
        values = wins[win]
        xw_ref[win] = values.astype(BF16)
        normed = (normalize(values)[0] * gain_ref[...]).astype(BF16)
        for part in range(3):
            qkv[part * D1 : part * D1 + D1, :] = dot(
                wt_ref[part * D1 : part * D1 + D1, :], normed, 1, 1
            )
        use_keep = jnp.where(win >= 1, keep[...], 1.0)
        for start in range(0, H1, FINE_BATCH):
            batch = range(start, start + FINE_BATCH)
            parts = []
            for head in batch:
                q_scaled, k_round, v_round, q_inverse, k_inverse = head_parts(
                    head, D1, scale_ref[head] / HEAD, qkv
                )
                qkv_ref[win, head_rows(0, D1, head), :] = q_scaled
                qkv_ref[win, head_rows(1, D1, head), :] = k_round
                qkv_ref[win, head_rows(2, D1, head), :] = v_round
                inv_ref[win, head : head + 1, :] = q_inverse
                inv_ref[win, H1 + head : H1 + head + 1, :] = k_inverse
                parts.append((q_scaled, k_round, v_round))
            scores = [dot(k_round, q_scaled, 0, 0) for q_scaled, k_round, _ in parts]
            softs = [softmax_rows(score, use_keep).astype(BF16) for score in scores]
            for head, soft, part in zip(batch, softs, parts):
                soft_ref[win, head] = soft
                att_ref[win, head_rows(0, D1, head), :] = dot(part[2], soft, 1, 0).astype(BF16)
        result = values + dot(att_ref[win], w_ref[:, 3 * D1 :], 0, 0)
        wins[win] = result
        y_ref[win] = result.astype(BF16)
        return carry

    lax.fori_loop(0, 2, window, 0)
    if side == 0:
        ylat_ref[...] = wins[0, 0:112, :].astype(BF16)
        for group in range(GROUPS):
            rows = wins[group // 18, WIN * (group % 18) : WIN * (group % 18) + 6, :]
            if group < EDGE:
                corner_rows[6 * group : 6 * group + 6, :] = rows
            else:
                lon_rows[6 * (group - EDGE) : 6 * (group - EDGE) + 6, :] = rows
        ylon_ref[...] = lon_rows[...].astype(BF16)
        ycor_ref[...] = corner_rows[...].astype(BF16)
    else:
        ylat_ref[0:112, :] = first_ref[...]
        ylat_ref[112:224, :] = wins[0, 0:112, :].astype(BF16)


def coarse_kernel(
    y0_ref, y1_ref, lat_ref, lon_ref, corner_ref, cotc_ref, mgain_ref, mw_ref, cw_ref, gain_ref,
    scale_ref, last_ref,
    att, val_ref, g_ref, glat_ref, glon_ref, gcor_ref,
    near, far, halo, cells, merged, mnorm, minv, qkv, gqkv, gatt, turned, keep, lon_rows, corner_rows, cot_rows,
):
    for group in range(18):
        cot_rows[WIN * group : WIN * group + WIN, :] = cotc_ref[group].astype(F32)
    cot = cot_rows[...].astype(BF16)
    for cut in range(4):
        lanes = slice(cut * 128, cut * 128 + 128)
        for win in range(2):
            near[cut, TOK * win : TOK * win + TOK, :] = y0_ref[win, :, lanes].astype(F32)
            far[cut, TOK * win : TOK * win + TOK, :] = y1_ref[win, :, lanes].astype(F32)
        near[cut, 2 * TOK :, :] = lat_ref[0:112, lanes].astype(F32)
        far[cut, 2 * TOK :, :] = lat_ref[112:224, lanes].astype(F32)
        halo[cut, 0:162, :] = lon_ref[:, lanes].astype(F32)
        halo[cut, 162:TOK, :] = corner_ref[:, lanes].astype(F32)
    for group in range(18):
        for part in range(4):
            cell = (2 * (group // LEV) + part % 2) * LEV + group % LEV
            source, odd, row = WIN * (cell + EDGE), part // 2, WIN * group
            for cut in range(4):
                lanes = slice(part * D1 + cut * 128, part * D1 + cut * 128 + 128)
                merged[row : row + 3, lanes] = near[cut, pl.ds(source + 6 + odd, 3, stride=2), :]
                merged[row + 3 : row + 9, lanes] = far[cut, pl.ds(source + odd, 6, stride=2), :]
                merged[row + 9 : row + WIN, lanes] = halo[cut, pl.ds(6 * cell + odd, 3, stride=2), :]
    for start in range(0, TOK, 72):
        normed, inverse = normalize(merged[start : start + 72, :])
        merged[start : start + 72, :] = normed
        minv[start : start + 72, :] = jnp.broadcast_to(inverse, (72, 128))
        mnorm[start : start + 72, :] = normed * mgain_ref[...]
    keep[...] = keep_matrix(last_ref)
    values = dot(mnorm[...].astype(BF16), mw_ref[...], 1, 0).astype(BF16).astype(F32)
    value_norm, value_inverse = normalize(values)
    normed = (value_norm * gain_ref[...]).astype(BF16)
    for start in range(0, 3 * D2, 512):
        qkv[start : start + 512, :] = dot(normed, cw_ref[:, start : start + 512], 1, 0).T
    for start in range(0, D2, 512):
        gatt[start : start + 512, :] = dot(
            cw_ref[start : start + 512, 3 * D2 :], cot, 1, 1
        ).astype(BF16)

    def heads(step, carry):
        batch = [step * COARSE_BATCH + inner for inner in range(COARSE_BATCH)]
        scales = [scale_ref[head] / HEAD for head in batch]
        parts = [head_parts(head, D2, scale, qkv) for head, scale in zip(batch, scales)]
        scores = [dot(part[1], part[0], 0, 0) for part in parts]
        softs = [softmax_rows(score, keep[...]) for score in scores]
        rounds = [soft.astype(BF16) for soft in softs]
        for head, soft, part in zip(batch, rounds, parts):
            att[head_rows(0, D2, head), :] = dot(part[2], soft, 1, 0).astype(BF16)
        grads = [gatt[head_rows(0, D2, head), :] for head in batch]
        results = heads_back(grads, parts, softs, rounds, [part[3:] for part in parts], scales)
        for head, result in zip(batch, results):
            for part in range(3):
                gqkv[head_rows(part, D2, head), :] = result[part].astype(BF16)
        return carry

    lax.fori_loop(0, H2 // COARSE_BATCH, heads, 0)
    val_ref[...] = values.astype(BF16)
    for start in range(0, D2, 256):
        turned[start : start + 256, :] = dot(
            cw_ref[start : start + 256, : 3 * D2], gqkv[...], 1, 0
        )
    scaled = turned[...].T * gain_ref[...]
    grad_in = cot_rows[...] + norm_back(scaled, value_norm, value_inverse)
    grad_in = grad_in.astype(BF16)
    for part in range(4):
        cols = slice(part * D1, part * D1 + D1)
        mnorm[:, cols] = dot(grad_in, mw_ref[cols, :], 1, 1) * mgain_ref[:, cols]
    for start in range(0, TOK, 72):
        mnorm[start : start + 72, :] = norm_back(
            mnorm[start : start + 72, :], merged[start : start + 72, :], minv[start : start + 72, 0:1]
        )
    for group in range(18):
        for part in range(4):
            target = (2 * (group // LEV) + part % 2) * LEV + group % LEV
            for cut in range(4):
                cells[cut, target, pl.ds(part // 2, WIN, stride=2), :] = mnorm[
                    WIN * group : WIN * group + WIN,
                    part * D1 + cut * 128 : part * D1 + cut * 128 + 128,
                ]
    done = jnp.concatenate([cells[cut] for cut in range(4)], -1)
    g_ref[...] = done.reshape(ROWS, D1).astype(BF16)
    glat_ref[...] = done[GROUPS - EDGE :].reshape(EDGE * LON, D1).astype(BF16)
    for group in range(GROUPS):
        rows = done[group, 18:24]
        if group < GROUPS - EDGE:
            lon_rows[6 * group : 6 * group + 6, :] = rows
        else:
            at = 6 * (group + EDGE - GROUPS)
            corner_rows[at : at + 6, :] = rows
    glon_ref[...] = lon_rows[...].astype(BF16)
    gcor_ref[...] = corner_rows[...].astype(BF16)


def coarse_out_kernel(att_ref, val_ref, cw_ref, out_ref):
    result = val_ref[...].astype(F32) + dot(att_ref[...], cw_ref[:, 3 * D2 :], 0, 0)
    for group in range(18):
        out_ref[group] = result[WIN * group : WIN * group + WIN].astype(BF16)


def normed_kernel(xw0_ref, xw1_ref, gain_ref, normt0_ref, normt1_ref):
    for xw_ref, normt_ref in ((xw0_ref, normt0_ref), (xw1_ref, normt1_ref)):
        normt_ref[...] = jnp.zeros_like(normt_ref)
        for win in range(2):
            normed = (normalize(xw_ref[win].astype(F32))[0] * gain_ref[...]).astype(BF16)
            normt_ref[win, :, 0:TOK] = normed.T


def fine_backward_kernel(side, *refs):
    if side == 1:
        (g_ref, lat_ref, cot_ref, clat_ref, clon_ref, ccor_ref,
         qkv_ref, inv_ref, soft_ref, att_ref, w_ref, scale_ref, gq_ref, e_ref, wins, gatt) = refs
        lon_cot = clon_ref[...].astype(F32)
        corner_cot = ccor_ref[...].astype(F32)
    else:
        (g_ref, lat_ref, lon_ref, corner_ref, cot_ref, clat_ref, qkv_ref, inv_ref, soft_ref, att_ref, w_ref,
         scale_ref, core_ref, gq1_ref, e1_ref, att1_ref, normt_ref, normt1_ref,
         gq_ref, e_ref, keep_ref, send_ref, wins, gatt) = refs
        lon_in = lon_ref[...].astype(F32)
        corner_in = corner_ref[...].astype(F32)
    tile = g_ref[...].astype(F32).reshape(GROUPS, LON, D1)
    lat_rows = lat_ref[...].astype(F32).reshape(EDGE, LON, D1)
    cot_tile = cot_ref[...].astype(F32).reshape(GROUPS, LON, D1)
    cot_lat = clat_ref[...].astype(F32).reshape(EDGE, LON, D1)
    for group in range(GROUPS):
        source = lat_rows[group] if group < EDGE else tile[group - EDGE]
        win, row = group // 18, WIN * (group % 18)
        inside = group + EDGE < GROUPS
        cot = cot_tile[group + EDGE] if inside else cot_lat[group + EDGE - GROUPS]
        if side == 1:
            at = 6 * group if inside else 6 * (group + EDGE - GROUPS)
            halo = lon_cot[at : at + 6] if inside else corner_cot[at : at + 6]
            wins[win, row : row + 6, :] = source[6:12] + cot[18:24]
            wins[win, row + 6 : row + WIN, :] = source[12:18] + halo
        else:
            if group < EDGE:
                halo = corner_in[6 * group : 6 * group + 6]
            else:
                halo = lon_in[6 * (group - EDGE) : 6 * (group - EDGE) + 6]
            wins[win, row : row + 6, :] = halo + cot[6:12]
            wins[win, row + 6 : row + WIN, :] = source[0:6] + cot[12:18]
    gq_ref[...] = jnp.zeros_like(gq_ref)

    def window(win, carry):
        cot = wins[win].astype(BF16)
        e_ref[win] = cot
        gatt[...] = dot(w_ref[:, 3 * D1 :], cot, 1, 1).astype(BF16)
        for start in range(0, H1, BACK_BATCH):
            batch = range(start, start + BACK_BATCH)
            rounds = [soft_ref[win, head] for head in batch]
            results = heads_back(
                [gatt[head_rows(0, D1, head), :] for head in batch],
                [[qkv_ref[win, head_rows(part, D1, head), :] for part in range(3)] for head in batch],
                [soft.astype(F32) for soft in rounds],
                rounds,
                [(inv_ref[win, head : head + 1, :], inv_ref[win, H1 + head : H1 + head + 1, :]) for head in batch],
                [scale_ref[head] / HEAD for head in batch],
            )
            for head, result in zip(batch, results):
                for part in range(3):
                    gq_ref[win, head_rows(part, D1, head), 0:TOK] = result[part].astype(BF16)
        return carry

    lax.fori_loop(0, 2, window, 0)
    if side == 0:
        sums = []
        for part in range(3):
            cols = slice(part * D1, part * D1 + D1)
            total = dot(normt_ref[0], gq_ref[0, cols, :], 1, 1) + dot(normt_ref[1], gq_ref[1, cols, :], 1, 1)
            total += dot(normt1_ref[0], gq1_ref[0, cols, :], 1, 1)
            sums.append(total + dot(normt1_ref[1], gq1_ref[1, cols, :], 1, 1))
        total = dot(att_ref[0], e_ref[0], 1, 0) + dot(att_ref[1], e_ref[1], 1, 0)
        sums.append(total + dot(att1_ref[0], e1_ref[0], 1, 0) + dot(att1_ref[1], e1_ref[1], 1, 0))
        for part in range(2):
            cols = slice(part * D1, part * D1 + D1)
            first = core_ref[0] == 0
            keep_ref[:, cols] = jnp.where(first, sums[part], sums[2 + part]).astype(BF16)
            send_ref[:, cols] = jnp.where(first, sums[2 + part], sums[part]).astype(BF16)


def fine_input_kernel(
    gq0_ref, gq1_ref, e0_ref, e1_ref, xw0_ref, xw1_ref, w_ref, gain_ref,
    g0_ref, g1_ref, glat_ref, glon_ref, gcor_ref, lat_rows, lon_rows, corner_rows,
):
    for side, (gq_ref, e_ref, xw_ref, g_ref) in enumerate(
        ((gq0_ref, e0_ref, xw0_ref, g0_ref), (gq1_ref, e1_ref, xw1_ref, g1_ref))
    ):
        for win in range(2):
            turned = dot(w_ref[:, : 3 * D1], gq_ref[win], 1, 0)
            scaled = turned.T[:TOK] * gain_ref[...]
            normed, inverse = normalize(xw_ref[win].astype(F32))
            grad_in = e_ref[win].astype(F32) + norm_back(scaled, normed, inverse)
            g_ref[win] = grad_in.astype(BF16)
            if win == 1:
                lat_rows[108 * side : 108 * side + 108, :] = grad_in[108:TOK]
            if side == 1:
                for group in range(18):
                    rows = grad_in[WIN * group + 6 : WIN * group + WIN]
                    at = 6 * (group + 18 * win)
                    if at < 162:
                        lon_rows[at : at + 6, :] = rows
                    else:
                        corner_rows[at - 162 : at - 156, :] = rows
    glat_ref[...] = lat_rows[...].astype(BF16)
    glon_ref[...] = lon_rows[...].astype(BF16)
    gcor_ref[...] = corner_rows[...].astype(BF16)


def assemble_kernel(g0_ref, g1_ref, lat_ref, lon_ref, corner_ref, out_ref, full):
    first = [g0_ref[win].astype(F32) for win in range(2)]
    second = [g1_ref[win].astype(F32) for win in range(2)]
    lat_rows = lat_ref[...].astype(F32)
    lon_rows = lon_ref[...].astype(F32)
    corner_rows = corner_ref[...].astype(F32)
    for group in range(GROUPS):
        if group < EDGE:
            full[group, 0:6, :] = corner_rows[6 * group : 6 * group + 6]
            full[group, 6:18, :] = lat_rows[WIN * group : WIN * group + WIN]
            full[group, 18:24, :] = lat_rows[108 + WIN * group : 108 + WIN * group + 6]
        else:
            own = group - EDGE
            win, row = own // 18, WIN * (own % 18)
            full[group, 0:6, :] = lon_rows[6 * own : 6 * own + 6]
            full[group, 6:18, :] = first[win][row : row + WIN]
            full[group, 18:24, :] = second[win][row : row + 6]
    out_ref[...] = full[...].reshape(ROWS, D1).astype(BF16)


def call(kernel, outs, scratch, smem_from, args, name, flops, vmem):
    whole = pl.BlockSpec(memory_space=pltpu.VMEM)
    scalars = pl.BlockSpec(memory_space=pltpu.SMEM)
    return pl.pallas_call(
        kernel,
        out_shape=[jax.ShapeDtypeStruct(shape, kind) for shape, kind in outs],
        in_specs=[scalars if position in smem_from else whole for position in range(len(args))],
        out_specs=[whole] * len(outs),
        scratch_shapes=[pltpu.VMEM(shape, kind) for shape, kind in scratch],
        compiler_params=pltpu.CompilerParams(vmem_limit_bytes=vmem * MIB),
        cost_estimate=pl.CostEstimate(flops=flops, bytes_accessed=1 << 22, transcendentals=0),
        name=name,
    )(*args)


HALF = ((2, TOK, D1), BF16)
LAT_BLOCK = ((EDGE * LON, D1), BF16)
LON_BLOCK = ((162, D1), BF16)
CORNER = ((54, D1), BF16)
LON_ROWS = ((162, D1), F32)
CORNER_ROWS = ((54, D1), F32)


def edges(tile):
    return call(edges_kernel, [LAT_BLOCK, LON_BLOCK, CORNER], [LON_ROWS, CORNER_ROWS], (), (tile,), "edges", 2 * 10**9, 6)


def turn(weights):
    return call(turn_kernel, [((3 * D1, D1), BF16)], [], (), (weights,), "turn", 10**9, 6)[0]


def fine_forward(side, ins, weights, scalars):
    outs = [HALF] + ([((112, D1), BF16), LON_BLOCK, CORNER] if side == 0 else [((224, D1), BF16)])
    outs += [
        HALF,
        ((2, 3 * D1, TOK), BF16),
        ((2, 2 * H1, TOK), F32),
        ((2, H1, TOK, TOK), BF16),
        ((2, D1, TOK), BF16),
    ]
    scratch = [((2, TOK, D1), F32), ((3 * D1, TOK), F32), ((TOK, TOK), F32)]
    if side == 0:
        scratch += [LON_ROWS, CORNER_ROWS]
    args = (*ins, *weights, *scalars)
    smem = (len(args) - 2, len(args) - 1)
    kernel = functools.partial(fine_forward_kernel, side)
    out = call(kernel, outs, scratch, smem, args, "fine_forward_" + str(side), 10**10, 10)
    return out[:-5], out[-5:]


def coarse_both(ins, cot_coarse, mgain, mw, cw, gain, scales, last):
    outs = [((D2, TOK), BF16), ((TOK, D2), BF16), ((ROWS, D1), BF16), LAT_BLOCK, LON_BLOCK, CORNER]
    scratch = [
        ((4, 2 * TOK + 112, 128), F32),
        ((4, 2 * TOK + 112, 128), F32),
        ((4, TOK, 128), F32),
        ((4, GROUPS, LON, 128), F32),
        ((TOK, 4 * D1), F32),
        ((TOK, 4 * D1), F32),
        ((TOK, 128), F32),
        ((3 * D2, TOK), F32),
        ((3 * D2, TOK), BF16),
        ((D2, TOK), BF16),
        ((D2, TOK), F32),
        ((TOK, TOK), F32),
        LON_ROWS,
        CORNER_ROWS,
        ((TOK, D2), F32),
    ]
    args = (*ins, cot_coarse, mgain, mw, cw, gain, scales, last)
    return call(coarse_kernel, outs, scratch, (10, 11), args, "coarse_both", 2 * 10**10, 22)


def coarse_result(att, values, weights):
    return call(
        coarse_out_kernel, [((18, WIN, D2), BF16)], [], (), (att, values, weights), "coarse_out", 10**9, 16
    )[0]


def normed_turned(xw0, xw1, gain):
    outs = [((2, D1, 256), BF16)] * 2
    return call(normed_kernel, outs, [], (), (xw0, xw1, gain), "normed", 10**9, 8)


def fine_backward(side, ins, saved, weights, scales, core=(), other=()):
    outs = [((2, 3 * D1, 256), BF16), HALF]
    scratch = [((2, TOK, D1), F32), ((D1, TOK), BF16)]
    if side == 0:
        outs += [((D1, 2 * D1), BF16)] * 2
    args = (*ins, *saved, weights, scales, *core, *other)
    scalars = len(args) - len(other) - len(core) - 1
    smem = tuple(range(scalars, scalars + 1 + len(core)))
    kernel = functools.partial(fine_backward_kernel, side)
    return call(kernel, outs, scratch, smem, args, "fine_backward_" + str(side), 10**10, 14)


def fine_input(args):
    outs = [HALF, HALF, LAT_BLOCK, LON_BLOCK, CORNER]
    scratch = [((EDGE * LON, D1), F32), LON_ROWS, CORNER_ROWS]
    return call(fine_input_kernel, outs, scratch, (), args, "fine_input", 6 * 10**9, 8)


def assemble(args):
    scratch = [((GROUPS, LON, D1), F32)]
    return call(assemble_kernel, [((ROWS, D1), BF16)], scratch, (), args, "assemble", 2 * 10**9, 6)[0]


def ring(axis_size, step):
    return [(i, (i + step) % axis_size) for i in range(axis_size)]


def moved(block, axis, step):
    return lax.ppermute(block, axis, ring(lax.axis_size(axis), step))


def moved_both(block, step):
    nlon, nlat = lax.axis_size("lon"), lax.axis_size(LAT_AXES)
    route = [
        (i * nlat + j, ((i + step) % nlon) * nlat + (j + step) % nlat)
        for i in range(nlon)
        for j in range(nlat)
    ]
    return lax.ppermute(block, ("lon", *LAT_AXES), route)


def half_moved(tile, axis, dim, step):
    near, far = jnp.split(tile, 2, dim)
    if step < 0:
        return jnp.concatenate([far, moved(near, axis, step)], dim)
    return jnp.concatenate([moved(far, axis, step), near], dim)


def after(value, *others):
    return lax.optimization_barrier((value, *others))[0]


def chip_sum(part):
    pieces = lax.all_to_all(part.reshape(64, 8, 2 * D1), ("lon", "chip"), 0, 0)
    return jnp.sum(pieces.astype(F32), 0)


def own_rows(total, core):
    first = core == 0
    mine = jnp.where(first, total[:4], total[4:])
    other = lax.ppermute(jnp.where(first, total[4:], total[:4]), "core", [(0, 1), (1, 0)])
    return jnp.concatenate([jnp.where(first, mine, other), jnp.where(first, other, mine)], 1)


def on_device(
    grid_field, fine_weights, fine_gain, fine_scales, merge_gain, merge_weight, coarse_weights, coarse_gain,
    coarse_scales, cot_fine, cot_coarse,
):
    core = lax.axis_index("core").astype(jnp.int32).reshape(1)
    last = (lax.axis_index(LAT_AXES) == lax.axis_size(LAT_AXES) - 1).astype(jnp.int32).reshape(1)
    fine_gain = fine_gain.reshape(1, -1)
    tile = grid_field.transpose(1, 2, 0, 3).reshape(ROWS, D1)
    lat, lon, corner = edges(tile)
    lat, lon, corner = moved(lat, LAT_AXES, -1), moved(lon, "lon", -1), moved_both(corner, -1)
    cot_coarse = after(cot_coarse, lat).transpose(1, 2, 0, 3)
    cot_coarse = half_moved(cot_coarse, "lon", 2, -1)
    weights = (turn(fine_weights), fine_weights, fine_gain)
    scalars = (fine_scales, last)
    (y0, ylat, ylon, ycor), saved0 = fine_forward(0, (tile, lat), weights, scalars)
    ylon, ycor = moved(ylon, "lon", -1), moved_both(ycor, -1)
    cot_coarse = half_moved(after(cot_coarse, y0), LAT_AXES, 0, -1).reshape(18, WIN, D2)
    (y1, ylat), saved1 = fine_forward(1, (tile, lat, lon, corner, ylat), weights, scalars)
    ylat, ylon, ycor, cot_coarse = lax.optimization_barrier((ylat, ylon, ycor, cot_coarse))
    ylat = moved(ylat, LAT_AXES, -1)
    cot_tile = after(cot_fine, y1).transpose(1, 2, 0, 3).reshape(ROWS, D1)
    cot_edges = edges(cot_tile)
    cot_edges = (moved(cot_edges[0], LAT_AXES, -1), moved(cot_edges[1], "lon", -1), moved_both(cot_edges[2], -1))
    att, values, grad, glat, glon, gcor = coarse_both(
        (y0, y1, ylat, ylon, ycor), cot_coarse, merge_gain.reshape(1, -1), merge_weight,
        coarse_weights, coarse_gain.reshape(1, -1), coarse_scales, last,
    )
    (glat, glon, gcor), cot_edges = lax.optimization_barrier(((glat, glon, gcor), cot_edges))
    glat, glon, gcor = moved(glat, LAT_AXES, 1), moved(glon, "lon", 1), moved_both(gcor, 1)
    coarse_out = coarse_result(att, values, coarse_weights)
    normt0, normt1 = normed_turned(saved0[0], saved1[0], after(fine_gain, att))
    coarse_out, glat, normt0, normt1 = lax.optimization_barrier((coarse_out, glat, normt0, normt1))
    coarse_out = half_moved(coarse_out.reshape(LAT // 2, LEV, LON // 2, D2), "lon", 2, 1)
    gq1, e1 = fine_backward(1, (grad, glat, cot_tile, *cot_edges), saved1[1:], fine_weights, fine_scales)
    gq1, coarse_out = lax.optimization_barrier((gq1, coarse_out))
    own, other = jnp.split(coarse_out, 2, 0)
    other = moved(other, LAT_AXES, 1)
    gq0, e0, keep, send = fine_backward(
        0, (grad, glat, glon, gcor, cot_tile, cot_edges[0]), saved0[1:], fine_weights, fine_scales,
        (core,), (gq1, e1, saved1[4], normt0, normt1),
    )
    sent = lax.ppermute(send, "core", [(0, 1), (1, 0)])
    g0, g1, lat, lon, corner = fine_input(
        (gq0, gq1, e0, e1, saved0[0], saved1[0], fine_weights, fine_gain)
    )
    lat, lon, corner = moved(lat, LAT_AXES, 1), moved(lon, "lon", 1), moved_both(corner, 1)
    sent, keep, g0 = lax.optimization_barrier((sent, keep, g0))
    part = (keep.astype(F32) + sent.astype(F32)).astype(BF16)
    total = chip_sum(part)
    share = own_rows(total, core[0])
    lat, lon, corner = (after(block, total) for block in (lat, lon, corner))
    grad_input = assemble((g0, g1, lat, lon, corner)).reshape(LAT, LEV, LON, D1)
    coarse_out = jnp.concatenate([after(other, total), own], 0)
    return coarse_out.transpose(2, 0, 1, 3), grad_input.transpose(2, 0, 1, 3), share


def solution(mesh):
    split = Mesh(mesh.devices.reshape(mesh.devices.shape[0], -1, 2), ("lon", *LAT_AXES))
    tile = P("lon", LAT_AXES, None, None)
    in_specs = (tile,) + (P(),) * 8 + (tile, tile)
    out_specs = (tile, tile, P(("lon", *LAT_AXES), None))
    return jax.shard_map(
        on_device, mesh=split, in_specs=in_specs, out_specs=out_specs, check_vma=False
    )
```

```python
import functools

import jax
import jax.numpy as jnp
from jax import lax
from jax.experimental import pallas as pl
from jax.experimental.pallas import tpu as pltpu
from jax.sharding import Mesh, PartitionSpec as P

LAT_AXES = ("chip", "core")
F32 = jnp.float32
BF16 = jnp.bfloat16
EPS_NORM = 1e-05
EPS_HEAD = 1e-06
D1, D2, H1, H2 = 512, 1024, 8, 16
HEAD = 64
TOK = 216
LON, LAT, LEV = 24, 12, 3
GROUPS = LAT * LEV
EDGE = 9
ROWS = GROUPS * LON
WIN = 12
FINE_BATCH, COARSE_BATCH, BACK_BATCH = 8, 4, 8
MIB = 1024 * 1024


def dot(left, right, left_dim, right_dim):
    return lax.dot_general(
        left, right, (((left_dim,), (right_dim,)), ((), ())), preferred_element_type=F32
    )


def mean_last(values):
    return jnp.mean(values, -1, keepdims=True)


def normalize(values):
    center = values - mean_last(values)
    inverse = lax.rsqrt(mean_last(center * center) + EPS_NORM)
    return center * inverse, inverse


def norm_back(scaled, normed, inverse):
    return inverse * (scaled - mean_last(scaled) - normed * mean_last(scaled * normed))


def keep_matrix(last_ref):
    half = TOK // 2
    keys = lax.broadcasted_iota(jnp.int32, (TOK, TOK), 0) >= half
    queries = lax.broadcasted_iota(jnp.int32, (TOK, TOK), 1) >= half
    apart = jnp.where(keys == queries, 0.0, 1.0)
    return 1.0 - apart * last_ref[0].astype(F32)


def unit_rows(values):
    inverse = lax.rsqrt(jnp.mean(values * values, 0, keepdims=True) + EPS_HEAD)
    return values * inverse, inverse


def softmax_rows(scores, keep):
    raw = jnp.exp(scores) * keep
    return raw * (1.0 / jnp.sum(raw, 0, keepdims=True))


def heads_back(grads, parts, softs, rounds, inverses, scales):
    grad_probs = [dot(part[2], grad, 0, 0) for part, grad in zip(parts, grads)]
    grad_values = [dot(grad, soft, 1, 1) for grad, soft in zip(grads, rounds)]
    grad_scores = [
        (soft * (probs - jnp.sum(probs * soft, 0, keepdims=True))).astype(BF16)
        for probs, soft in zip(grad_probs, softs)
    ]
    grad_q = [dot(part[1], scores, 1, 0) for part, scores in zip(parts, grad_scores)]
    grad_k = [dot(part[0], scores, 1, 1) for part, scores in zip(parts, grad_scores)]
    results = []
    for index, part in enumerate(parts):
        scale, (q_inverse, k_inverse) = scales[index], inverses[index]
        q_wide, k_wide = part[0].astype(F32), part[1].astype(F32)
        q_mean = jnp.mean(grad_q[index] * q_wide, 0, keepdims=True)
        k_mean = jnp.mean(grad_k[index] * k_wide, 0, keepdims=True)
        results.append((
            q_inverse * (grad_q[index] * scale - q_wide * (q_mean * (1.0 / scale))),
            k_inverse * (grad_k[index] - k_wide * k_mean),
            grad_values[index],
        ))
    return results


def head_rows(part, width, head):
    if isinstance(head, int):
        return slice(part * width + head * HEAD, part * width + head * HEAD + HEAD)
    return pl.ds(pl.multiple_of(part * width + head * HEAD, HEAD), HEAD)


def head_parts(head, width, scale, qkv):
    q_unit, q_inverse = unit_rows(qkv[head_rows(0, width, head), :])
    k_unit, k_inverse = unit_rows(qkv[head_rows(1, width, head), :])
    v_round = qkv[head_rows(2, width, head), :].astype(BF16)
    return (q_unit * scale).astype(BF16), k_unit.astype(BF16), v_round, q_inverse, k_inverse


def edges_kernel(x_ref, lat_ref, lon_ref, corner_ref, lon_rows, corner_rows):
    tile = x_ref[...].astype(F32).reshape(GROUPS, LON, D1)
    lat_ref[...] = tile[:EDGE].reshape(EDGE * LON, D1).astype(BF16)
    for group in range(GROUPS):
        rows = tile[group, 0:6]
        if group < EDGE:
            corner_rows[6 * group : 6 * group + 6, :] = rows
        else:
            lon_rows[6 * (group - EDGE) : 6 * (group - EDGE) + 6, :] = rows
    lon_ref[...] = lon_rows[...].astype(BF16)
    corner_ref[...] = corner_rows[...].astype(BF16)


def turn_kernel(w_ref, wt_ref):
    for part in range(3):
        cols = slice(part * D1, part * D1 + D1)
        wt_ref[cols, :] = w_ref[:, cols].T


def fine_forward_kernel(side, *refs):
    if side == 0:
        (x_ref, lat_ref, wt_ref, w_ref, gain_ref, scale_ref, last_ref,
         y_ref, ylat_ref, ylon_ref, ycor_ref, xw_ref, qkv_ref, inv_ref, soft_ref, att_ref,
         wins, qkv, keep, lon_rows, corner_rows) = refs
    else:
        (x_ref, lat_ref, lon_ref, corner_ref, first_ref, wt_ref, w_ref, gain_ref, scale_ref, last_ref,
         y_ref, ylat_ref, xw_ref, qkv_ref, inv_ref, soft_ref, att_ref, wins, qkv, keep) = refs
    tile = x_ref[...].astype(F32).reshape(GROUPS, LON, D1)
    lat_rows = lat_ref[...].astype(F32).reshape(EDGE, LON, D1)
    if side == 1:
        lon_in = lon_ref[...].astype(F32)
        corner_in = corner_ref[...].astype(F32)
    for group in range(GROUPS):
        source = tile[group + EDGE] if group + EDGE < GROUPS else lat_rows[group + EDGE - GROUPS]
        win, row = group // 18, WIN * (group % 18)
        if side == 0:
            wins[win, row : row + WIN, :] = source[6:18]
        else:
            wins[win, row : row + 6, :] = source[18:24]
            if group + EDGE < GROUPS:
                halo = lon_in[6 * group : 6 * group + 6]
            else:
                halo = corner_in[6 * (group + EDGE - GROUPS) : 6 * (group + EDGE - GROUPS) + 6]
            wins[win, row + 6 : row + WIN, :] = halo
    keep[...] = keep_matrix(last_ref)

    def window(win, carry):
        values = wins[win]
        xw_ref[win] = values.astype(BF16)
        normed = (normalize(values)[0] * gain_ref[...]).astype(BF16)
        for part in range(3):
            qkv[part * D1 : part * D1 + D1, :] = dot(
                wt_ref[part * D1 : part * D1 + D1, :], normed, 1, 1
            )
        use_keep = jnp.where(win >= 1, keep[...], 1.0)
        for start in range(0, H1, FINE_BATCH):
            batch = range(start, start + FINE_BATCH)
            parts = []
            for head in batch:
                q_scaled, k_round, v_round, q_inverse, k_inverse = head_parts(
                    head, D1, scale_ref[head] / HEAD, qkv
                )
                qkv_ref[win, head_rows(0, D1, head), :] = q_scaled
                qkv_ref[win, head_rows(1, D1, head), :] = k_round
                qkv_ref[win, head_rows(2, D1, head), :] = v_round
                inv_ref[win, head : head + 1, :] = q_inverse
                inv_ref[win, H1 + head : H1 + head + 1, :] = k_inverse
                parts.append((q_scaled, k_round, v_round))
            scores = [dot(k_round, q_scaled, 0, 0) for q_scaled, k_round, _ in parts]
            softs = [softmax_rows(score, use_keep).astype(BF16) for score in scores]
            for head, soft, part in zip(batch, softs, parts):
                soft_ref[win, head] = soft
                att_ref[win, head_rows(0, D1, head), :] = dot(part[2], soft, 1, 0).astype(BF16)
        result = values + dot(att_ref[win], w_ref[:, 3 * D1 :], 0, 0)
        wins[win] = result
        y_ref[win] = result.astype(BF16)
        return carry

    lax.fori_loop(0, 2, window, 0)
    if side == 0:
        ylat_ref[...] = wins[0, 0:112, :].astype(BF16)
        for group in range(GROUPS):
            rows = wins[group // 18, WIN * (group % 18) : WIN * (group % 18) + 6, :]
            if group < EDGE:
                corner_rows[6 * group : 6 * group + 6, :] = rows
            else:
                lon_rows[6 * (group - EDGE) : 6 * (group - EDGE) + 6, :] = rows
        ylon_ref[...] = lon_rows[...].astype(BF16)
        ycor_ref[...] = corner_rows[...].astype(BF16)
    else:
        ylat_ref[0:112, :] = first_ref[...]
        ylat_ref[112:224, :] = wins[0, 0:112, :].astype(BF16)


def coarse_kernel(
    y0_ref, y1_ref, lat_ref, lon_ref, corner_ref, cotc_ref, mgain_ref, mw_ref, cw_ref, gain_ref,
    scale_ref, last_ref,
    att, val_ref, g_ref, glat_ref, glon_ref, gcor_ref,
    near, far, halo, cells, merged, mnorm, minv, qkv, gqkv, gatt, turned, keep, lon_rows, corner_rows, cot_rows,
):
    for group in range(18):
        cot_rows[WIN * group : WIN * group + WIN, :] = cotc_ref[group].astype(F32)
    cot = cot_rows[...].astype(BF16)
    for cut in range(4):
        lanes = slice(cut * 128, cut * 128 + 128)
        for win in range(2):
            near[cut, TOK * win : TOK * win + TOK, :] = y0_ref[win, :, lanes].astype(F32)
            far[cut, TOK * win : TOK * win + TOK, :] = y1_ref[win, :, lanes].astype(F32)
        near[cut, 2 * TOK : 2 * TOK + 112, :] = lat_ref[0:112, lanes].astype(F32)
        far[cut, 2 * TOK : 2 * TOK + 112, :] = lat_ref[112:224, lanes].astype(F32)
        halo[cut, 0:162, :] = lon_ref[:, lanes].astype(F32)
        halo[cut, 162:TOK, :] = corner_ref[:, lanes].astype(F32)
    for group in range(18):
        for part in range(4):
            cell = (2 * (group // LEV) + part % 2) * LEV + group % LEV
            source, odd, row = WIN * (cell + EDGE), part // 2, WIN * group
            for cut in range(4):
                lanes = slice(part * D1 + cut * 128, part * D1 + cut * 128 + 128)
                merged[row : row + 3, lanes] = near[cut, pl.ds(source + 6 + odd, 3, stride=2), :]
                merged[row + 3 : row + 9, lanes] = far[cut, pl.ds(source + odd, 6, stride=2), :]
                merged[row + 9 : row + WIN, lanes] = halo[cut, pl.ds(6 * cell + odd, 3, stride=2), :]
    for start in range(0, TOK, 72):
        normed, inverse = normalize(merged[start : start + 72, :])
        merged[start : start + 72, :] = normed
        minv[start : start + 72, :] = jnp.broadcast_to(inverse, (72, 128))
        mnorm[start : start + 72, :] = normed * mgain_ref[...]
    keep[...] = keep_matrix(last_ref)
    values = dot(mnorm[...].astype(BF16), mw_ref[...], 1, 0).astype(BF16).astype(F32)
    value_norm, value_inverse = normalize(values)
    normed = (value_norm * gain_ref[...]).astype(BF16)
    for start in range(0, 3 * D2, 512):
        qkv[start : start + 512, :] = dot(normed, cw_ref[:, start : start + 512], 1, 0).T
    for start in range(0, D2, 512):
        gatt[start : start + 512, :] = dot(
            cw_ref[start : start + 512, 3 * D2 :], cot, 1, 1
        ).astype(BF16)

    def heads(step, carry):
        batch = [step * COARSE_BATCH + inner for inner in range(COARSE_BATCH)]
        scales = [scale_ref[head] / HEAD for head in batch]
        parts = [head_parts(head, D2, scale, qkv) for head, scale in zip(batch, scales)]
        scores = [dot(part[1], part[0], 0, 0) for part in parts]
        softs = [softmax_rows(score, keep[...]) for score in scores]
        rounds = [soft.astype(BF16) for soft in softs]
        for head, soft, part in zip(batch, rounds, parts):
            att[head_rows(0, D2, head), :] = dot(part[2], soft, 1, 0).astype(BF16)
        grads = [gatt[head_rows(0, D2, head), :] for head in batch]
        results = heads_back(grads, parts, softs, rounds, [part[3:] for part in parts], scales)
        for head, result in zip(batch, results):
            for part in range(3):
                gqkv[head_rows(part, D2, head), :] = result[part].astype(BF16)
        return carry

    lax.fori_loop(0, H2 // COARSE_BATCH, heads, 0)
    val_ref[...] = values.astype(BF16)
    for start in range(0, D2, 256):
        turned[start : start + 256, :] = dot(
            cw_ref[start : start + 256, : 3 * D2], gqkv[...], 1, 0
        )
    scaled = turned[...].T * gain_ref[...]
    grad_in = cot_rows[...] + norm_back(scaled, value_norm, value_inverse)
    grad_in = grad_in.astype(BF16)
    for part in range(4):
        cols = slice(part * D1, part * D1 + D1)
        mnorm[:, cols] = dot(grad_in, mw_ref[cols, :], 1, 1) * mgain_ref[:, cols]
    for start in range(0, TOK, 72):
        mnorm[start : start + 72, :] = norm_back(
            mnorm[start : start + 72, :], merged[start : start + 72, :], minv[start : start + 72, 0:1]
        )
    for group in range(18):
        for part in range(4):
            target = (2 * (group // LEV) + part % 2) * LEV + group % LEV
            for cut in range(4):
                cells[cut, target, pl.ds(part // 2, WIN, stride=2), :] = mnorm[
                    WIN * group : WIN * group + WIN,
                    part * D1 + cut * 128 : part * D1 + cut * 128 + 128,
                ]
    done = jnp.concatenate([cells[cut, 0:GROUPS] for cut in range(4)], -1)
    g_ref[...] = done.reshape(ROWS, D1).astype(BF16)
    glat_ref[...] = done[GROUPS - EDGE :].reshape(EDGE * LON, D1).astype(BF16)
    for group in range(GROUPS):
        rows = done[group, 18:24]
        if group < GROUPS - EDGE:
            lon_rows[6 * group : 6 * group + 6, :] = rows
        else:
            at = 6 * (group + EDGE - GROUPS)
            corner_rows[at : at + 6, :] = rows
    glon_ref[...] = lon_rows[...].astype(BF16)
    gcor_ref[...] = corner_rows[...].astype(BF16)


def coarse_out_kernel(att_ref, val_ref, cw_ref, out_ref):
    result = val_ref[...].astype(F32) + dot(att_ref[...], cw_ref[:, 3 * D2 :], 0, 0)
    for group in range(18):
        out_ref[group] = result[WIN * group : WIN * group + WIN].astype(BF16)


def normed_kernel(xw0_ref, xw1_ref, gain_ref, normt0_ref, normt1_ref):
    for xw_ref, normt_ref in ((xw0_ref, normt0_ref), (xw1_ref, normt1_ref)):
        normt_ref[...] = jnp.zeros_like(normt_ref)
        for win in range(2):
            normed = (normalize(xw_ref[win].astype(F32))[0] * gain_ref[...]).astype(BF16)
            normt_ref[win, :, 0:TOK] = normed.T


def fine_backward_kernel(side, *refs):
    if side == 1:
        (g_ref, lat_ref, cot_ref, clat_ref, clon_ref, ccor_ref,
         qkv_ref, inv_ref, soft_ref, att_ref, w_ref, scale_ref, gq_ref, e_ref, wins, gatt) = refs
        lon_cot = clon_ref[...].astype(F32)
        corner_cot = ccor_ref[...].astype(F32)
    else:
        (g_ref, lat_ref, lon_ref, corner_ref, cot_ref, clat_ref, qkv_ref, inv_ref, soft_ref, att_ref, w_ref,
         scale_ref, core_ref, gq1_ref, e1_ref, att1_ref, normt_ref, normt1_ref,
         gq_ref, e_ref, keep_ref, send_ref, wins, gatt) = refs
        lon_in = lon_ref[...].astype(F32)
        corner_in = corner_ref[...].astype(F32)
    tile = g_ref[...].astype(F32).reshape(GROUPS, LON, D1)
    lat_rows = lat_ref[...].astype(F32).reshape(EDGE, LON, D1)
    cot_tile = cot_ref[...].astype(F32).reshape(GROUPS, LON, D1)
    cot_lat = clat_ref[...].astype(F32).reshape(EDGE, LON, D1)
    for group in range(GROUPS):
        source = lat_rows[group] if group < EDGE else tile[group - EDGE]
        win, row = group // 18, WIN * (group % 18)
        inside = group + EDGE < GROUPS
        cot = cot_tile[group + EDGE] if inside else cot_lat[group + EDGE - GROUPS]
        if side == 1:
            at = 6 * group if inside else 6 * (group + EDGE - GROUPS)
            halo = lon_cot[at : at + 6] if inside else corner_cot[at : at + 6]
            wins[win, row : row + 6, :] = source[6:12] + cot[18:24]
            wins[win, row + 6 : row + WIN, :] = source[12:18] + halo
        else:
            if group < EDGE:
                halo = corner_in[6 * group : 6 * group + 6]
            else:
                halo = lon_in[6 * (group - EDGE) : 6 * (group - EDGE) + 6]
            wins[win, row : row + 6, :] = halo + cot[6:12]
            wins[win, row + 6 : row + WIN, :] = source[0:6] + cot[12:18]
    gq_ref[...] = jnp.zeros_like(gq_ref)

    def window(win, carry):
        cot = wins[win].astype(BF16)
        e_ref[win] = cot
        gatt[...] = dot(w_ref[:, 3 * D1 :], cot, 1, 1).astype(BF16)
        for start in range(0, H1, BACK_BATCH):
            batch = range(start, start + BACK_BATCH)
            rounds = [soft_ref[win, head] for head in batch]
            results = heads_back(
                [gatt[head_rows(0, D1, head), :] for head in batch],
                [[qkv_ref[win, head_rows(part, D1, head), :] for part in range(3)] for head in batch],
                [soft.astype(F32) for soft in rounds],
                rounds,
                [(inv_ref[win, head : head + 1, :], inv_ref[win, H1 + head : H1 + head + 1, :]) for head in batch],
                [scale_ref[head] / HEAD for head in batch],
            )
            for head, result in zip(batch, results):
                for part in range(3):
                    gq_ref[win, head_rows(part, D1, head), 0:TOK] = result[part].astype(BF16)
        return carry

    lax.fori_loop(0, 2, window, 0)
    if side == 0:
        sums = []
        for part in range(3):
            cols = slice(part * D1, part * D1 + D1)
            total = dot(normt_ref[0], gq_ref[0, cols, :], 1, 1) + dot(normt_ref[1], gq_ref[1, cols, :], 1, 1)
            total += dot(normt1_ref[0], gq1_ref[0, cols, :], 1, 1)
            sums.append(total + dot(normt1_ref[1], gq1_ref[1, cols, :], 1, 1))
        total = dot(att_ref[0], e_ref[0], 1, 0) + dot(att_ref[1], e_ref[1], 1, 0)
        sums.append(total + dot(att1_ref[0], e1_ref[0], 1, 0) + dot(att1_ref[1], e1_ref[1], 1, 0))
        for part in range(2):
            cols = slice(part * D1, part * D1 + D1)
            first = core_ref[0] == 0
            keep_ref[:, cols] = jnp.where(first, sums[part], sums[2 + part]).astype(BF16)
            send_ref[:, cols] = jnp.where(first, sums[2 + part], sums[part]).astype(BF16)


def fine_input_kernel(
    gq0_ref, gq1_ref, e0_ref, e1_ref, xw0_ref, xw1_ref, w_ref, gain_ref,
    g0_ref, g1_ref, glat_ref, glon_ref, gcor_ref, lat_rows, lon_rows, corner_rows,
):
    for side, (gq_ref, e_ref, xw_ref, g_ref) in enumerate(
        ((gq0_ref, e0_ref, xw0_ref, g0_ref), (gq1_ref, e1_ref, xw1_ref, g1_ref))
    ):
        for win in range(2):
            turned = dot(w_ref[:, : 3 * D1], gq_ref[win], 1, 0)
            scaled = turned.T[:TOK] * gain_ref[...]
            normed, inverse = normalize(xw_ref[win].astype(F32))
            grad_in = e_ref[win].astype(F32) + norm_back(scaled, normed, inverse)
            g_ref[win] = grad_in.astype(BF16)
            if win == 1:
                lat_rows[108 * side : 108 * side + 108, :] = grad_in[108:TOK]
            if side == 1:
                for group in range(18):
                    rows = grad_in[WIN * group + 6 : WIN * group + WIN]
                    at = 6 * (group + 18 * win)
                    if at < 162:
                        lon_rows[at : at + 6, :] = rows
                    else:
                        corner_rows[at - 162 : at - 156, :] = rows
    glat_ref[...] = lat_rows[...].astype(BF16)
    glon_ref[...] = lon_rows[...].astype(BF16)
    gcor_ref[...] = corner_rows[...].astype(BF16)


def assemble_kernel(g0_ref, g1_ref, lat_ref, lon_ref, corner_ref, out_ref, full):
    first = [g0_ref[win].astype(F32) for win in range(2)]
    second = [g1_ref[win].astype(F32) for win in range(2)]
    lat_rows = lat_ref[...].astype(F32)
    lon_rows = lon_ref[...].astype(F32)
    corner_rows = corner_ref[...].astype(F32)
    for group in range(GROUPS):
        if group < EDGE:
            full[group, 0:6, :] = corner_rows[6 * group : 6 * group + 6]
            full[group, 6:18, :] = lat_rows[WIN * group : WIN * group + WIN]
            full[group, 18:24, :] = lat_rows[108 + WIN * group : 108 + WIN * group + 6]
        else:
            own = group - EDGE
            win, row = own // 18, WIN * (own % 18)
            full[group, 0:6, :] = lon_rows[6 * own : 6 * own + 6]
            full[group, 6:18, :] = first[win][row : row + WIN]
            full[group, 18:24, :] = second[win][row : row + 6]
    out_ref[...] = full[...].reshape(ROWS, D1).astype(BF16)


def call(kernel, outs, scratch, smem_from, args, name, flops, vmem):
    whole = pl.BlockSpec(memory_space=pltpu.VMEM)
    scalars = pl.BlockSpec(memory_space=pltpu.SMEM)
    return pl.pallas_call(
        kernel,
        out_shape=[jax.ShapeDtypeStruct(shape, kind) for shape, kind in outs],
        in_specs=[scalars if position in smem_from else whole for position in range(len(args))],
        out_specs=[whole] * len(outs),
        scratch_shapes=[pltpu.VMEM(shape, kind) for shape, kind in scratch],
        compiler_params=pltpu.CompilerParams(vmem_limit_bytes=vmem * MIB),
        cost_estimate=pl.CostEstimate(flops=flops, bytes_accessed=1 << 22, transcendentals=0),
        name=name,
    )(*args)


HALF = ((2, TOK, D1), BF16)
LAT_BLOCK = ((EDGE * LON, D1), BF16)
LON_BLOCK = ((162, D1), BF16)
CORNER = ((54, D1), BF16)
LON_ROWS = ((162, D1), F32)
CORNER_ROWS = ((54, D1), F32)


def edges(tile):
    return call(edges_kernel, [LAT_BLOCK, LON_BLOCK, CORNER], [LON_ROWS, CORNER_ROWS], (), (tile,), "edges", 2 * 10**9, 6)


def turn(weights):
    return call(turn_kernel, [((3 * D1, D1), BF16)], [], (), (weights,), "turn", 10**9, 6)[0]


def fine_forward(side, ins, weights, scalars):
    outs = [HALF] + ([((112, D1), BF16), LON_BLOCK, CORNER] if side == 0 else [((224, D1), BF16)])
    outs += [
        HALF,
        ((2, 3 * D1, TOK), BF16),
        ((2, 2 * H1, TOK), F32),
        ((2, H1, TOK, TOK), BF16),
        ((2, D1, TOK), BF16),
    ]
    scratch = [((2, TOK, D1), F32), ((3 * D1, TOK), F32), ((TOK, TOK), F32)]
    if side == 0:
        scratch += [LON_ROWS, CORNER_ROWS]
    args = (*ins, *weights, *scalars)
    smem = (len(args) - 2, len(args) - 1)
    kernel = functools.partial(fine_forward_kernel, side)
    out = call(kernel, outs, scratch, smem, args, "fine_forward_" + str(side), 10**10, 10)
    return out[:-5], out[-5:]


def coarse_both(ins, cot_coarse, mgain, mw, cw, gain, scales, last):
    outs = [((D2, TOK), BF16), ((TOK, D2), BF16), ((ROWS, D1), BF16), LAT_BLOCK, LON_BLOCK, CORNER]
    scratch = [
        ((4, 2 * TOK + 128, 128), F32),
        ((4, 2 * TOK + 128, 128), F32),
        ((4, TOK + 16, 128), F32),
        ((4, GROUPS + 1, LON, 128), F32),
        ((TOK, 4 * D1), F32),
        ((TOK, 4 * D1), F32),
        ((TOK, 128), F32),
        ((3 * D2, TOK), F32),
        ((3 * D2, TOK), BF16),
        ((D2, TOK), BF16),
        ((D2, TOK), F32),
        ((TOK, TOK), F32),
        LON_ROWS,
        CORNER_ROWS,
        ((TOK, D2), F32),
    ]
    args = (*ins, cot_coarse, mgain, mw, cw, gain, scales, last)
    return call(coarse_kernel, outs, scratch, (10, 11), args, "coarse_both", 2 * 10**10, 22)


def coarse_result(att, values, weights):
    return call(
        coarse_out_kernel, [((18, WIN, D2), BF16)], [], (), (att, values, weights), "coarse_out", 10**9, 16
    )[0]


def normed_turned(xw0, xw1, gain):
    outs = [((2, D1, 256), BF16)] * 2
    return call(normed_kernel, outs, [], (), (xw0, xw1, gain), "normed", 10**9, 8)


def fine_backward(side, ins, saved, weights, scales, core=(), other=()):
    outs = [((2, 3 * D1, 256), BF16), HALF]
    scratch = [((2, TOK, D1), F32), ((D1, TOK), BF16)]
    if side == 0:
        outs += [((D1, 2 * D1), BF16)] * 2
    args = (*ins, *saved, weights, scales, *core, *other)
    scalars = len(args) - len(other) - len(core) - 1
    smem = tuple(range(scalars, scalars + 1 + len(core)))
    kernel = functools.partial(fine_backward_kernel, side)
    return call(kernel, outs, scratch, smem, args, "fine_backward_" + str(side), 10**10, 14)


def fine_input(args):
    outs = [HALF, HALF, LAT_BLOCK, LON_BLOCK, CORNER]
    scratch = [((EDGE * LON, D1), F32), LON_ROWS, CORNER_ROWS]
    return call(fine_input_kernel, outs, scratch, (), args, "fine_input", 6 * 10**9, 8)


def assemble(args):
    scratch = [((GROUPS, LON, D1), F32)]
    return call(assemble_kernel, [((ROWS, D1), BF16)], scratch, (), args, "assemble", 2 * 10**9, 6)[0]


def ring(axis_size, step):
    return [(i, (i + step) % axis_size) for i in range(axis_size)]


def moved(block, axis, step):
    return lax.ppermute(block, axis, ring(lax.axis_size(axis), step))


def moved_both(block, step):
    nlon, nlat = lax.axis_size("lon"), lax.axis_size(LAT_AXES)
    route = [
        (i * nlat + j, ((i + step) % nlon) * nlat + (j + step) % nlat)
        for i in range(nlon)
        for j in range(nlat)
    ]
    return lax.ppermute(block, ("lon", *LAT_AXES), route)


def half_moved(tile, axis, dim, step):
    near, far = jnp.split(tile, 2, dim)
    if step < 0:
        return jnp.concatenate([far, moved(near, axis, step)], dim)
    return jnp.concatenate([moved(far, axis, step), near], dim)


def after(value, *others):
    return lax.optimization_barrier((value, *others))[0]


def chip_sum(part):
    pieces = lax.all_to_all(part.reshape(64, 8, 2 * D1), ("lon", "chip"), 0, 0)
    return jnp.sum(pieces.astype(F32), 0)


def own_rows(total, core):
    first = core == 0
    mine = jnp.where(first, total[:4], total[4:])
    other = lax.ppermute(jnp.where(first, total[4:], total[:4]), "core", [(0, 1), (1, 0)])
    return jnp.concatenate([jnp.where(first, mine, other), jnp.where(first, other, mine)], 1)


def on_device(
    grid_field, fine_weights, fine_gain, fine_scales, merge_gain, merge_weight, coarse_weights, coarse_gain,
    coarse_scales, cot_fine, cot_coarse,
):
    core = lax.axis_index("core").astype(jnp.int32).reshape(1)
    last = (lax.axis_index(LAT_AXES) == lax.axis_size(LAT_AXES) - 1).astype(jnp.int32).reshape(1)
    fine_gain = fine_gain.reshape(1, -1)
    tile = grid_field.transpose(1, 2, 0, 3).reshape(ROWS, D1)
    lat, lon, corner = edges(tile)
    lat, lon, corner = moved(lat, LAT_AXES, -1), moved(lon, "lon", -1), moved_both(corner, -1)
    cot_coarse = after(cot_coarse, lat).transpose(1, 2, 0, 3)
    cot_coarse = half_moved(cot_coarse, "lon", 2, -1)
    weights = (turn(fine_weights), fine_weights, fine_gain)
    scalars = (fine_scales, last)
    (y0, ylat, ylon, ycor), saved0 = fine_forward(0, (tile, lat), weights, scalars)
    ylon, ycor = moved(ylon, "lon", -1), moved_both(ycor, -1)
    cot_coarse = half_moved(after(cot_coarse, y0), LAT_AXES, 0, -1).reshape(18, WIN, D2)
    (y1, ylat), saved1 = fine_forward(1, (tile, lat, lon, corner, ylat), weights, scalars)
    ylat, ylon, ycor, cot_coarse = lax.optimization_barrier((ylat, ylon, ycor, cot_coarse))
    ylat = moved(ylat, LAT_AXES, -1)
    cot_tile = after(cot_fine, y1).transpose(1, 2, 0, 3).reshape(ROWS, D1)
    cot_edges = edges(cot_tile)
    cot_edges = (moved(cot_edges[0], LAT_AXES, -1), moved(cot_edges[1], "lon", -1), moved_both(cot_edges[2], -1))
    att, values, grad, glat, glon, gcor = coarse_both(
        (y0, y1, ylat, ylon, ycor), cot_coarse, merge_gain.reshape(1, -1), merge_weight,
        coarse_weights, coarse_gain.reshape(1, -1), coarse_scales, last,
    )
    (glat, glon, gcor), cot_edges = lax.optimization_barrier(((glat, glon, gcor), cot_edges))
    glat, glon, gcor = moved(glat, LAT_AXES, 1), moved(glon, "lon", 1), moved_both(gcor, 1)
    coarse_out = coarse_result(att, values, coarse_weights)
    normt0, normt1 = normed_turned(saved0[0], saved1[0], after(fine_gain, att))
    coarse_out, glat, normt0, normt1 = lax.optimization_barrier((coarse_out, glat, normt0, normt1))
    coarse_out = half_moved(coarse_out.reshape(LAT // 2, LEV, LON // 2, D2), "lon", 2, 1)
    gq1, e1 = fine_backward(1, (grad, glat, cot_tile, *cot_edges), saved1[1:], fine_weights, fine_scales)
    gq1, coarse_out = lax.optimization_barrier((gq1, coarse_out))
    own, other = jnp.split(coarse_out, 2, 0)
    other = moved(other, LAT_AXES, 1)
    gq0, e0, keep, send = fine_backward(
        0, (grad, glat, glon, gcor, cot_tile, cot_edges[0]), saved0[1:], fine_weights, fine_scales,
        (core,), (gq1, e1, saved1[4], normt0, normt1),
    )
    sent = lax.ppermute(send, "core", [(0, 1), (1, 0)])
    g0, g1, lat, lon, corner = fine_input(
        (gq0, gq1, e0, e1, saved0[0], saved1[0], fine_weights, fine_gain)
    )
    lat, lon, corner = moved(lat, LAT_AXES, 1), moved(lon, "lon", 1), moved_both(corner, 1)
    sent, keep, g0 = lax.optimization_barrier((sent, keep, g0))
    part = (keep.astype(F32) + sent.astype(F32)).astype(BF16)
    total = chip_sum(part)
    share = own_rows(total, core[0])
    lat, lon, corner = (after(block, total) for block in (lat, lon, corner))
    grad_input = assemble((g0, g1, lat, lon, corner)).reshape(LAT, LEV, LON, D1)
    coarse_out = jnp.concatenate([after(other, total), own], 0)
    return coarse_out.transpose(2, 0, 1, 3), grad_input.transpose(2, 0, 1, 3), share


def solution(mesh):
    split = Mesh(mesh.devices.reshape(mesh.devices.shape[0], -1, 2), ("lon", *LAT_AXES))
    tile = P("lon", LAT_AXES, None, None)
    in_specs = (tile,) + (P(),) * 8 + (tile, tile)
    out_specs = (tile, tile, P(("lon", *LAT_AXES), None))
    return jax.shard_map(
        on_device, mesh=split, in_specs=in_specs, out_specs=out_specs, check_vma=False
    )
```

```python
import functools

import jax
import jax.numpy as jnp
from jax import lax
from jax.experimental import pallas as pl
from jax.experimental.pallas import tpu as pltpu
from jax.sharding import Mesh, PartitionSpec as P

LAT_AXES = ("chip", "core")
F32 = jnp.float32
BF16 = jnp.bfloat16
EPS_NORM = 1e-05
EPS_HEAD = 1e-06
D1, D2, H1, H2 = 512, 1024, 8, 16
HEAD = 64
TOK = 216
LON, LAT, LEV = 24, 12, 3
GROUPS = LAT * LEV
EDGE = 9
ROWS = GROUPS * LON
WIN = 12
FINE_BATCH, COARSE_BATCH, BACK_BATCH = 8, 4, 8
MIB = 1024 * 1024


def dot(left, right, left_dim, right_dim):
    return lax.dot_general(
        left, right, (((left_dim,), (right_dim,)), ((), ())), preferred_element_type=F32
    )


def mean_last(values):
    return jnp.mean(values, -1, keepdims=True)


def normalize(values):
    center = values - mean_last(values)
    inverse = lax.rsqrt(mean_last(center * center) + EPS_NORM)
    return center * inverse, inverse


def norm_back(scaled, normed, inverse):
    return inverse * (scaled - mean_last(scaled) - normed * mean_last(scaled * normed))


def keep_matrix(last_ref):
    half = TOK // 2
    keys = lax.broadcasted_iota(jnp.int32, (TOK, TOK), 0) >= half
    queries = lax.broadcasted_iota(jnp.int32, (TOK, TOK), 1) >= half
    apart = jnp.where(keys == queries, 0.0, 1.0)
    return 1.0 - apart * last_ref[0].astype(F32)


def unit_rows(values):
    inverse = lax.rsqrt(jnp.mean(values * values, 0, keepdims=True) + EPS_HEAD)
    return values * inverse, inverse


def softmax_rows(scores, keep):
    raw = jnp.exp(scores) * keep
    return raw * (1.0 / jnp.sum(raw, 0, keepdims=True))


def heads_back(grads, parts, softs, rounds, inverses, scales):
    grad_probs = [dot(part[2], grad, 0, 0) for part, grad in zip(parts, grads)]
    grad_values = [dot(grad, soft, 1, 1) for grad, soft in zip(grads, rounds)]
    grad_scores = [
        (soft * (probs - jnp.sum(probs * soft, 0, keepdims=True))).astype(BF16)
        for probs, soft in zip(grad_probs, softs)
    ]
    grad_q = [dot(part[1], scores, 1, 0) for part, scores in zip(parts, grad_scores)]
    grad_k = [dot(part[0], scores, 1, 1) for part, scores in zip(parts, grad_scores)]
    results = []
    for index, part in enumerate(parts):
        scale, (q_inverse, k_inverse) = scales[index], inverses[index]
        q_wide, k_wide = part[0].astype(F32), part[1].astype(F32)
        q_mean = jnp.mean(grad_q[index] * q_wide, 0, keepdims=True)
        k_mean = jnp.mean(grad_k[index] * k_wide, 0, keepdims=True)
        results.append((
            q_inverse * (grad_q[index] * scale - q_wide * (q_mean * (1.0 / scale))),
            k_inverse * (grad_k[index] - k_wide * k_mean),
            grad_values[index],
        ))
    return results


def head_rows(part, width, head):
    if isinstance(head, int):
        return slice(part * width + head * HEAD, part * width + head * HEAD + HEAD)
    return pl.ds(pl.multiple_of(part * width + head * HEAD, HEAD), HEAD)


def head_parts(head, width, scale, qkv):
    q_unit, q_inverse = unit_rows(qkv[head_rows(0, width, head), :])
    k_unit, k_inverse = unit_rows(qkv[head_rows(1, width, head), :])
    v_round = qkv[head_rows(2, width, head), :].astype(BF16)
    return (q_unit * scale).astype(BF16), k_unit.astype(BF16), v_round, q_inverse, k_inverse


def edges_kernel(x_ref, lat_ref, lon_ref, corner_ref, lon_rows, corner_rows):
    tile = x_ref[...].astype(F32).reshape(GROUPS, LON, D1)
    lat_ref[...] = tile[:EDGE].reshape(EDGE * LON, D1).astype(BF16)
    for group in range(GROUPS):
        rows = tile[group, 0:6]
        if group < EDGE:
            corner_rows[6 * group : 6 * group + 6, :] = rows
        else:
            lon_rows[6 * (group - EDGE) : 6 * (group - EDGE) + 6, :] = rows
    lon_ref[...] = lon_rows[...].astype(BF16)
    corner_ref[...] = corner_rows[...].astype(BF16)


def turn_kernel(w_ref, wt_ref):
    for part in range(3):
        cols = slice(part * D1, part * D1 + D1)
        wt_ref[cols, :] = w_ref[:, cols].T


def fine_forward_kernel(side, *refs):
    if side == 0:
        (x_ref, lat_ref, wt_ref, w_ref, gain_ref, scale_ref, last_ref,
         y_ref, ylat_ref, ylon_ref, ycor_ref, xw_ref, qkv_ref, inv_ref, soft_ref, att_ref,
         wins, qkv, keep, lon_rows, corner_rows) = refs
    else:
        (x_ref, lat_ref, lon_ref, corner_ref, first_ref, wt_ref, w_ref, gain_ref, scale_ref, last_ref,
         y_ref, ylat_ref, xw_ref, qkv_ref, inv_ref, soft_ref, att_ref, wins, qkv, keep) = refs
    tile = x_ref[...].astype(F32).reshape(GROUPS, LON, D1)
    lat_rows = lat_ref[...].astype(F32).reshape(EDGE, LON, D1)
    if side == 1:
        lon_in = lon_ref[...].astype(F32)
        corner_in = corner_ref[...].astype(F32)
    for group in range(GROUPS):
        source = tile[group + EDGE] if group + EDGE < GROUPS else lat_rows[group + EDGE - GROUPS]
        win, row = group // 18, WIN * (group % 18)
        if side == 0:
            wins[win, row : row + WIN, :] = source[6:18]
        else:
            wins[win, row : row + 6, :] = source[18:24]
            if group + EDGE < GROUPS:
                halo = lon_in[6 * group : 6 * group + 6]
            else:
                halo = corner_in[6 * (group + EDGE - GROUPS) : 6 * (group + EDGE - GROUPS) + 6]
            wins[win, row + 6 : row + WIN, :] = halo
    keep[...] = keep_matrix(last_ref)

    def window(win, carry):
        values = wins[win]
        xw_ref[win] = values.astype(BF16)
        normed = (normalize(values)[0] * gain_ref[...]).astype(BF16)
        for part in range(3):
            qkv[part * D1 : part * D1 + D1, :] = dot(
                wt_ref[part * D1 : part * D1 + D1, :], normed, 1, 1
            )
        use_keep = jnp.where(win >= 1, keep[...], 1.0)
        for start in range(0, H1, FINE_BATCH):
            batch = range(start, start + FINE_BATCH)
            parts = []
            for head in batch:
                q_scaled, k_round, v_round, q_inverse, k_inverse = head_parts(
                    head, D1, scale_ref[head] / HEAD, qkv
                )
                qkv_ref[win, head_rows(0, D1, head), :] = q_scaled
                qkv_ref[win, head_rows(1, D1, head), :] = k_round
                qkv_ref[win, head_rows(2, D1, head), :] = v_round
                inv_ref[win, head : head + 1, :] = q_inverse
                inv_ref[win, H1 + head : H1 + head + 1, :] = k_inverse
                parts.append((q_scaled, k_round, v_round))
            scores = [dot(k_round, q_scaled, 0, 0) for q_scaled, k_round, _ in parts]
            softs = [softmax_rows(score, use_keep).astype(BF16) for score in scores]
            for head, soft, part in zip(batch, softs, parts):
                soft_ref[win, head] = soft
                att_ref[win, head_rows(0, D1, head), :] = dot(part[2], soft, 1, 0).astype(BF16)
        result = values + dot(att_ref[win], w_ref[:, 3 * D1 :], 0, 0)
        wins[win] = result
        y_ref[win] = result.astype(BF16)
        return carry

    lax.fori_loop(0, 2, window, 0)
    if side == 0:
        ylat_ref[...] = wins[0, 0:112, :].astype(BF16)
        for group in range(GROUPS):
            rows = wins[group // 18, WIN * (group % 18) : WIN * (group % 18) + 6, :]
            if group < EDGE:
                corner_rows[6 * group : 6 * group + 6, :] = rows
            else:
                lon_rows[6 * (group - EDGE) : 6 * (group - EDGE) + 6, :] = rows
        ylon_ref[...] = lon_rows[...].astype(BF16)
        ycor_ref[...] = corner_rows[...].astype(BF16)
    else:
        ylat_ref[0:112, :] = first_ref[...]
        ylat_ref[112:224, :] = wins[0, 0:112, :].astype(BF16)


def coarse_kernel(
    y0_ref, y1_ref, lat_ref, lon_ref, corner_ref, cotc_ref, mgain_ref, mw_ref, cw_ref, gain_ref,
    scale_ref, last_ref,
    att, val_ref, g_ref, glat_ref, glon_ref, gcor_ref,
    near, far, halo, cells, merged, mnorm, minv, qkv, gqkv, gatt, turned, keep, lon_rows, corner_rows, cot_rows,
):
    for group in range(18):
        cot_rows[WIN * group : WIN * group + WIN, :] = cotc_ref[group].astype(F32)
    cot = cot_rows[...].astype(BF16)
    for cut in range(4):
        lanes = slice(cut * 128, cut * 128 + 128)
        for win in range(2):
            near[cut, TOK * win : TOK * win + TOK, :] = y0_ref[win, :, lanes].astype(F32)
            far[cut, TOK * win : TOK * win + TOK, :] = y1_ref[win, :, lanes].astype(F32)
        near[cut, 2 * TOK : 2 * TOK + 112, :] = lat_ref[0:112, lanes].astype(F32)
        far[cut, 2 * TOK : 2 * TOK + 112, :] = lat_ref[112:224, lanes].astype(F32)
        halo[cut, 0:162, :] = lon_ref[:, lanes].astype(F32)
        halo[cut, 162:TOK, :] = corner_ref[:, lanes].astype(F32)
    for group in range(18):
        for part in range(4):
            cell = (2 * (group // LEV) + part % 2) * LEV + group % LEV
            source, odd, row = WIN * (cell + EDGE), part // 2, WIN * group
            for cut in range(4):
                lanes = slice(part * D1 + cut * 128, part * D1 + cut * 128 + 128)
                merged[row : row + 3, lanes] = near[cut, pl.ds(source + 6 + odd, 3, stride=2), :]
                merged[row + 3 : row + 9, lanes] = far[cut, pl.ds(source + odd, 6, stride=2), :]
                merged[row + 9 : row + WIN, lanes] = halo[cut, pl.ds(6 * cell + odd, 3, stride=2), :]
    for start in range(0, TOK, 72):
        normed, inverse = normalize(merged[start : start + 72, :])
        merged[start : start + 72, :] = normed
        minv[start : start + 72, :] = jnp.broadcast_to(inverse, (72, 128))
        mnorm[start : start + 72, :] = normed * mgain_ref[...]
    keep[...] = keep_matrix(last_ref)
    values = dot(mnorm[...].astype(BF16), mw_ref[...], 1, 0).astype(BF16).astype(F32)
    value_norm, value_inverse = normalize(values)
    normed = (value_norm * gain_ref[...]).astype(BF16)
    for start in range(0, 3 * D2, 512):
        qkv[start : start + 512, :] = dot(normed, cw_ref[:, start : start + 512], 1, 0).T
    for start in range(0, D2, 512):
        gatt[start : start + 512, :] = dot(
            cw_ref[start : start + 512, 3 * D2 :], cot, 1, 1
        ).astype(BF16)

    def heads(step, carry):
        batch = [step * COARSE_BATCH + inner for inner in range(COARSE_BATCH)]
        scales = [scale_ref[head] / HEAD for head in batch]
        parts = [head_parts(head, D2, scale, qkv) for head, scale in zip(batch, scales)]
        scores = [dot(part[1], part[0], 0, 0) for part in parts]
        softs = [softmax_rows(score, keep[...]) for score in scores]
        rounds = [soft.astype(BF16) for soft in softs]
        for head, soft, part in zip(batch, rounds, parts):
            att[head_rows(0, D2, head), :] = dot(part[2], soft, 1, 0).astype(BF16)
        grads = [gatt[head_rows(0, D2, head), :] for head in batch]
        results = heads_back(grads, parts, softs, rounds, [part[3:] for part in parts], scales)
        for head, result in zip(batch, results):
            for part in range(3):
                gqkv[head_rows(part, D2, head), :] = result[part].astype(BF16)
        return carry

    lax.fori_loop(0, H2 // COARSE_BATCH, heads, 0)
    val_ref[...] = values.astype(BF16)
    for start in range(0, D2, 256):
        turned[start : start + 256, :] = dot(
            cw_ref[start : start + 256, : 3 * D2], gqkv[...], 1, 0
        )
    scaled = turned[...].T * gain_ref[...]
    grad_in = cot_rows[...] + norm_back(scaled, value_norm, value_inverse)
    grad_in = grad_in.astype(BF16)
    for part in range(4):
        cols = slice(part * D1, part * D1 + D1)
        mnorm[:, cols] = dot(grad_in, mw_ref[cols, :], 1, 1) * mgain_ref[:, cols]
    for start in range(0, TOK, 72):
        mnorm[start : start + 72, :] = norm_back(
            mnorm[start : start + 72, :], merged[start : start + 72, :], minv[start : start + 72, 0:1]
        )
    for group in range(18):
        for part in range(4):
            target = (2 * (group // LEV) + part % 2) * LEV + group % LEV
            for cut in range(4):
                cells[cut, target, pl.ds(part // 2, WIN, stride=2), :] = mnorm[
                    WIN * group : WIN * group + WIN,
                    part * D1 + cut * 128 : part * D1 + cut * 128 + 128,
                ]
    done = jnp.concatenate([cells[cut, 0:GROUPS] for cut in range(4)], -1)
    g_ref[...] = done.reshape(ROWS, D1).astype(BF16)
    glat_ref[...] = done[GROUPS - EDGE :].reshape(EDGE * LON, D1).astype(BF16)
    for group in range(GROUPS):
        rows = done[group, 18:24]
        if group < GROUPS - EDGE:
            lon_rows[6 * group : 6 * group + 6, :] = rows
        else:
            at = 6 * (group + EDGE - GROUPS)
            corner_rows[at : at + 6, :] = rows
    glon_ref[...] = lon_rows[...].astype(BF16)
    gcor_ref[...] = corner_rows[...].astype(BF16)


def coarse_out_kernel(att_ref, val_ref, cw_ref, out_ref):
    result = val_ref[...].astype(F32) + dot(att_ref[...], cw_ref[:, 3 * D2 :], 0, 0)
    for group in range(18):
        out_ref[group] = result[WIN * group : WIN * group + WIN].astype(BF16)


def normed_kernel(xw0_ref, xw1_ref, gain_ref, normt0_ref, normt1_ref):
    for xw_ref, normt_ref in ((xw0_ref, normt0_ref), (xw1_ref, normt1_ref)):
        normt_ref[...] = jnp.zeros_like(normt_ref)
        for win in range(2):
            normed = (normalize(xw_ref[win].astype(F32))[0] * gain_ref[...]).astype(BF16)
            normt_ref[win, :, 0:TOK] = normed.T


def fine_backward_kernel(side, *refs):
    if side == 1:
        (g_ref, lat_ref, cot_ref, clat_ref, clon_ref, ccor_ref,
         qkv_ref, inv_ref, soft_ref, att_ref, w_ref, scale_ref, gq_ref, e_ref, wins, gatt) = refs
        lon_cot = clon_ref[...].astype(F32)
        corner_cot = ccor_ref[...].astype(F32)
    else:
        (g_ref, lat_ref, lon_ref, corner_ref, cot_ref, clat_ref, qkv_ref, inv_ref, soft_ref, att_ref, w_ref,
         scale_ref, core_ref, gq1_ref, e1_ref, att1_ref, normt_ref, normt1_ref,
         gq_ref, e_ref, keep_ref, send_ref, wins, gatt) = refs
        lon_in = lon_ref[...].astype(F32)
        corner_in = corner_ref[...].astype(F32)
    tile = g_ref[...].astype(F32).reshape(GROUPS, LON, D1)
    lat_rows = lat_ref[...].astype(F32).reshape(EDGE, LON, D1)
    cot_tile = cot_ref[...].astype(F32).reshape(GROUPS, LON, D1)
    cot_lat = clat_ref[...].astype(F32).reshape(EDGE, LON, D1)
    for group in range(GROUPS):
        source = lat_rows[group] if group < EDGE else tile[group - EDGE]
        win, row = group // 18, WIN * (group % 18)
        inside = group + EDGE < GROUPS
        cot = cot_tile[group + EDGE] if inside else cot_lat[group + EDGE - GROUPS]
        if side == 1:
            at = 6 * group if inside else 6 * (group + EDGE - GROUPS)
            halo = lon_cot[at : at + 6] if inside else corner_cot[at : at + 6]
            wins[win, row : row + 6, :] = source[6:12] + cot[18:24]
            wins[win, row + 6 : row + WIN, :] = source[12:18] + halo
        else:
            if group < EDGE:
                halo = corner_in[6 * group : 6 * group + 6]
            else:
                halo = lon_in[6 * (group - EDGE) : 6 * (group - EDGE) + 6]
            wins[win, row : row + 6, :] = halo + cot[6:12]
            wins[win, row + 6 : row + WIN, :] = source[0:6] + cot[12:18]
    gq_ref[...] = jnp.zeros_like(gq_ref)

    def window(win, carry):
        cot = wins[win].astype(BF16)
        e_ref[win] = cot
        gatt[...] = dot(w_ref[:, 3 * D1 :], cot, 1, 1).astype(BF16)
        for start in range(0, H1, BACK_BATCH):
            batch = range(start, start + BACK_BATCH)
            rounds = [soft_ref[win, head] for head in batch]
            results = heads_back(
                [gatt[head_rows(0, D1, head), :] for head in batch],
                [[qkv_ref[win, head_rows(part, D1, head), :] for part in range(3)] for head in batch],
                [soft.astype(F32) for soft in rounds],
                rounds,
                [(inv_ref[win, head : head + 1, :], inv_ref[win, H1 + head : H1 + head + 1, :]) for head in batch],
                [scale_ref[head] / HEAD for head in batch],
            )
            for head, result in zip(batch, results):
                for part in range(3):
                    gq_ref[win, head_rows(part, D1, head), 0:TOK] = result[part].astype(BF16)
        return carry

    lax.fori_loop(0, 2, window, 0)
    if side == 0:
        sums = []
        for part in range(3):
            cols = slice(part * D1, part * D1 + D1)
            total = dot(normt_ref[0], gq_ref[0, cols, :], 1, 1) + dot(normt_ref[1], gq_ref[1, cols, :], 1, 1)
            total += dot(normt1_ref[0], gq1_ref[0, cols, :], 1, 1)
            sums.append(total + dot(normt1_ref[1], gq1_ref[1, cols, :], 1, 1))
        total = dot(att_ref[0], e_ref[0], 1, 0) + dot(att_ref[1], e_ref[1], 1, 0)
        sums.append(total + dot(att1_ref[0], e1_ref[0], 1, 0) + dot(att1_ref[1], e1_ref[1], 1, 0))
        for part in range(2):
            cols = slice(part * D1, part * D1 + D1)
            first = core_ref[0] == 0
            keep_ref[:, cols] = jnp.where(first, sums[part], sums[2 + part]).astype(BF16)
            send_ref[:, cols] = jnp.where(first, sums[2 + part], sums[part]).astype(BF16)


def fine_input_kernel(
    gq0_ref, gq1_ref, e0_ref, e1_ref, xw0_ref, xw1_ref, w_ref, gain_ref,
    g0_ref, g1_ref, glat_ref, glon_ref, gcor_ref, lat_rows, lon_rows, corner_rows,
):
    for side, (gq_ref, e_ref, xw_ref, g_ref) in enumerate(
        ((gq0_ref, e0_ref, xw0_ref, g0_ref), (gq1_ref, e1_ref, xw1_ref, g1_ref))
    ):
        for win in range(2):
            turned = dot(w_ref[:, : 3 * D1], gq_ref[win], 1, 0)
            scaled = turned.T[:TOK] * gain_ref[...]
            normed, inverse = normalize(xw_ref[win].astype(F32))
            grad_in = e_ref[win].astype(F32) + norm_back(scaled, normed, inverse)
            g_ref[win] = grad_in.astype(BF16)
            if win == 1:
                lat_rows[108 * side : 108 * side + 108, :] = grad_in[108:TOK]
            if side == 1:
                for group in range(18):
                    rows = grad_in[WIN * group + 6 : WIN * group + WIN]
                    at = 6 * (group + 18 * win)
                    if at < 162:
                        lon_rows[at : at + 6, :] = rows
                    else:
                        corner_rows[at - 162 : at - 156, :] = rows
    glat_ref[...] = lat_rows[...].astype(BF16)
    glon_ref[...] = lon_rows[...].astype(BF16)
    gcor_ref[...] = corner_rows[...].astype(BF16)


def assemble_kernel(g0_ref, g1_ref, lat_ref, lon_ref, corner_ref, out_ref, full):
    first = [g0_ref[win].astype(F32) for win in range(2)]
    second = [g1_ref[win].astype(F32) for win in range(2)]
    lat_rows = lat_ref[...].astype(F32)
    lon_rows = lon_ref[...].astype(F32)
    corner_rows = corner_ref[...].astype(F32)
    for group in range(GROUPS):
        if group < EDGE:
            full[group, 0:6, :] = corner_rows[6 * group : 6 * group + 6]
            full[group, 6:18, :] = lat_rows[WIN * group : WIN * group + WIN]
            full[group, 18:24, :] = lat_rows[108 + WIN * group : 108 + WIN * group + 6]
        else:
            own = group - EDGE
            win, row = own // 18, WIN * (own % 18)
            full[group, 0:6, :] = lon_rows[6 * own : 6 * own + 6]
            full[group, 6:18, :] = first[win][row : row + WIN]
            full[group, 18:24, :] = second[win][row : row + 6]
    out_ref[...] = full[...].reshape(ROWS, D1).astype(BF16)


def call(kernel, outs, scratch, smem_from, args, name, flops, vmem):
    whole = pl.BlockSpec(memory_space=pltpu.VMEM)
    scalars = pl.BlockSpec(memory_space=pltpu.SMEM)
    return pl.pallas_call(
        kernel,
        out_shape=[jax.ShapeDtypeStruct(shape, kind) for shape, kind in outs],
        in_specs=[scalars if position in smem_from else whole for position in range(len(args))],
        out_specs=[whole] * len(outs),
        scratch_shapes=[pltpu.VMEM(shape, kind) for shape, kind in scratch],
        compiler_params=pltpu.CompilerParams(vmem_limit_bytes=vmem * MIB),
        cost_estimate=pl.CostEstimate(flops=flops, bytes_accessed=1 << 22, transcendentals=0),
        name=name,
    )(*args)


HALF = ((2, TOK, D1), BF16)
LAT_BLOCK = ((EDGE * LON, D1), BF16)
LON_BLOCK = ((162, D1), BF16)
CORNER = ((54, D1), BF16)
LON_ROWS = ((162, D1), F32)
CORNER_ROWS = ((54, D1), F32)


def edges(tile):
    return call(edges_kernel, [LAT_BLOCK, LON_BLOCK, CORNER], [LON_ROWS, CORNER_ROWS], (), (tile,), "edges", 2 * 10**9, 6)


def turn(weights):
    return call(turn_kernel, [((3 * D1, D1), BF16)], [], (), (weights,), "turn", 10**9, 6)[0]


def fine_forward(side, ins, weights, scalars):
    outs = [HALF] + ([((112, D1), BF16), LON_BLOCK, CORNER] if side == 0 else [((224, D1), BF16)])
    outs += [
        HALF,
        ((2, 3 * D1, TOK), BF16),
        ((2, 2 * H1, TOK), F32),
        ((2, H1, TOK, TOK), BF16),
        ((2, D1, TOK), BF16),
    ]
    scratch = [((2, TOK, D1), F32), ((3 * D1, TOK), F32), ((TOK, TOK), F32)]
    if side == 0:
        scratch += [LON_ROWS, CORNER_ROWS]
    args = (*ins, *weights, *scalars)
    smem = (len(args) - 2, len(args) - 1)
    kernel = functools.partial(fine_forward_kernel, side)
    out = call(kernel, outs, scratch, smem, args, "fine_forward_" + str(side), 10**10, 10)
    return out[:-5], out[-5:]


def coarse_both(ins, cot_coarse, mgain, mw, cw, gain, scales, last):
    outs = [((D2, TOK), BF16), ((TOK, D2), BF16), ((ROWS, D1), BF16), LAT_BLOCK, LON_BLOCK, CORNER]
    scratch = [
        ((4, 2 * TOK + 128, 128), F32),
        ((4, 2 * TOK + 128, 128), F32),
        ((4, TOK + 16, 128), F32),
        ((4, GROUPS + 1, LON, 128), F32),
        ((TOK, 4 * D1), F32),
        ((TOK, 4 * D1), F32),
        ((TOK, 128), F32),
        ((3 * D2, TOK), F32),
        ((3 * D2, TOK), BF16),
        ((D2, TOK), BF16),
        ((D2, TOK), F32),
        ((TOK, TOK), F32),
        LON_ROWS,
        CORNER_ROWS,
        ((TOK, D2), F32),
    ]
    args = (*ins, cot_coarse, mgain, mw, cw, gain, scales, last)
    return call(coarse_kernel, outs, scratch, (10, 11), args, "coarse_both", 2 * 10**10, 22)


def coarse_result(att, values, weights):
    return call(
        coarse_out_kernel, [((18, WIN, D2), BF16)], [], (), (att, values, weights), "coarse_out", 10**9, 16
    )[0]


def normed_turned(xw0, xw1, gain):
    outs = [((2, D1, 256), BF16)] * 2
    return call(normed_kernel, outs, [], (), (xw0, xw1, gain), "normed", 10**9, 8)


def fine_backward(side, ins, saved, weights, scales, core=(), other=()):
    outs = [((2, 3 * D1, 256), BF16), HALF]
    scratch = [((2, TOK, D1), F32), ((D1, TOK), BF16)]
    if side == 0:
        outs += [((D1, 2 * D1), BF16)] * 2
    args = (*ins, *saved, weights, scales, *core, *other)
    scalars = len(args) - len(other) - len(core) - 1
    smem = tuple(range(scalars, scalars + 1 + len(core)))
    kernel = functools.partial(fine_backward_kernel, side)
    return call(kernel, outs, scratch, smem, args, "fine_backward_" + str(side), 10**10, 14)


def fine_input(args):
    outs = [HALF, HALF, LAT_BLOCK, LON_BLOCK, CORNER]
    scratch = [((EDGE * LON, D1), F32), LON_ROWS, CORNER_ROWS]
    return call(fine_input_kernel, outs, scratch, (), args, "fine_input", 6 * 10**9, 8)


def assemble(args):
    scratch = [((GROUPS, LON, D1), F32)]
    return call(assemble_kernel, [((ROWS, D1), BF16)], scratch, (), args, "assemble", 2 * 10**9, 6)[0]


def ring(axis_size, step):
    return [(i, (i + step) % axis_size) for i in range(axis_size)]


def moved(block, axis, step):
    return lax.ppermute(block, axis, ring(lax.axis_size(axis), step))


def moved_both(block, step):
    nlon, nlat = lax.axis_size("lon"), lax.axis_size(LAT_AXES)
    route = [
        (i * nlat + j, ((i + step) % nlon) * nlat + (j + step) % nlat)
        for i in range(nlon)
        for j in range(nlat)
    ]
    return lax.ppermute(block, ("lon", *LAT_AXES), route)


def half_moved(tile, axis, dim, step):
    near, far = jnp.split(tile, 2, dim)
    if step < 0:
        return jnp.concatenate([far, moved(near, axis, step)], dim)
    return jnp.concatenate([moved(far, axis, step), near], dim)


def after(value, *others):
    return lax.optimization_barrier((value, *others))[0]


def chip_sum(part):
    pieces = lax.all_to_all(part.reshape(64, 8, 2 * D1), ("lon", "chip"), 0, 0)
    return jnp.sum(pieces.astype(F32), 0)


def own_rows(total, core):
    first = core == 0
    mine = jnp.where(first, total[:4], total[4:])
    leaving = jnp.where(first, total[4:], total[:4])
    other = lax.ppermute(leaving, "core", [(0, 1), (1, 0)])
    return jnp.concatenate([jnp.where(first, mine, other), jnp.where(first, other, mine)], 1), leaving


def on_device(
    grid_field, fine_weights, fine_gain, fine_scales, merge_gain, merge_weight, coarse_weights, coarse_gain,
    coarse_scales, cot_fine, cot_coarse,
):
    core = lax.axis_index("core").astype(jnp.int32).reshape(1)
    last = (lax.axis_index(LAT_AXES) == lax.axis_size(LAT_AXES) - 1).astype(jnp.int32).reshape(1)
    fine_gain = fine_gain.reshape(1, -1)
    tile = grid_field.transpose(1, 2, 0, 3).reshape(ROWS, D1)
    lat, lon, corner = edges(tile)
    lat, lon, corner = moved(lat, LAT_AXES, -1), moved(lon, "lon", -1), moved_both(corner, -1)
    cot_coarse = after(cot_coarse, lat).transpose(1, 2, 0, 3)
    cot_coarse = half_moved(cot_coarse, "lon", 2, -1)
    weights = (turn(fine_weights), fine_weights, fine_gain)
    scalars = (fine_scales, last)
    (y0, ylat, ylon, ycor), saved0 = fine_forward(0, (tile, lat), weights, scalars)
    ylon, ycor = moved(ylon, "lon", -1), moved_both(ycor, -1)
    cot_coarse = half_moved(after(cot_coarse, y0), LAT_AXES, 0, -1).reshape(18, WIN, D2)
    (y1, ylat), saved1 = fine_forward(1, (tile, lat, lon, corner, ylat), weights, scalars)
    ylat, ylon, ycor, cot_coarse = lax.optimization_barrier((ylat, ylon, ycor, cot_coarse))
    ylat = moved(ylat, LAT_AXES, -1)
    cot_tile = after(cot_fine, y1).transpose(1, 2, 0, 3).reshape(ROWS, D1)
    cot_edges = edges(cot_tile)
    cot_edges = (moved(cot_edges[0], LAT_AXES, -1), moved(cot_edges[1], "lon", -1), moved_both(cot_edges[2], -1))
    att, values, grad, glat, glon, gcor = coarse_both(
        (y0, y1, ylat, ylon, ycor), cot_coarse, merge_gain.reshape(1, -1), merge_weight,
        coarse_weights, coarse_gain.reshape(1, -1), coarse_scales, last,
    )
    (glat, glon, gcor), cot_edges = lax.optimization_barrier(((glat, glon, gcor), cot_edges))
    glat, glon, gcor = moved(glat, LAT_AXES, 1), moved(glon, "lon", 1), moved_both(gcor, 1)
    coarse_out = coarse_result(att, values, coarse_weights)
    normt0, normt1 = normed_turned(saved0[0], saved1[0], after(fine_gain, att))
    coarse_out, glat, normt0, normt1 = lax.optimization_barrier((coarse_out, glat, normt0, normt1))
    coarse_out = half_moved(coarse_out.reshape(LAT // 2, LEV, LON // 2, D2), "lon", 2, 1)
    gq1, e1 = fine_backward(1, (grad, glat, cot_tile, *cot_edges), saved1[1:], fine_weights, fine_scales)
    gq1, coarse_out = lax.optimization_barrier((gq1, coarse_out))
    own, other = jnp.split(coarse_out, 2, 0)
    other = moved(other, LAT_AXES, 1)
    gq0, e0, keep, send = fine_backward(
        0, (grad, glat, glon, gcor, cot_tile, cot_edges[0]), saved0[1:], fine_weights, fine_scales,
        (core,), (gq1, e1, saved1[4], normt0, normt1),
    )
    sent = lax.ppermute(send, "core", [(0, 1), (1, 0)])
    g0, g1, lat, lon, corner = fine_input(
        (gq0, gq1, e0, e1, saved0[0], saved1[0], fine_weights, fine_gain)
    )
    lat, lon, corner = moved(lat, LAT_AXES, 1), moved(lon, "lon", 1), moved_both(corner, 1)
    sent, keep, g0 = lax.optimization_barrier((sent, keep, g0))
    part = (keep.astype(F32) + sent.astype(F32)).astype(BF16)
    total = chip_sum(part)
    share, leaving = own_rows(total, core[0])
    lat, lon, corner = (after(block, leaving) for block in (lat, lon, corner))
    grad_input = assemble((g0, g1, lat, lon, corner)).reshape(LAT, LEV, LON, D1)
    coarse_out = jnp.concatenate([after(other, leaving), own], 0)
    return coarse_out.transpose(2, 0, 1, 3), grad_input.transpose(2, 0, 1, 3), share


def solution(mesh):
    split = Mesh(mesh.devices.reshape(mesh.devices.shape[0], -1, 2), ("lon", *LAT_AXES))
    tile = P("lon", LAT_AXES, None, None)
    in_specs = (tile,) + (P(),) * 8 + (tile, tile)
    out_specs = (tile, tile, P(("lon", *LAT_AXES), None))
    return jax.shard_map(
        on_device, mesh=split, in_specs=in_specs, out_specs=out_specs, check_vma=False
    )
```
